32 devices in a mesh: seq: 4 (over y, core), ctx: 8 (over z, x).
Axes of the slice: x: 2, y: 2, z: 4, core: 2. Of those that a mesh axis runs over, the one named last changes fastest.
Arguments:
- block_input: bfloat16 [4, 8, 128, 1600], P('seq', 'ctx'), may hold values from -6 to 6
- out_cot: bfloat16 [4, 8, 128, 1600], P('seq', 'ctx'), may hold values from -6 to 6
- pair_of: int32 [8], replicated, may hold values from 0 to 7, each once
- ln1_gain: float32 [1600], replicated, may hold values from 0.5 to 1.5
- ln1_bias: float32 [1600], replicated, may hold values from -2 to 2
- qkv_weight: bfloat16 [1600, 4800], P('seq', 'ctx'), may hold values from -0.15625 to 0.15625
- qv_bias: float32 [2, 1600], replicated, may hold values from -3 to 3
- out_weight: bfloat16 [1600, 1600], P('seq', 'ctx'), may hold values from -0.625 to 0.625
- out_bias: float32 [1600], replicated, may hold values from -3 to 3
- ln2_gain: float32 [1600], replicated, may hold values from 0.5 to 1.5
- ln2_bias: float32 [1600], replicated, may hold values from -2 to 2
- fc_weight: bfloat16 [1600, 6400], P('seq', 'ctx'), may hold values from -0.15625 to 0.15625
- fc_bias: float32 [6400], replicated, may hold values from -3 to 3
- proj_weight: bfloat16 [6400, 1600], P('ctx', 'seq'), may hold values from -0.078125 to 0.078125
- proj_bias: float32 [1600], replicated, may hold values from -3 to 3
Outputs:
- block_output: bfloat16 [4, 8, 128, 1600], P('seq', 'ctx')
- input_grad: bfloat16 [4, 8, 128, 1600], P('seq', 'ctx')
- ln1_gain_grad: float32 [1600], replicated
- ln1_bias_grad: float32 [1600], replicated
- qkv_weight_grad: float32 [1600, 4800], P('seq', 'ctx')
- qv_bias_grad: float32 [2, 1600], replicated
- out_weight_grad: float32 [1600, 1600], P('seq', 'ctx')
- out_bias_grad: float32 [1600], replicated
- ln2_gain_grad: float32 [1600], replicated
- ln2_bias_grad: float32 [1600], replicated
- fc_weight_grad: float32 [1600, 6400], P('seq', 'ctx')
- fc_bias_grad: float32 [6400], replicated
- proj_weight_grad: float32 [6400, 1600], P('ctx', 'seq')
- proj_bias_grad: float32 [1600], replicated
The draws below stay inside these ranges and needn't reach their ends.
Inputs may be any that keep to these rules, and one draw needn't show every extreme that they name: `pair_of`: a permutation: each context rank gets a different pair of blocks p and 15 - p.
All inputs are finite; a program needn't handle non-finite values.
Results may differ from the reference program's by a relative error of at most 0.012.
Values may be sent and summed in bfloat16 or wider, within the bound.
No kernel may reach another device: no remote copies, remote signals or barrier semaphores. Data moves between devices by JAX's collectives and lax.ppermute only.
A program may use at most 576 MiB of HBM per device.

```python
import math
import jax
import jax.numpy as jnp
from jax import lax

D = 1600
HEADS = 25
HEAD = 64
FF = 6400
BLK = 64
SEQS = 4
N_CTX = 8


def levels(key, shape, pieces, low, high):
    level, own = 1.0, jax.random.fold_in(key, 6)
    for position, shards_of in pieces:
        draws = jnp.exp(jax.random.uniform(jax.random.fold_in(own, position), (shards_of,), jnp.float32, low / len(pieces), high / len(pieces)))
        level = level * jnp.repeat(draws, shape[position] // shards_of).reshape([-1 if axis == position else 1 for axis in range(len(shape))])
    return level


def noise(key, extent, width, reach, cuts=(), held_as=jnp.bfloat16):
    factor_of = levels(key, extent, cuts, -0.22, 0.18) if cuts else 1.0
    values = jax.random.normal(key, extent, jnp.float32) * width * factor_of
    return jnp.minimum(jnp.maximum(values, -reach), reach).astype(held_as)


def setup_inputs(seed: int = 0) -> dict:
    keys = jax.random.split(jax.random.key(seed), 16)
    return {
        "block_input": noise(keys[0], (SEQS, N_CTX, 2 * BLK, D), 1.0, 6.0, ((0, 4), (1, 8))),
        "out_cot": noise(keys[1], (SEQS, N_CTX, 2 * BLK, D), 1.0, 6.0, ((0, 4), (1, 8))),
        "pair_of": jax.random.permutation(keys[2], N_CTX).astype(jnp.int32),
        "ln1_gain": jnp.clip(1.0 + 0.1 * jax.random.normal(keys[3], (D,), jnp.float32), 0.5, 1.5),
        "ln1_bias": noise(keys[4], (D,), 0.3, 2.0, (), jnp.float32),
        "qkv_weight": noise(keys[5], (D, 3 * D), D ** -0.5, 0.15625, ((0, 4), (1, 8))),
        "qv_bias": noise(keys[6], (2, D), 0.5, 3.0, (), jnp.float32),
        "out_weight": noise(keys[7], (D, D), (D // 16) ** -0.5, 0.625, ((0, 4), (1, 8))),
        "out_bias": noise(keys[8], (D,), 0.5, 3.0, (), jnp.float32),
        "ln2_gain": jnp.clip(1.0 + 0.1 * jax.random.normal(keys[9], (D,), jnp.float32), 0.5, 1.5),
        "ln2_bias": noise(keys[10], (D,), 0.3, 2.0, (), jnp.float32),
        "fc_weight": noise(keys[11], (D, FF), D ** -0.5, 0.15625, ((0, 4), (1, 8))),
        "fc_bias": noise(keys[12], (FF,), 0.5, 3.0, (), jnp.float32),
        "proj_weight": noise(keys[13], (FF, D), FF ** -0.5, 0.078125, ((0, 8), (1, 4))),
        "proj_bias": noise(keys[14], (D,), 0.5, 3.0, (), jnp.float32),
    }


@jax.custom_vjp
def low(v):
    return lax.optimization_barrier(v.astype(jnp.bfloat16)).astype(jnp.float32)

@jax.custom_vjp
def low_back(v):
    return v

def low_keep(v):
    return (low(v), None)

def low_pass(kept, grad):
    return (grad,)

def back_keep(v):
    return (v, None)

def back_low(kept, grad):
    return (low(grad),)
low.defvjp(low_keep, low_pass)
low_back.defvjp(back_keep, back_low)
EPSILON = 1e-05
NEGATIVE = -1e+30
GELU_COEF = 0.7978845608028654

def layer_norm(values, gain, shift):
    center = values - lax.optimization_barrier(jnp.mean(values, axis=-1, keepdims=True))
    spread = lax.optimization_barrier(jnp.mean(center * center, axis=-1, keepdims=True))
    return center * lax.rsqrt(spread + EPSILON) * gain + shift

def gelu_tanh(values):
    return 0.5 * values * (1.0 + jnp.tanh(GELU_COEF * (values + 0.044715 * values * values * values)))

def positions(pair_of, block):
    ranks = pair_of.shape[0]
    local_index = jnp.arange(2 * block, dtype=jnp.int32)
    first_half = local_index < block
    chosen = jnp.where(first_half[None, :], pair_of[:, None], 2 * ranks - 1 - pair_of[:, None])
    return (chosen * block + local_index[None, :] % block).reshape(-1).astype(jnp.int32)

def matmul(left, right):
    return jnp.dot(left, right, precision=lax.Precision.HIGHEST)

def attend_sequence(parts, key_pos):
    query, key, value = parts
    length = query.shape[0]
    block = math.gcd(length, 512)
    scale = 1.0 / math.sqrt(HEAD)
    query_blocks = query.reshape(length // block, block, HEADS, HEAD)
    pos_blocks = key_pos.reshape(length // block, block)

    def one_block(args):
        query_block, pos_block = args
        score = jnp.einsum('qhd,khd->hqk', query_block, key, precision=lax.Precision.HIGHEST) * scale
        score = low_back(score)
        allowed = key_pos[None, :] <= pos_block[:, None]
        score = jnp.where(allowed[None], score, NEGATIVE)
        prob = jax.nn.softmax(score, axis=-1)
        return jnp.einsum('hqk,khd->qhd', prob, value, precision=lax.Precision.HIGHEST)
    result = lax.map(jax.checkpoint(one_block), (query_blocks, pos_blocks))
    return result.reshape(length, HEADS * HEAD)

def reference(block_input, out_cot, pair_of, ln1_gain, ln1_bias, qkv_weight, qv_bias, out_weight, out_bias, ln2_gain, ln2_bias, fc_weight, fc_bias, proj_weight, proj_bias):
    length = 2 * N_CTX * BLK
    key_pos = positions(pair_of, BLK)
    inputs = block_input.astype(jnp.float32).reshape(SEQS, length, D)
    cotangent = out_cot.astype(jnp.float32).reshape(SEQS, length, D)
    params = (ln1_gain, ln1_bias, qkv_weight.astype(jnp.float32), qv_bias, out_weight.astype(jnp.float32), out_bias, ln2_gain, ln2_bias, fc_weight.astype(jnp.float32), fc_bias, proj_weight.astype(jnp.float32), proj_bias)

    def forward(values, weights):
        gain_one, shift_one, w_qkv, b_qv, w_out, b_out, gain_two, shift_two, w_fc, b_fc, w_proj, b_proj = weights
        flat = values.reshape(SEQS * length, D)
        normed_one = low(layer_norm(flat, gain_one, shift_one))
        qkv_shift = jnp.concatenate([b_qv[0], jnp.zeros((D,), jnp.float32), b_qv[1]])
        qkv = low(low_back(matmul(normed_one, w_qkv) + qkv_shift))
        qkv = qkv.reshape(SEQS, length, 3, HEADS, HEAD)

        def per_sequence(parts):
            return attend_sequence(parts, key_pos)
        attn = lax.map(jax.checkpoint(per_sequence), (qkv[:, :, 0], qkv[:, :, 1], qkv[:, :, 2]))
        attn_low = low(low_back(attn.reshape(SEQS * length, D)))
        branch_one = low_back(matmul(attn_low, w_out) + b_out)
        middle = flat + branch_one
        normed_two = low(layer_norm(middle, gain_two, shift_two))
        hidden_pre = low_back(matmul(normed_two, w_fc) + b_fc)
        hidden = low(gelu_tanh(hidden_pre))
        output = middle + matmul(hidden, w_proj) + b_proj
        return output.reshape(SEQS, length, D)
    output, pullback = jax.vjp(forward, inputs, params)
    input_grad, grads = pullback(cotangent)
    shape = block_input.shape
    return (output.astype(jnp.bfloat16).reshape(shape), input_grad.astype(jnp.bfloat16).reshape(shape), grads[0], grads[1], grads[2], grads[3], grads[4], grads[5], grads[6], grads[7], grads[8], grads[9], grads[10], grads[11])
```

```python
import functools
import math

import jax
import jax.numpy as jnp
import numpy as np
from jax import lax
from jax.experimental import pallas as pl
from jax.experimental.pallas import tpu as pltpu
from jax.sharding import PartitionSpec as P

HEAD = 64
EPSILON = 1e-05
NEGATIVE = -1e30
GELU_COEF = 0.7978845608028654
LOW = jnp.bfloat16
FULL = jnp.float32


def norm_parts(values):
    center = values - jnp.mean(values, axis=-1, keepdims=True)
    rate = lax.rsqrt(jnp.mean(center * center, axis=-1, keepdims=True) + EPSILON)
    return center * rate, rate


def norm_back(grad, scaled, rate, gain):
    inner = grad * gain
    return rate * (
        inner
        - jnp.mean(inner, axis=-1, keepdims=True)
        - scaled * jnp.mean(inner * scaled, axis=-1, keepdims=True)
    )


def gelu_parts(values):
    square = values * values
    bent = jnp.tanh(GELU_COEF * values * (1.0 + 0.044715 * square))
    slope = 0.5 * (1.0 + bent) + 0.5 * values * (1.0 - bent * bent) * GELU_COEF * (
        1.0 + 3.0 * 0.044715 * square
    )
    return 0.5 * values * (1.0 + bent), slope


def dot(left, right):
    return jnp.dot(left, right, preferred_element_type=FULL)


def dot_t(left, right):
    return lax.dot_general(left, right, (((1,), (1,)), ((), ())), preferred_element_type=FULL)


def t_dot(left, right):
    return lax.dot_general(left, right, (((0,), (0,)), ((), ())), preferred_element_type=FULL)


def swap(values, axis, bit):
    count = lax.axis_size(axis)
    return lax.ppermute(values, axis, [(i, i ^ bit) for i in range(count)])


def ordered(flag, own, got):
    return jnp.where(flag == 0, own, got), jnp.where(flag == 0, got, own)


def joined(flag, own, got, axis):
    return jnp.concatenate(ordered(flag, own, got), axis)


def ring_order(count):
    return list(range(0, count, 2)) + list(range(count - 1, 0, -2))


def shift(values, offset):
    order = ring_order(lax.axis_size("ctx"))
    count = len(order)
    return lax.ppermute(
        values, "ctx", [(order[i], order[(i + offset) % count]) for i in range(count)]
    )


def ring_offsets(count):
    half = count // 2
    found = [0]
    for k in range(1, half):
        found += [-k, k]
    return found + [half]


def ring_gather(values):
    count = lax.axis_size("ctx")
    half = count // 2
    rows = values.shape[0] // 2
    ahead = [values[:rows], values[rows:]]
    behind = [values[:rows], values[rows:]]
    pieces = {0: values}
    for k in range(1, half):
        ahead = [shift(a, 1) for a in ahead]
        behind = [shift(b, -1) for b in behind]
        pieces[-k] = jnp.concatenate(ahead)
        pieces[k] = jnp.concatenate(behind)
    pieces[half] = jnp.concatenate([shift(ahead[0], 1), shift(behind[1], -1)])
    return [pieces[o] for o in ring_offsets(count)]


def ring_sum(pieces):
    count = lax.axis_size("ctx")
    half = count // 2
    held = dict(zip(ring_offsets(count), pieces, strict=True))
    rows = held[0].shape[0] // 2
    up = [held[half][:rows], None]
    down = [None, held[half][rows:]]
    for k in range(half - 1, -1, -1):
        for which in range(2):
            part = slice(which * rows, (which + 1) * rows)
            if up[which] is not None:
                got = shift(up[which].astype(LOW), 1).astype(FULL)
                up[which] = got if k == 0 else held[k][part] + got
            else:
                up[which] = held[k][part]
            if down[which] is not None:
                got = shift(down[which].astype(LOW), -1).astype(FULL)
                down[which] = got if k == 0 else held[-k][part] + got
            else:
                down[which] = held[-k][part]
    return held[0] + jnp.concatenate(up) + jnp.concatenate(down)


def square_gather(values):
    rows = values.shape[0] // 2
    one, two = values[:rows], values[rows:]
    one = jnp.concatenate([one, swap(one, "ctx", 1)])
    two = jnp.concatenate([two, swap(two, "ctx", 2)])
    near = jnp.concatenate([one, two])
    far = jnp.concatenate([swap(one, "ctx", 2), swap(two, "ctx", 1)])
    return jnp.concatenate([near, swap(near, "seq", 1), far, swap(far, "seq", 1)])


def square_sum(partial):
    rows = partial.shape[0] // 16
    near, near_other, far, far_other = jnp.split(partial, 4)
    far = far + swap(far_other.astype(LOW), "seq", 1).astype(FULL)
    near = near + swap(near_other.astype(LOW), "seq", 1).astype(FULL)
    one = near[: 2 * rows] + swap(far[: 2 * rows].astype(LOW), "ctx", 2).astype(FULL)
    two = near[2 * rows :] + swap(far[2 * rows :].astype(LOW), "ctx", 1).astype(FULL)
    one = one[:rows] + swap(one[rows:].astype(LOW), "ctx", 1).astype(FULL)
    two = two[:rows] + swap(two[rows:].astype(LOW), "ctx", 2).astype(FULL)
    return jnp.concatenate([one, two])


def sum_everywhere(values):
    for axis in ("seq", "ctx"):
        bit = 1
        while bit < lax.axis_size(axis):
            values = values + swap(values, axis, bit)
            bit *= 2
    return values


def head_plan(count, width):
    heads = width // HEAD
    group = -(-heads // count) * HEAD
    shard = 3 * width // count
    edges = []
    for to in range(count):
        for part in range(3):
            low = part * width + to * group
            high = min(part * width + (to + 1) * group, (part + 1) * width)
            for come in range(count):
                a, b = max(low, come * shard), min(high, (come + 1) * shard)
                if a < b:
                    edges.append((come, to, a - come * shard, part * group + a - low, b - a))
    edges.sort(key=lambda e: -e[4])
    rounds = []
    for edge in edges:
        for known in rounds:
            if all(edge[0] != e[0] and edge[1] != e[1] for e in known):
                known.append(edge)
                break
        else:
            rounds.append([edge])
    sent = np.full((count, len(rounds) * group), -1, np.int32)
    kept = np.full((count, 3 * group), -1, np.int32)
    pairs = []
    for number, known in enumerate(rounds):
        pairs.append([(e[0], e[1]) for e in known])
        for come, to, start, place, size in known:
            sent[come, number * group : number * group + size] = np.arange(start, start + size)
            kept[to, place : place + size] = number * group + np.arange(size)
    return group, pairs, sent, kept


def picker(places, size):
    return (lax.broadcasted_iota(jnp.int32, (size, places.shape[0]), 0) == places[None, :]).astype(LOW)


def to_heads(shard, group, pairs, pick_sent, pick_kept):
    sent = dot(shard, pick_sent).astype(LOW)
    got = [
        lax.ppermute(sent[:, i * group : (i + 1) * group], "ctx", pairs[i])
        for i in range(len(pairs))
    ]
    return dot(jnp.concatenate(got, axis=1), pick_kept).astype(LOW)


def from_heads(held, group, pairs, pick_sent, pick_kept):
    sent = dot_t(held, pick_kept).astype(LOW)
    got = [
        lax.ppermute(sent[:, i * group : (i + 1) * group], "ctx", [(b, a) for a, b in pairs[i]])
        for i in range(len(pairs))
    ]
    return dot_t(jnp.concatenate(got, axis=1), pick_sent)


def attend_kernel(heads, q_ref, k_ref, v_ref, row_ref, col_ref, full_ref, low_ref, lse_ref):
    allowed = col_ref[...] <= row_ref[...]
    for h in range(heads):
        part = slice(h * HEAD, (h + 1) * HEAD)
        query = q_ref[:, part] * (1.0 / math.sqrt(HEAD))
        score = jnp.where(allowed, dot_t(query.astype(LOW), k_ref[:, part]), NEGATIVE)
        top = jnp.max(score, axis=1, keepdims=True)
        weight = jnp.exp(score - top)
        total = jnp.sum(weight, axis=1, keepdims=True)
        result = dot(weight.astype(LOW), v_ref[:, part]) / total
        full_ref[:, part] = result
        low_ref[:, part] = result.astype(LOW)
        lse_ref[:, h : h + 1] = top + jnp.log(total)


def attend_back_kernel(
    heads, q_ref, k_ref, v_ref, row_ref, col_ref, full_ref, lse_ref, grad_ref, dq_ref, dk_ref, dv_ref
):
    @pl.when(pl.program_id(0) == 0)
    def _():
        dk_ref[...] = jnp.zeros_like(dk_ref)
        dv_ref[...] = jnp.zeros_like(dv_ref)

    allowed = col_ref[...] <= row_ref[...]
    scale = 1.0 / math.sqrt(HEAD)
    for h in range(heads):
        part = slice(h * HEAD, (h + 1) * HEAD)
        query = (q_ref[:, part] * scale).astype(LOW)
        grad = grad_ref[:, part]
        delta = jnp.sum(grad.astype(FULL) * full_ref[:, part], axis=1, keepdims=True)
        score = dot_t(query, k_ref[:, part])
        prob = jnp.where(allowed, jnp.exp(score - lse_ref[:, h : h + 1]), 0.0)
        prob_grad = dot_t(grad, v_ref[:, part])
        score_grad = (prob * (prob_grad - delta)).astype(LOW)
        dq_ref[:, part] = (dot(score_grad, k_ref[:, part]) * scale).astype(LOW)
        dk_ref[:, part] += t_dot(score_grad, query)
        dv_ref[:, part] += t_dot(prob.astype(LOW), grad)


def attend_sizes(qkv):
    tokens, group = qkv.shape[0], qkv.shape[1] // 3
    rows = min(256, tokens)
    return tokens, group, rows


def attend(qkv, pos):
    tokens, group, rows = attend_sizes(qkv)
    heads = group // HEAD
    q, k, v = qkv[:, :group], qkv[:, group : 2 * group], qkv[:, 2 * group :]
    some = pl.BlockSpec((rows, group), lambda i: (i, 0))
    whole = pl.BlockSpec((tokens, group), lambda i: (0, 0))
    return pl.pallas_call(
        functools.partial(attend_kernel, heads),
        grid=(tokens // rows,),
        in_specs=[
            some,
            whole,
            whole,
            pl.BlockSpec((rows, 1), lambda i: (i, 0)),
            pl.BlockSpec((1, tokens), lambda i: (0, 0)),
        ],
        out_specs=[some, some, pl.BlockSpec((rows, heads), lambda i: (i, 0))],
        out_shape=[
            jax.ShapeDtypeStruct((tokens, group), FULL),
            jax.ShapeDtypeStruct((tokens, group), LOW),
            jax.ShapeDtypeStruct((tokens, heads), FULL),
        ],
        compiler_params=pltpu.CompilerParams(vmem_limit_bytes=48 * 2**20),
        cost_estimate=pl.CostEstimate(
            flops=4 * tokens * tokens * group,
            bytes_accessed=12 * tokens * group,
            transcendentals=tokens * tokens * heads,
        ),
        name="attend",
    )(q, k, v, pos[:, None], pos[None, :])


def attend_back(qkv, pos, full, lse, grad):
    tokens, group, rows = attend_sizes(qkv)
    heads = group // HEAD
    q, k, v = qkv[:, :group], qkv[:, group : 2 * group], qkv[:, 2 * group :]
    some = pl.BlockSpec((rows, group), lambda i: (i, 0))
    whole = pl.BlockSpec((tokens, group), lambda i: (0, 0))
    return pl.pallas_call(
        functools.partial(attend_back_kernel, heads),
        grid=(tokens // rows,),
        in_specs=[
            some,
            whole,
            whole,
            pl.BlockSpec((rows, 1), lambda i: (i, 0)),
            pl.BlockSpec((1, tokens), lambda i: (0, 0)),
            some,
            pl.BlockSpec((rows, heads), lambda i: (i, 0)),
            some,
        ],
        out_specs=[some, whole, whole],
        out_shape=[
            jax.ShapeDtypeStruct((tokens, group), LOW),
            jax.ShapeDtypeStruct((tokens, group), FULL),
            jax.ShapeDtypeStruct((tokens, group), FULL),
        ],
        compiler_params=pltpu.CompilerParams(vmem_limit_bytes=48 * 2**20),
        cost_estimate=pl.CostEstimate(
            flops=10 * tokens * tokens * group,
            bytes_accessed=24 * tokens * group,
            transcendentals=tokens * tokens * heads,
        ),
        name="attend_back",
    )(q, k, v, pos[:, None], pos[None, :], full, lse, grad)


def high_bits():
    bits, bit = [], 4
    while bit < lax.axis_size("ctx"):
        bits.append(bit)
        bit *= 2
    return bits


def unit_rows(shard, core, row):
    parts = shard.reshape(2, shard.shape[0] // 2, shard.shape[1])
    mine, other = ordered(core, parts[0], parts[1])
    held = joined(core, mine, swap(other, "seq", 1), 1)[None]
    for bit in high_bits():
        held = jnp.concatenate([held, swap(held, "ctx", bit)])
    held = joined(row, held, swap(held, "seq", 2), 2)
    return held.reshape(-1, held.shape[2])


def unit_rows_sum(grad, core, row):
    count = 2 ** len(high_bits())
    half = grad.shape[1] // 2
    keep, send = ordered(row, grad[:, :half], grad[:, half:])
    held = keep + swap(send.astype(LOW), "seq", 2).astype(FULL)
    held = held.reshape(count, -1, half)
    for bit in reversed(high_bits()):
        some = held.shape[0] // 2
        held = held[:some] + swap(held[some:].astype(LOW), "ctx", bit).astype(FULL)
    held = held[0]
    keep, send = ordered(core, held[:, : half // 2], held[:, half // 2 :])
    return joined(core, keep, swap(send, "seq", 1), 0)


def whole_out_weight(shard, core, row, ctx):
    held = jnp.transpose(shard)[None]
    bits = lax.axis_size("ctx").bit_length() - 1
    held = held.reshape((1,) * bits + held.shape[1:])
    for place in range(bits):
        bit = bits - 1 - place
        flag = (ctx >> bit) & 1
        held = joined(flag, held, swap(held, "ctx", 1 << bit), place)
    held = held.reshape(-1, held.shape[-1])
    both = jnp.stack(ordered(row, held, swap(held, "seq", 2)))
    peer = swap(both, "seq", 1)
    return jnp.concatenate([joined(core, both[i], peer[i], 1) for i in range(2)], axis=1)


def out_weight_sum(attn_low, branch_low, core, row, ctx):
    part = attn_low.shape[1] // 4
    blocks = [attn_low[:, i * part : (i + 1) * part] for i in range(4)]
    mine, other = ordered(
        core, jnp.concatenate([blocks[0], blocks[2]], 1), jnp.concatenate([blocks[1], blocks[3]], 1)
    )
    got = swap(t_dot(branch_low, other).astype(LOW), "seq", 1)
    held = t_dot(branch_low, mine) + got.astype(FULL)
    count = lax.axis_size("ctx")
    held = held.reshape(count, -1, held.shape[1])
    bit = 1
    while bit < count:
        flag = lax.bitwise_and(ctx, bit)
        held = held.reshape(held.shape[0] // 2, 2, *held.shape[1:])
        keep, send = ordered(flag, held[:, 0], held[:, 1])
        held = keep + swap(send.astype(LOW), "ctx", bit).astype(FULL)
        bit *= 2
    held = held[0]
    keep, send = ordered(row, held[:, :part], held[:, part:])
    return jnp.transpose(keep + swap(send.astype(LOW), "seq", 2).astype(FULL))


def body(
    block_input,
    out_cot,
    pair_of,
    ln1_gain,
    ln1_bias,
    qkv_weight,
    qv_bias,
    out_weight,
    out_bias,
    ln2_gain,
    ln2_bias,
    fc_weight,
    fc_bias,
    proj_weight,
    proj_bias,
):
    rows, width = block_input.shape[2], block_input.shape[3]
    block = rows // 2
    count = lax.axis_size("ctx")
    seq, ctx = lax.axis_index("seq"), lax.axis_index("ctx")
    core, row = seq % 2, seq // 2
    order = ring_order(count)
    place = np.argsort(np.array(order)).astype(np.int32)
    mine = jnp.asarray(place)[ctx]
    offsets = ring_offsets(count)
    inputs = block_input.reshape(rows, width).astype(FULL)
    cot_low = out_cot.reshape(rows, width)
    cot_full = cot_low.astype(FULL)

    members = jnp.asarray(np.array(order, np.int32))[(mine + np.array(offsets, np.int32)) % count]
    pairs = pair_of[members]
    inner = jnp.arange(block, dtype=jnp.int32)
    pos = jnp.stack(
        [pairs[:, None] * block + inner, (2 * count - 1 - pairs)[:, None] * block + inner], axis=1
    ).reshape(-1)

    scaled_one, rate_one = norm_parts(inputs)
    normed_one = (scaled_one * ln1_gain + ln1_bias).astype(LOW)
    group, rounds, sent, kept = head_plan(count, width)
    pick_sent = picker(jnp.asarray(sent)[ctx], qkv_weight.shape[1])
    pick_kept = picker(jnp.asarray(kept)[ctx], sent.shape[1])
    qkv_part = to_heads(qkv_weight, group, rounds, pick_sent, pick_kept)
    qkv_pair = ordered(row, qkv_part, swap(qkv_part, "seq", 2))
    qkv_pair = jnp.stack(qkv_pair)
    qkv_peer = swap(qkv_pair, "seq", 1)
    first, second = ordered(core, qkv_pair, qkv_peer)
    qkv_cols = jnp.stack([first, second], axis=1).reshape(width, 3 * group)
    bias_rows = jnp.pad(qv_bias, ((0, 0), (0, count * group - width)))
    bias_mine = lax.dynamic_slice_in_dim(bias_rows, ctx * group, group, 1)
    qkv_shift = jnp.concatenate([bias_mine[0], jnp.zeros((group,), FULL), bias_mine[1]])

    gathered = ring_gather(normed_one)
    qkv = jnp.concatenate([(dot(x, qkv_cols) + qkv_shift).astype(LOW) for x in gathered])
    attn_full, attn_part, lse = attend(qkv, pos)

    def chunk(values, at):
        return values[at * rows : (at + 1) * rows]

    at_offset = {o % count: i for i, o in enumerate(offsets)}
    back = [
        chunk(attn_part, at_offset[0]) if o == 0 else shift(chunk(attn_part, at_offset[(-o) % count]), -o)
        for o in range(count)
    ]
    back = jnp.stack(back)
    where_is = (jnp.asarray(place) - mine) % count
    attn_low = jnp.concatenate(
        [lax.dynamic_index_in_dim(back, where_is[d], keepdims=False) for d in range(count)], axis=1
    )[:, :width]
    out_rows = whole_out_weight(out_weight, core, row, ctx)
    middle = inputs + dot_t(attn_low, out_rows) + out_bias

    scaled_two, rate_two = norm_parts(middle)
    normed_two = (scaled_two * ln2_gain + ln2_bias).astype(LOW)
    fc_rows = unit_rows(jnp.transpose(fc_weight), core, row)
    proj_rows = unit_rows(proj_weight, core, row)
    high = 2 ** len(high_bits())
    units = jnp.concatenate(
        [
            lax.dynamic_index_in_dim(
                fc_bias.reshape(2 * count, -1), 2 * (ctx ^ (4 * j)) + core, keepdims=False
            )
            for j in range(high)
        ]
    )
    cots = square_gather(cot_low)
    hidden_grad = dot_t(cots, proj_rows)
    tokens = square_gather(normed_two)
    hidden_pre = dot_t(tokens, fc_rows) + units
    value, slope = gelu_parts(hidden_pre)
    hidden = value.astype(LOW)
    hidden_pre_grad = (hidden_grad * slope).astype(LOW)
    normed_two_grad = square_sum(dot(hidden_pre_grad, fc_rows))
    branch_two = square_sum(dot(hidden, proj_rows))
    block_output = (middle + branch_two + proj_bias).astype(LOW).reshape(block_input.shape)
    proj_weight_grad = unit_rows_sum(t_dot(hidden, cots), core, row)
    fc_weight_grad = jnp.transpose(unit_rows_sum(t_dot(hidden_pre_grad, tokens), core, row))
    units_grad = jnp.sum(hidden_pre_grad.astype(FULL), axis=0).reshape(high, -1)

    middle_grad = cot_full + norm_back(normed_two_grad, scaled_two, rate_two, ln2_gain)
    branch_low = middle_grad.astype(LOW)
    attn_grad = jnp.pad(dot(branch_low, out_rows).astype(LOW), ((0, 0), (0, count * group - width)))
    attn_grad = jnp.stack([attn_grad[:, d * group : (d + 1) * group] for d in range(count)])
    whose = jnp.asarray(np.array(order, np.int32))[(mine + np.arange(count, dtype=np.int32)) % count]
    came = {}
    for o in range(count):
        piece = lax.dynamic_index_in_dim(attn_grad, whose[o], keepdims=False)
        came[(-o) % count] = piece if o == 0 else shift(piece, o)
    grad_part = jnp.concatenate([came[o % count] for o in offsets])
    out_weight_grad = out_weight_sum(attn_low, branch_low, core, row, ctx)

    query_grad, key_grad, value_grad = attend_back(qkv, pos, attn_full, lse, grad_part)
    qkv_grad = jnp.concatenate([query_grad, key_grad.astype(LOW), value_grad.astype(LOW)], axis=1)
    normed_one_grad = ring_sum([dot_t(chunk(qkv_grad, i), qkv_cols) for i in range(count)])
    middle_part = norm_back(normed_one_grad, scaled_one, rate_one, ln1_gain)
    input_grad = (middle_grad + middle_part).astype(LOW).reshape(block_input.shape)

    whole = t_dot(jnp.concatenate(gathered), qkv_grad).reshape(2, 2, -1, 3 * group)
    keep, send = ordered(core, whole[:, 0], whole[:, 1])
    whole = keep + swap(send.astype(LOW), "seq", 1).astype(FULL)
    keep, send = ordered(row, whole[0], whole[1])
    whole = keep + swap(send.astype(LOW), "seq", 2).astype(FULL)
    qkv_weight_grad = from_heads(whole.astype(LOW), group, rounds, pick_sent, pick_kept)

    qkv_sums = jnp.sum(qkv_grad.astype(FULL), axis=0)
    qv_sums = jnp.stack([qkv_sums[:group], qkv_sums[2 * group :]])
    qv_sums = lax.dynamic_update_slice(
        jnp.zeros((2, count * group), FULL), qv_sums, (0, ctx * group)
    )[:, :width]
    unit_sums = jnp.zeros((2 * count, units_grad.shape[1]), FULL)
    for j in range(high):
        unit_sums = lax.dynamic_update_slice(
            unit_sums, units_grad[j : j + 1], (2 * (ctx ^ (4 * j)) + core, 0)
        )
    early = jnp.concatenate(
        [
            jnp.sum(branch_low.astype(FULL), axis=0),
            jnp.sum(normed_two_grad * scaled_two, axis=0),
            jnp.sum(normed_two_grad, axis=0),
            unit_sums.reshape(-1),
            jnp.sum(cot_full, axis=0),
        ]
    )
    early = sum_everywhere(early)
    late = jnp.concatenate(
        [
            jnp.sum(normed_one_grad * scaled_one, axis=0),
            jnp.sum(normed_one_grad, axis=0),
            qv_sums.reshape(-1),
        ]
    )
    late = sum_everywhere(late)
    ends = np.cumsum([0, width, width, width, fc_bias.shape[0], width])
    out_bias_grad, ln2_gain_grad, ln2_bias_grad, fc_bias_grad, proj_bias_grad = [
        early[ends[i] : ends[i + 1]] for i in range(5)
    ]
    return (
        block_output,
        input_grad,
        late[:width],
        late[width : 2 * width],
        qkv_weight_grad,
        late[2 * width :].reshape(2, width),
        out_weight_grad,
        out_bias_grad,
        ln2_gain_grad,
        ln2_bias_grad,
        fc_weight_grad,
        fc_bias_grad,
        proj_weight_grad,
        proj_bias_grad,
    )


def solution(mesh):
    rows = P("seq", "ctx", None, None)
    cols = P("seq", "ctx")
    flip = P("ctx", "seq")
    one = P()
    return jax.shard_map(
        body,
        mesh=mesh,
        in_specs=(rows, rows, one, one, one, cols, one, cols, one, one, one, cols, one, flip, one),
        out_specs=(rows, rows, one, one, cols, one, cols, one, one, one, cols, one, flip, one),
        check_vma=False,
    )
```

```python
import functools
import math
import random

import jax
import jax.numpy as jnp
import numpy as np
from jax import lax
from jax.experimental import pallas as pl
from jax.experimental.pallas import tpu as pltpu
from jax.sharding import PartitionSpec as P

HEAD = 64
EPSILON = 1e-05
NEGATIVE = -1e30
GELU_COEF = 0.7978845608028654
LOW = jnp.bfloat16
FULL = jnp.float32
VMEM_BYTES = 56 * 2**20


def norm_parts(values):
    center = values - jnp.mean(values, axis=-1, keepdims=True)
    rate = lax.rsqrt(jnp.mean(center * center, axis=-1, keepdims=True) + EPSILON)
    return center * rate, rate


def norm_back(grad, scaled, rate, gain):
    inner = grad * gain
    return rate * (
        inner
        - jnp.mean(inner, axis=-1, keepdims=True)
        - scaled * jnp.mean(inner * scaled, axis=-1, keepdims=True)
    )


def gelu_parts(values):
    square = values * values
    bent = jnp.tanh(GELU_COEF * values * (1.0 + 0.044715 * square))
    slope = 0.5 * (1.0 + bent) + 0.5 * values * (1.0 - bent * bent) * GELU_COEF * (
        1.0 + 3.0 * 0.044715 * square
    )
    return 0.5 * values * (1.0 + bent), slope


def dot(left, right):
    return jnp.dot(left, right, preferred_element_type=FULL)


def dot_t(left, right):
    return lax.dot_general(left, right, (((1,), (1,)), ((), ())), preferred_element_type=FULL)


def t_dot(left, right):
    return lax.dot_general(left, right, (((0,), (0,)), ((), ())), preferred_element_type=FULL)


def swap(values, axis, bit):
    count = lax.axis_size(axis)
    return lax.ppermute(values, axis, [(i, i ^ bit) for i in range(count)])


def pick(values, places, count):
    return jnp.stack([lax.dynamic_index_in_dim(values, places[i], keepdims=False) for i in range(count)])


def ordered(flag, own, got):
    return jnp.where(flag == 0, own, got), jnp.where(flag == 0, got, own)


def joined(flag, own, got, axis):
    return jnp.concatenate(ordered(flag, own, got), axis)


def after(value, *first):
    return lax.optimization_barrier((value, *first))[0]


def ring_order(count):
    return list(range(0, count, 2)) + list(range(count - 1, 0, -2))


def shift(values, offset):
    order = ring_order(lax.axis_size("ctx"))
    count = len(order)
    return lax.ppermute(
        values, "ctx", [(order[i], order[(i + offset) % count]) for i in range(count)]
    )


def ring_gather(values, riders=()):
    count = lax.axis_size("ctx")
    half, rows = count // 2, values.shape[0] // 2
    ahead = behind = values
    riders = list(riders)
    pieces = [values] + [None] * (count - 1)
    for k in range(1, half + 1):
        rode = riders.pop(0)(lambda x, *more: after(x, ahead, behind, *more)) if riders else ()
        if k == half:
            pieces[half] = (shift(ahead[:rows], 1), shift(behind[rows:], -1))
            break
        ahead, behind = shift(ahead, 1), shift(behind, -1)
        pieces[count - k], pieces[k] = ahead, behind
        if rode:
            ahead, behind, *_ = lax.optimization_barrier((ahead, behind, *rode))
    return pieces[:half] + list(pieces[half]) + pieces[half + 1 :]


def ring_sum(held, far, riders=()):
    count = lax.axis_size("ctx")
    half, rows = count // 2, far.shape[0] // 2
    riders = list(riders)
    up, down = far[:rows], far[rows:]
    for k in range(half - 1, -1, -1):
        rode = riders.pop(0)(lambda x, *more: after(x, up, down, *more)) if riders else ()
        low_up, low_down = up.astype(LOW), down.astype(LOW)
        up, down = shift(low_up, 1).astype(FULL), shift(low_down, -1).astype(FULL)
        if k == half - 1:
            near, back = held[k], held[count - k]
            up = jnp.concatenate([near[:rows] + up, near[rows:]])
            down = jnp.concatenate([back[:rows], back[rows:] + down])
        elif k:
            up, down = held[k] + up, held[count - k] + down
        if rode:
            up, down, *_ = lax.optimization_barrier((up, down, *rode))
    return held[0] + up + down


def sum_over(values, axis):
    bit = 1
    while bit < lax.axis_size(axis):
        values = values + swap(values, axis, bit)
        bit *= 2
    return values


def seq_parts(shard):
    other = swap(shard, "seq", 2)
    pair = jnp.stack([shard, other])
    return pair, swap(pair, "seq", 1)


def seq_columns(tokens, core):
    part = tokens.shape[1] // 4
    blocks = [tokens[:, i * part : (i + 1) * part] for i in range(4)]
    return ordered(
        core, jnp.concatenate([blocks[0], blocks[2]], 1), jnp.concatenate([blocks[1], blocks[3]], 1)
    )


def seq_halves(held, got, row):
    half = held.shape[-2] // 2
    held = held + got.astype(FULL)
    keep, send = ordered(row, held[..., :half, :], held[..., half:, :])
    return keep, send.astype(LOW)


def head_plan(count, width):
    heads = width // HEAD
    group = -(-heads // count) * HEAD
    shard = 3 * width // count
    small = min(group, 128)
    edges = []
    for to in range(count):
        for part in range(3):
            low = part * width + to * group
            high = min(part * width + (to + 1) * group, (part + 1) * width)
            for come in range(count):
                a, b = max(low, come * shard), min(high, (come + 1) * shard)
                if a < b:
                    edges.append((come, to, a - come * shard, part * group + a - low, b - a))
    draw = random.Random(0)
    best, least = None, None
    for _ in range(300):
        draw.shuffle(edges)
        rounds = []
        for edge in sorted(edges, key=lambda e: e[4] <= small):
            for known in rounds:
                if all(edge[0] != e[0] and edge[1] != e[1] for e in known):
                    known.append(edge)
                    break
            else:
                rounds.append([edge])
        cost = sum(200 + (small if all(e[4] <= small for e in r) else group) for r in rounds)
        if least is None or cost < least:
            best, least = [list(r) for r in rounds], cost
    pairs, starts, sizes, total = [], [], [], 0
    for known in best:
        pairs.append([(e[0], e[1]) for e in known])
        starts.append(total)
        sizes.append(small if all(e[4] <= small for e in known) else group)
        total += sizes[-1]
    sent = np.full((count, total), -1, np.int32)
    kept = np.full((count, 3 * group), -1, np.int32)
    for known, begin in zip(best, starts, strict=True):
        for come, to, start, place, size in known:
            sent[come, begin : begin + size] = np.arange(start, start + size)
            kept[to, place : place + size] = begin + np.arange(size)
    moves = list(zip(pairs, starts, sizes, strict=True))
    return group, moves, sent, kept


def picker(places, size):
    return (lax.broadcasted_iota(jnp.int32, (size, places.shape[0]), 0) == places[None, :]).astype(LOW)


def move(values, pairs):
    return values if all(a == b for a, b in pairs) else lax.ppermute(values, "ctx", pairs)


def take_rounds(sent, moves):
    return [move(sent[:, start : start + size], pairs) for pairs, start, size in moves]


def from_heads(sent, moves, pick_sent):
    got = [
        move(sent[:, start : start + size], [(b, a) for a, b in pairs]) for pairs, start, size in moves
    ]
    return dot_t(jnp.concatenate(got, axis=1), pick_sent)


COST_US = {
    "attend": 15,
    "out": 8,
    "hidden_grad": 9,
    "hidden": 20,
    "branch": 8,
    "out_back": 12,
    "unit_other": 8,
    "unit_mine": 10,
    "qkv_other": 5,
    "qkv_mine": 6,
    "attend_back": 20,
    "project_back": 6,
}


def call(kernel, outs, args, scalars, name, flops, scratch=()):
    spec = [pl.BlockSpec(memory_space=pltpu.SMEM)] * len(scalars)
    spec += [pl.BlockSpec(memory_space=pltpu.VMEM)] * len(args)
    moved = sum(math.prod(a.shape) * a.dtype.itemsize for a in args)
    moved += sum(math.prod(o[0]) * jnp.dtype(o[1]).itemsize for o in outs)
    return pl.pallas_call(
        kernel,
        in_specs=spec,
        out_specs=[pl.BlockSpec(memory_space=pltpu.VMEM)] * len(outs),
        out_shape=[jax.ShapeDtypeStruct(s, d) for s, d in outs],
        scratch_shapes=list(scratch),
        compiler_params=pltpu.CompilerParams(vmem_limit_bytes=VMEM_BYTES),
        cost_estimate=pl.CostEstimate(flops=1000, bytes_accessed=int(COST_US[name] * 3e6), transcendentals=0),
        name=name,
    )(*scalars, *args)


def put_tokens(member_ref, pieces, put, rows, count):
    half, middle = count // 2, rows // 2
    at = 0
    for k in range(count):
        member = member_ref[k]
        if k == half:
            put(member, 0, pieces[at][...])
            put(member, 1, pieces[at + 1][...])
            at += 2
        else:
            put(member, 0, pieces[at][:middle, :])
            put(member, 1, pieces[at][middle:, :])
            at += 1


def put_shards(place_ref, pair_ref, peer_ref, out_ref):
    seq = place_ref[0]
    height = out_ref.shape[0] // 4
    for k in range(4):
        source = pair_ref if k % 2 == 0 else peer_ref
        start = pl.multiple_of((seq ^ k) * height, 16)
        out_ref[pl.ds(start, height), :] = source[k // 2]


def causal(step, start, keys):
    query = lax.broadcasted_iota(jnp.int32, (step, keys), 0) + start
    return lax.broadcasted_iota(jnp.int32, (step, keys), 1) <= query


def each_step(tokens, run):
    if tokens <= 1024:
        step = min(256, tokens)
        for start in range(0, tokens, step):
            run(start, slice(start, start + step), step, start + step)
    else:
        step = 128

        @pl.loop(0, tokens // step)
        def _(i):
            start = pl.multiple_of(i * step, step)
            run(start, pl.ds(start, step), step, tokens)


def attend_kernel(
    n_pieces, heads, member_ref, place_ref, pair_of_ref, who_ref, pair_ref, peer_ref, shift_ref, *rest
):
    pieces = rest[:n_pieces]
    x_ref, w_ref, qkv_ref, full_ref, low_ref, lse_ref = rest[n_pieces:]
    count, rows, group = low_ref.shape
    tokens, block = count * rows, rows // 2
    put_shards(place_ref, pair_ref, peer_ref, w_ref)

    def put(member, half, values):
        pair = pair_of_ref[member]
        at = (2 * count - 1 - pair if half else pair) * block
        x_ref[pl.ds(pl.multiple_of(at, block), block), :] = values

    put_tokens(member_ref, pieces, put, rows, count)

    def project(start, part, step, keys):
        qkv_ref[part, :] = (dot(x_ref[part, :], w_ref[...]) + shift_ref[...]).astype(LOW)

    def some(start, part, step, keys):
        allowed = causal(step, start, keys)
        for h in range(heads):
            a, b = h * HEAD, (h + 1) * HEAD
            query = (qkv_ref[part, a:b] * (1.0 / math.sqrt(HEAD))).astype(LOW)
            score = jnp.where(allowed, dot_t(query, qkv_ref[:keys, group + a : group + b]), NEGATIVE)
            top = jnp.max(score, axis=1, keepdims=True)
            weight = jnp.exp(score - top)
            total = jnp.sum(weight, axis=1, keepdims=True)
            result = dot(weight.astype(LOW), qkv_ref[:keys, 2 * group + a : 2 * group + b]) / total
            full_ref[part, a:b] = result
            lse_ref[part, h : h + 1] = top + jnp.log(total)

    each_step(tokens, project)
    each_step(tokens, some)
    for j in range(2 * count):
        half = j // count * block
        low_ref[who_ref[j], half : half + block, :] = full_ref[j * block : (j + 1) * block, :].astype(LOW)


def attend_back_kernel(
    heads,
    who_ref,
    far_ref,
    qkv_ref,
    w_ref,
    full_ref,
    lse_ref,
    come_ref,
    out_ref,
    sum_ref,
    low_ref,
    dk_ref,
    dv_ref,
    grad_ref,
):
    count, rows, group = come_ref.shape
    tokens, block = count * rows, rows // 2
    scale = 1.0 / math.sqrt(HEAD)
    dk_ref[...] = jnp.zeros_like(dk_ref)
    dv_ref[...] = jnp.zeros_like(dv_ref)
    for j in range(2 * count):
        half = j // count * block
        grad_ref[j * block : (j + 1) * block, :] = come_ref[who_ref[j], half : half + block, :]

    def some(start, part, step, keys):
        allowed = causal(step, start, keys)
        for h in range(heads):
            a, b = h * HEAD, (h + 1) * HEAD
            query = (qkv_ref[part, a:b] * scale).astype(LOW)
            key = qkv_ref[:keys, group + a : group + b]
            value = qkv_ref[:keys, 2 * group + a : 2 * group + b]
            grad = grad_ref[part, a:b]
            delta = jnp.sum(grad.astype(FULL) * full_ref[part, a:b], axis=1, keepdims=True)
            score = dot_t(query, key)
            prob = jnp.where(allowed, jnp.exp(score - lse_ref[part, h : h + 1]), 0.0)
            score_grad = (prob * (dot_t(grad, value) - delta)).astype(LOW)
            out_ref[part, a:b] = (dot(score_grad, key) * scale).astype(LOW)
            dk_ref[:keys, a:b] += t_dot(score_grad, query)
            dv_ref[:keys, a:b] += t_dot(prob.astype(LOW), grad)

    each_step(tokens, some)
    out_ref[:, group : 2 * group] = dk_ref[...].astype(LOW)
    out_ref[:, 2 * group :] = dv_ref[...].astype(LOW)
    sum_ref[...] = jnp.sum(out_ref[...].astype(FULL), axis=0, keepdims=True)
    for half in range(2):
        start = pl.multiple_of(far_ref[half] * block, block)
        low_ref[half * block : (half + 1) * block, :] = dot_t(out_ref[pl.ds(start, block), :], w_ref[...]).astype(LOW)


def project_back_kernel(far_ref, grad_ref, w_ref, x_ref, norm_ref, gain_ref):
    count, rows, width = norm_ref.shape
    tokens, block = count * rows, rows // 2
    gain_ref[...] = jnp.zeros_like(gain_ref)
    step = min(256, tokens)
    for start in range(0, tokens, step):
        part = slice(start, start + step)
        total = dot_t(grad_ref[part, :], w_ref[...])
        gain_ref[0:1, :] += jnp.sum(total * x_ref[part, :].astype(FULL), axis=0, keepdims=True)
        gain_ref[1:2, :] += jnp.sum(total, axis=0, keepdims=True)
        for j in range(start // block, (start + step) // block):
            half, at = j // count * block, j * block - start
            norm_ref[far_ref[j], half : half + block, :] = total[at : at + block, :]


def put_ring(offset, count, full_ref, low_ref, start, values):
    end = start + values.shape[0]

    @pl.when(offset == count // 2)
    def _():
        low_ref[start:end, :] = values.astype(LOW)

    @pl.when(offset != count // 2)
    def _():
        full_ref[offset, start:end, :] = values


def out_kernel(back_ref, input_ref, bias_ref, gain_ref, shift_ref, w_ref, mid_ref, low_ref, scaled_ref, rate_ref, attn_ref, wide_ref):
    count, rows, group = back_ref.shape
    width = mid_ref.shape[1]
    for d in range(count):
        wide_ref[:, d * group : (d + 1) * group] = back_ref[d]
    attn_ref[...] = wide_ref[:, :width]
    quarter, size = w_ref.shape[3], w_ref.shape[2]
    mid_ref[...] = input_ref[...].astype(FULL) + bias_ref[...]
    parts = [attn_ref[:, s * quarter : (s + 1) * quarter] for s in range(4)]
    for d in range(count):
        total = dot_t(parts[0], w_ref[0, d])
        for s in range(1, 4):
            total = total + dot_t(parts[s], w_ref[s, d])
        mid_ref[:, d * size : (d + 1) * size] += total
    scaled, rate = norm_parts(mid_ref[...])
    scaled_ref[...] = scaled
    rate_ref[...] = rate
    low_ref[...] = (scaled * gain_ref[...] + shift_ref[...]).astype(LOW)


def out_back_kernel(
    core_ref,
    sum_ref,
    cot_ref,
    scaled_ref,
    rate_ref,
    gain_ref,
    w_ref,
    attn_ref,
    mid_ref,
    low_ref,
    grad_ref,
    line_ref,
    mine_ref,
    other_ref,
    wide_ref,
    part_ref,
):
    count, rows, group = grad_ref.shape
    width = mid_ref.shape[1]
    cot = cot_ref[...].astype(FULL)
    total, scaled = sum_ref[...], scaled_ref[...]
    mid_ref[...] = cot + norm_back(total, scaled, rate_ref[...], gain_ref[...])
    low_ref[...] = mid_ref[...].astype(LOW)
    line_ref[0:1, :] = jnp.sum(low_ref[...].astype(FULL), axis=0, keepdims=True)
    line_ref[1:2, :] = jnp.sum(total * scaled, axis=0, keepdims=True)
    line_ref[2:3, :] = jnp.sum(total, axis=0, keepdims=True)
    line_ref[3:4, :] = jnp.sum(cot, axis=0, keepdims=True)
    quarter, size = w_ref.shape[3], w_ref.shape[2]
    wide_ref[:, width:] = jnp.zeros((rows, count * group - width), LOW)
    parts = [low_ref[:, d * size : (d + 1) * size] for d in range(count)]
    for s in range(4):
        part_ref[s] = attn_ref[:, s * quarter : (s + 1) * quarter]
        total = dot(parts[0], w_ref[s, 0])
        for d in range(1, count):
            total = total + dot(parts[d], w_ref[s, d])
        wide_ref[:, s * quarter : (s + 1) * quarter] = total.astype(LOW)
    core = core_ref[0]
    for d in range(count):
        grad_ref[d] = wide_ref[:, d * group : (d + 1) * group]
        for y in range(2):
            lanes = slice(y * quarter, (y + 1) * quarter)
            mine_ref[d, :, lanes] = t_dot(parts[d], part_ref[2 * y + core])
            other_ref[d, :, lanes] = t_dot(parts[d], part_ref[2 * y + 1 - core]).astype(LOW)


def seq_dots(core, left_ref, right, put):
    part = left_ref.shape[1] // 4
    for some in range(2):

        @pl.when(core == some)
        def _(some=some):
            for y in range(2):
                at = (2 * y + some) * part
                put(y, t_dot(left_ref[:, at : at + part], right))


def other_kernel(core_ref, *rest):
    *pairs, out_ref = rest

    for m in range(len(pairs) // 2):

        def put(y, total, m=m):
            out_ref[m, y] = total.astype(LOW)

        seq_dots(1 - core_ref[0], pairs[2 * m], pairs[2 * m + 1][...], put)


def mine_kernel(core_ref, row_ref, got_ref, *rest):
    *pairs, keep_ref, send_ref = rest

    for m in range(len(pairs) // 2):

        def put(y, total, m=m):
            total = total + got_ref[m, y].astype(FULL)

            @pl.when(row_ref[0] == y)
            def _():
                keep_ref[m] = total

            @pl.when(row_ref[0] != y)
            def _():
                send_ref[m] = total.astype(LOW)

        seq_dots(core_ref[0], pairs[2 * m], pairs[2 * m + 1][...], put)


def hidden_grad_kernel(place_ref, cot_ref, pair_ref, peer_ref, w_ref, grad_ref):
    put_shards(place_ref, pair_ref, peer_ref, w_ref)
    step = min(512, cot_ref.shape[0])
    for start in range(0, cot_ref.shape[0], step):
        grad_ref[start : start + step, :] = dot(cot_ref[start : start + step, :], w_ref[...])


def hidden_kernel(
    n_pieces, member_ref, offset_ref, place_ref, pair_ref, peer_ref, bias_ref, grad_ref, *rest
):
    pieces = rest[:n_pieces]
    x_ref, value_ref, slope_ref, sum_ref, far_ref, unit_ref, w_ref = rest[n_pieces:]
    count, rows, _ = sum_ref.shape
    middle = rows // 2
    put_shards(place_ref, pair_ref, peer_ref, w_ref)

    def put(member, half, values):
        at = pl.multiple_of(member * rows + half * middle, middle)
        x_ref[pl.ds(at, middle), :] = values

    put_tokens(member_ref, pieces, put, rows, count)
    unit_ref[...] = jnp.zeros_like(unit_ref)
    step = min(512, count * rows)
    for start in range(0, count * rows, step):
        part = slice(start, start + step)
        value, slope = gelu_parts(dot(x_ref[part, :], w_ref[...]) + bias_ref[...])
        value_ref[part, :] = value.astype(LOW)
        low = (grad_ref[part, :] * slope).astype(LOW)
        slope_ref[part, :] = low
        unit_ref[...] += jnp.sum(low.astype(FULL), axis=0, keepdims=True)
        total = dot_t(low, w_ref[...])
        for m in range(start // rows, (start + step) // rows):
            at = m * rows - start
            put_ring(offset_ref[m], count, sum_ref, far_ref, 0, total[at : at + rows, :])


def branch_kernel(value_ref, w_ref, out_ref):
    step = min(512, value_ref.shape[0])
    for start in range(0, value_ref.shape[0], step):
        part = slice(start, start + step)
        out_ref[part, :] = dot_t(value_ref[part, :], w_ref[...]).astype(LOW)


def body(
    block_input,
    out_cot,
    pair_of,
    ln1_gain,
    ln1_bias,
    qkv_weight,
    qv_bias,
    out_weight,
    out_bias,
    ln2_gain,
    ln2_bias,
    fc_weight,
    fc_bias,
    proj_weight,
    proj_bias,
):
    rows, width = block_input.shape[2], block_input.shape[3]
    count = lax.axis_size("ctx")
    tokens = count * rows
    fused = count <= 8
    seq, ctx = lax.axis_index("seq"), lax.axis_index("ctx")
    core, row = seq % 2, seq // 2
    order = np.array(ring_order(count), np.int32)
    rank = np.argsort(order)
    member = jnp.asarray(np.stack([np.roll(order, -i) for i in rank]).astype(np.int32))[ctx]
    offset = jnp.asarray(((rank[None, :] - rank[:, None]) % count).astype(np.int32))[ctx]
    place, core_at, row_at = seq[None], core[None], row[None]
    ranks = jnp.arange(count, dtype=jnp.int32)
    who = jnp.sum(jnp.where(pair_of[None, :] == ranks[:, None], ranks[None, :], 0), axis=1)
    who = jnp.concatenate([who, who[::-1]]).astype(jnp.int32)
    far_of = offset[who]
    input_low = block_input.reshape(rows, width)
    inputs = input_low.astype(FULL)
    cot_low = out_cot.reshape(rows, width)

    group, moves, sent, kept = head_plan(count, width)
    heads = group // HEAD
    pick_sent = picker(jnp.asarray(sent)[ctx], qkv_weight.shape[1])
    pick_kept = picker(jnp.asarray(kept)[ctx], sent.shape[1])
    scaled_one, rate_one = norm_parts(inputs)
    normed_one = (scaled_one * ln1_gain + ln1_bias).astype(LOW)
    units = fc_weight.shape[1]
    held = {}

    with jax.named_scope("to_heads"):
        sent_heads = dot(qkv_weight, pick_sent).astype(LOW)
    first = len(moves) // 2

    def ride_first(hold):
        with jax.named_scope("to_heads"):
            held["first"] = take_rounds(sent_heads, moves[:first])
        return held["first"]

    def ride_second(hold):
        with jax.named_scope("to_heads"):
            held["second"] = take_rounds(hold(sent_heads), moves[first:])
        return held["second"]

    def ride_row_parts(hold):
        held["out"] = lax.all_gather(jnp.transpose(hold(out_weight)), ("seq", "ctx"), axis=0)
        with jax.named_scope("qkv_parts"):
            pieces = jnp.concatenate(held["first"] + held["second"], axis=1)
            own = dot(hold(pieces), pick_kept).astype(LOW)
            held["pair"] = jnp.stack([own, swap(own, "seq", 2)])
        return ()

    with jax.named_scope("gather_one"):
        gathered = ring_gather(normed_one, [ride_first, ride_second, ride_row_parts])
    with jax.named_scope("qkv_parts"):
        qkv_pair = held["pair"]
        qkv_peer = swap(qkv_pair, "seq", 1)
    out_t = held["out"].reshape(4, count, out_weight.shape[1], out_weight.shape[0])
    bias_rows = jnp.pad(qv_bias, ((0, 0), (0, count * group - width)))
    bias_mine = lax.dynamic_slice_in_dim(bias_rows, ctx * group, group, 1)
    qkv_shift = jnp.concatenate([bias_mine[:1], jnp.zeros((1, group), FULL), bias_mine[1:]], axis=1)
    with jax.named_scope("unit_parts"):
        proj_own = after(jnp.transpose(proj_weight), qkv_peer)
        proj_pair = jnp.stack([proj_own, swap(proj_own, "seq", 2)])

    one_tokens, qkv_cols, qkv, attn_full, attn_part, lse = call(
        functools.partial(attend_kernel, len(gathered), heads),
        [
            ((tokens, width), LOW),
            ((width, 3 * group), LOW),
            ((tokens, 3 * group), LOW),
            ((tokens, group), FULL),
            ((count, rows, group), LOW),
            ((tokens, heads), FULL),
        ],
        [qkv_pair, qkv_peer, qkv_shift, *gathered],
        [member, place, pair_of, who],
        "attend",
        2 * tokens * width * 3 * group + 16 * tokens * tokens * group,
    )
    attn_part, proj_pair = lax.optimization_barrier((attn_part, proj_pair))
    with jax.named_scope("unit_parts"):
        fc_own = after(fc_weight, attn_part)
        fc_pair = jnp.stack([fc_own, swap(fc_own, "seq", 2)])
    cots = lax.all_gather(after(cot_low, qkv_peer), "ctx", axis=0, tiled=True)

    back = lax.all_to_all(attn_part, "ctx", 0, 0, tiled=True)
    back, proj_pair, fc_pair = lax.optimization_barrier((back, proj_pair, fc_pair))
    with jax.named_scope("unit_parts"):
        proj_peer = swap(proj_pair, "seq", 1)
        fc_peer = swap(fc_pair, "seq", 1)
    middle, normed_two, scaled_two, rate_two, attn_low = call(
        out_kernel,
        [
            ((rows, width), FULL),
            ((rows, width), LOW),
            ((rows, width), FULL),
            ((rows, 1), FULL),
            ((rows, width), LOW),
        ],
        [back, input_low, out_bias[None], ln2_gain[None], ln2_bias[None], out_t],
        [],
        "out",
        2 * rows * width * width,
        [pltpu.VMEM((rows, count * group), LOW)],
    )

    proj_cols, hidden_grad = call(
        hidden_grad_kernel,
        [((width, units), LOW), ((tokens, units), FULL)],
        [cots, proj_pair, proj_peer],
        [place],
        "hidden_grad",
        2 * tokens * width * units,
    )
    with jax.named_scope("gather_two"):
        two_gathered = ring_gather(normed_two)
    bias_units = lax.dynamic_slice_in_dim(fc_bias, ctx * units, units)[None]
    if fused:
        two_tokens, hidden, hidden_pre_grad, two_parts, two_far, units_grad = call(
            functools.partial(hidden_kernel, len(two_gathered)),
            [
                ((tokens, width), LOW),
                ((tokens, units), LOW),
                ((tokens, units), LOW),
                ((count, rows, width), FULL),
                ((rows, width), LOW),
                ((1, units), FULL),
            ],
            [fc_pair, fc_peer, bias_units, hidden_grad, *two_gathered],
            [member, offset, place],
            "hidden",
            4 * tokens * width * units,
            [pltpu.VMEM((width, units), LOW)],
        )
    else:
        far = count // 2
        pieces = two_gathered[:far] + [jnp.concatenate(two_gathered[far : far + 2])] + two_gathered[far + 2 :]
        two_tokens = pick(jnp.stack(pieces), offset, count).reshape(tokens, width)
        shards = jnp.stack([fc_pair[0], fc_peer[0], fc_pair[1], fc_peer[1]])
        fc_cols = pick(shards, seq ^ jnp.arange(4), 4).reshape(width, units)
        value, slope = gelu_parts(dot(two_tokens, fc_cols) + bias_units)
        hidden = value.astype(LOW)
        hidden_pre_grad = (hidden_grad * slope).astype(LOW)
        two_parts = pick(dot_t(hidden_pre_grad, fc_cols).reshape(count, rows, width), member, count)
        two_far = two_parts[far].astype(LOW)
        units_grad = jnp.sum(hidden_pre_grad.astype(FULL), axis=0)
    def ride_branch(hold):
        (held["branch"],) = call(
            branch_kernel, [((tokens, width), LOW)], [hidden, proj_cols], [], "branch", 2 * tokens * width * units
        )
        return (held["branch"],)

    def ride_other(hold):
        with jax.named_scope("unit_sum"):
            (other,) = call(
                other_kernel,
                [((2, 2, width // 4, units), LOW)],
                [two_tokens, hidden_pre_grad, cots, hidden],
                [hold(core_at)],
                "unit_other",
                0,
            )
            held["peer"] = swap(other, "seq", 1)
        return (other,)

    with jax.named_scope("sum_two"):
        normed_two_grad = ring_sum(two_parts, two_far, [ride_branch, ride_other])
    branch_two = lax.psum_scatter(held["branch"], "ctx", scatter_dimension=0, tiled=True)
    block_output = (middle + branch_two.astype(FULL) + proj_bias).astype(LOW).reshape(block_input.shape)

    size, quarter = out_t.shape[2], out_t.shape[3]
    middle_grad, branch_low, attn_grad, lines, whole_out, other = call(
        out_back_kernel,
        [
            ((rows, width), FULL),
            ((rows, width), LOW),
            ((count, rows, group), LOW),
            ((4, width), FULL),
            ((count, size, 2 * quarter), FULL),
            ((count, size, 2 * quarter), LOW),
        ],
        [normed_two_grad, cot_low, scaled_two, rate_two, ln2_gain[None], out_t, attn_low],
        [core_at],
        "out_back",
        2 * rows * width * width,
        [pltpu.VMEM((rows, count * group), LOW), pltpu.VMEM((4, rows, quarter), LOW)],
    )
    grad_part = lax.all_to_all(attn_grad, "ctx", 0, 0, tiled=True)
    with jax.named_scope("unit_sum"):
        keep_units, send_units = call(
            mine_kernel,
            [((2, width // 4, units), FULL), ((2, width // 4, units), LOW)],
            [held["peer"], two_tokens, hidden_pre_grad, cots, hidden],
            [after(core_at, branch_low), row_at],
            "unit_mine",
            0,
        )
    with jax.named_scope("out_sum"):
        got_core_out = swap(other, "seq", 1)
        grad_part, got_core_out, block_output, send_units = lax.optimization_barrier(
            (grad_part, got_core_out, block_output, send_units)
        )
        with jax.named_scope("unit_sum"):
            got_units = swap(send_units, "seq", 2)
        half_sum = (whole_out + got_core_out.astype(FULL)).astype(LOW)
        out_sum = lax.psum_scatter(half_sum, "ctx", scatter_dimension=0)

    far_pair = pair_of[member[count // 2]]
    qkv_grad, cols_sum, one_far = call(
        functools.partial(attend_back_kernel, heads),
        [((tokens, 3 * group), LOW), ((1, 3 * group), FULL), ((rows, width), LOW)],
        [qkv, qkv_cols, attn_full, lse, grad_part],
        [who, jnp.stack([far_pair, 2 * count - 1 - far_pair])],
        "attend_back",
        0,
        [pltpu.VMEM((tokens, group), FULL)] * 2 + [pltpu.VMEM((tokens, group), LOW)],
    )
    if fused:
        one_parts, one_lines = call(
            project_back_kernel,
            [((count, rows, width), FULL), ((2, width), FULL)],
            [qkv_grad, qkv_cols, one_tokens],
            [far_of],
            "project_back",
            0,
        )
    else:
        parts = dot_t(qkv_grad, qkv_cols)
        one_lines = jnp.stack([jnp.sum(parts * one_tokens.astype(FULL), axis=0), jnp.sum(parts, axis=0)])
        parts = parts.reshape(2 * count, rows // 2, width)
        pairs = pair_of[member]
        one_parts = jnp.concatenate([pick(parts, pairs, count), pick(parts, 2 * count - 1 - pairs, count)], axis=1)

    shift_one = one_lines[1]
    gain_one = (one_lines[0] - ln1_bias * shift_one) / ln1_gain
    qv_sums = jnp.concatenate([cols_sum[:, :group], cols_sum[:, 2 * group :]])
    qv_sums = lax.dynamic_update_slice(
        jnp.zeros((2, count * group), FULL), qv_sums, (0, ctx * group)
    )[:, :width]
    unit_sums = lax.dynamic_update_slice(
        jnp.zeros((count * units,), FULL), units_grad.reshape(-1), (ctx * units,)
    )
    flat = [gain_one, shift_one, qv_sums.reshape(-1), lines.reshape(-1), unit_sums]
    flat = jnp.concatenate(flat)

    def ride_core(hold):
        with jax.named_scope("qkv_sum"):
            (other,) = call(
                other_kernel,
                [((1, 2, width // 4, 3 * group), LOW)],
                [one_tokens, qkv_grad],
                [hold(core_at)],
                "qkv_other",
                0,
            )
            held["core"] = swap(other, "seq", 1)
        return (held["core"],)

    def ride_row(hold):
        with jax.named_scope("qkv_sum"):
            held["qkv"], send = call(
                mine_kernel,
                [((1, width // 4, 3 * group), FULL), ((1, width // 4, 3 * group), LOW)],
                [held["core"], one_tokens, qkv_grad],
                [hold(core_at), row_at],
                "qkv_mine",
                0,
            )
            held["row"] = swap(send, "seq", 2)
        with jax.named_scope("sum_vectors"):
            held["flat"] = sum_over(hold(flat), "seq")
        return (send, held["flat"])

    def ride_heads(hold):
        with jax.named_scope("from_heads"):
            whole = (held["qkv"] + hold(held["row"]).astype(FULL))[0]
            sent = dot_t(whole.astype(LOW), pick_kept).astype(LOW)
            held["sent"] = sent
        with jax.named_scope("sum_vectors"):
            held["flat"] = sum_over(hold(held["flat"]), "ctx")
            got = hold(got_units).astype(FULL)
            held["fc"] = keep_units[0] + got[0]
            held["proj"] = jnp.transpose(keep_units[1] + got[1])
        return (out_sum, held["fc"], held["proj"])

    with jax.named_scope("sum_one"):
        normed_one_grad = ring_sum(one_parts, one_far, [lambda hold: (), ride_core, ride_row, ride_heads])
    with jax.named_scope("out_sum"):
        keep, send = ordered(row, out_sum[:, :quarter], out_sum[:, quarter:])
        out_weight_grad = jnp.transpose(keep.astype(FULL) + swap(send, "seq", 2).astype(FULL))
    middle_part = norm_back(normed_one_grad, scaled_one, rate_one, ln1_gain)
    input_grad = (middle_grad + middle_part).astype(LOW).reshape(block_input.shape)
    with jax.named_scope("from_heads"):
        qkv_weight_grad = from_heads(held["sent"], moves, pick_sent)

    fc_weight_grad, proj_weight_grad = held["fc"], held["proj"]
    flat = held["flat"]
    vectors = flat[: 8 * width].reshape(8, width)
    return (
        block_output,
        input_grad,
        vectors[0],
        vectors[1],
        qkv_weight_grad,
        vectors[2:4],
        out_weight_grad,
        vectors[4],
        vectors[5],
        vectors[6],
        fc_weight_grad,
        flat[8 * width :],
        proj_weight_grad,
        vectors[7],
    )


def solution(mesh):
    rows = P("seq", "ctx", None, None)
    cols = P("seq", "ctx")
    flip = P("ctx", "seq")
    one = P()
    return jax.shard_map(
        body,
        mesh=mesh,
        in_specs=(rows, rows, one, one, one, cols, one, cols, one, one, one, cols, one, flip, one),
        out_specs=(rows, rows, one, one, cols, one, cols, one, one, one, cols, one, flip, one),
        check_vma=False,
    )
```

```python
import functools
import math
import random

import jax
import jax.numpy as jnp
import numpy as np
from jax import lax
from jax.experimental import pallas as pl
from jax.experimental.pallas import tpu as pltpu
from jax.sharding import PartitionSpec as P

HEAD = 64
EPSILON = 1e-05
NEGATIVE = -1e30
GELU_COEF = 0.7978845608028654
LOW = jnp.bfloat16
FULL = jnp.float32
VMEM_BYTES = 56 * 2**20


def norm_parts(values):
    center = values - jnp.mean(values, axis=-1, keepdims=True)
    rate = lax.rsqrt(jnp.mean(center * center, axis=-1, keepdims=True) + EPSILON)
    return center * rate, rate


def norm_back(grad, scaled, rate, gain):
    inner = grad * gain
    return rate * (
        inner
        - jnp.mean(inner, axis=-1, keepdims=True)
        - scaled * jnp.mean(inner * scaled, axis=-1, keepdims=True)
    )


def gelu_parts(values):
    square = values * values
    bent = jnp.tanh(GELU_COEF * values * (1.0 + 0.044715 * square))
    slope = 0.5 * (1.0 + bent) + 0.5 * values * (1.0 - bent * bent) * GELU_COEF * (
        1.0 + 3.0 * 0.044715 * square
    )
    return 0.5 * values * (1.0 + bent), slope


def dot(left, right):
    return jnp.dot(left, right, preferred_element_type=FULL)


def dot_t(left, right):
    return lax.dot_general(left, right, (((1,), (1,)), ((), ())), preferred_element_type=FULL)


def t_dot(left, right):
    return lax.dot_general(left, right, (((0,), (0,)), ((), ())), preferred_element_type=FULL)


def swap(values, axis, bit):
    count = lax.axis_size(axis)
    return lax.ppermute(values, axis, [(i, i ^ bit) for i in range(count)])


def pick(values, places, count):
    return jnp.stack([lax.dynamic_index_in_dim(values, places[i], keepdims=False) for i in range(count)])


def ordered(flag, own, got):
    return jnp.where(flag == 0, own, got), jnp.where(flag == 0, got, own)


def joined(flag, own, got, axis):
    return jnp.concatenate(ordered(flag, own, got), axis)


def after(value, *first):
    return lax.optimization_barrier((value, *first))[0]


def after_all(first, value, *more):
    return after(value, *first, *more)


def ring_order(count):
    return list(range(0, count, 2)) + list(range(count - 1, 0, -2))


def shift(values, offset):
    order = ring_order(lax.axis_size("ctx"))
    count = len(order)
    return lax.ppermute(
        values, "ctx", [(order[i], order[(i + offset) % count]) for i in range(count)]
    )


def ring_gather(values, riders=()):
    count = lax.axis_size("ctx")
    half, rows = count // 2, values.shape[0] // 2
    ahead = behind = values
    riders = list(riders)
    pieces = [values] + [None] * (count - 1)
    for k in range(1, half + 1):
        rode = riders.pop(0)(lambda x, *more: after(x, ahead, behind, *more)) if riders else ()
        if k == half:
            pieces[half] = (shift(ahead[:rows], 1), shift(behind[rows:], -1))
            break
        ahead, behind = shift(ahead, 1), shift(behind, -1)
        pieces[count - k], pieces[k] = ahead, behind
        if rode:
            ahead, behind, *_ = lax.optimization_barrier((ahead, behind, *rode))
    return pieces[:half] + list(pieces[half]) + pieces[half + 1 :]


def ring_sum(held, far, riders=()):
    count = lax.axis_size("ctx")
    half, rows = count // 2, far.shape[0] // 2
    riders = list(riders)
    up, down = far[:rows], far[rows:]
    state = (up, down)
    for k in range(half - 1, -1, -1):
        rode = riders.pop(0)(functools.partial(after_all, state)) if riders else ()
        low_up, low_down = up.astype(LOW), down.astype(LOW)
        up, down = shift(low_up, 1).astype(FULL), shift(low_down, -1).astype(FULL)
        if k == half - 1:
            near, back = held[k], held[count - k]
            zero = jnp.zeros_like(up)
            up = near.astype(FULL) + jnp.concatenate([up, zero])
            down = back.astype(FULL) + jnp.concatenate([zero, down])
        elif k:
            up, down = held[k].astype(FULL) + up, held[count - k].astype(FULL) + down
        state = (up, down)
        if rode:
            up, down, *_ = lax.optimization_barrier((up, down, *rode))
    return held[0].astype(FULL) + up + down


def sum_over(values, axis, *gate):
    bit = 1
    while bit < lax.axis_size(axis):
        values = values + swap(values, axis, bit)
        bit *= 2
        if gate and 2 * bit == lax.axis_size(axis):
            values = after(values, *gate)
    return values


def seq_parts(shard):
    other = swap(shard, "seq", 2)
    pair = jnp.stack([shard, other])
    return pair, swap(pair, "seq", 1)


def seq_columns(tokens, core):
    part = tokens.shape[1] // 4
    blocks = [tokens[:, i * part : (i + 1) * part] for i in range(4)]
    return ordered(
        core, jnp.concatenate([blocks[0], blocks[2]], 1), jnp.concatenate([blocks[1], blocks[3]], 1)
    )


def seq_halves(held, got, row):
    half = held.shape[-2] // 2
    held = held + got.astype(FULL)
    keep, send = ordered(row, held[..., :half, :], held[..., half:, :])
    return keep, send.astype(LOW)


def head_plan(count, width):
    heads = width // HEAD
    group = -(-heads // count) * HEAD
    shard = 3 * width // count
    small = min(group, 128)
    edges = []
    for to in range(count):
        for part in range(3):
            low = part * width + to * group
            high = min(part * width + (to + 1) * group, (part + 1) * width)
            for come in range(count):
                a, b = max(low, come * shard), min(high, (come + 1) * shard)
                if a < b:
                    edges.append((come, to, a - come * shard, part * group + a - low, b - a))
    draw = random.Random(0)
    best, least = None, None
    for _ in range(300):
        draw.shuffle(edges)
        rounds = []
        for edge in sorted(edges, key=lambda e: e[4] <= small):
            for known in rounds:
                if all(edge[0] != e[0] and edge[1] != e[1] for e in known):
                    known.append(edge)
                    break
            else:
                rounds.append([edge])
        cost = sum(200 + (small if all(e[4] <= small for e in r) else group) for r in rounds)
        if least is None or cost < least:
            best, least = [list(r) for r in rounds], cost
    pairs, starts, sizes, total = [], [], [], 0
    for known in best:
        pairs.append([(e[0], e[1]) for e in known])
        starts.append(total)
        sizes.append(small if all(e[4] <= small for e in known) else group)
        total += sizes[-1]
    sent = np.full((count, total), -1, np.int32)
    kept = np.full((count, 3 * group), -1, np.int32)
    for known, begin in zip(best, starts, strict=True):
        for come, to, start, place, size in known:
            sent[come, begin : begin + size] = np.arange(start, start + size)
            kept[to, place : place + size] = begin + np.arange(size)
    moves = list(zip(pairs, starts, sizes, strict=True))
    return group, moves, sent, kept


def picker(places, size):
    return (lax.broadcasted_iota(jnp.int32, (size, places.shape[0]), 0) == places[None, :]).astype(LOW)


def move(values, pairs):
    return values if all(a == b for a, b in pairs) else lax.ppermute(values, "ctx", pairs)


def take_rounds(sent, moves):
    return [move(sent[:, start : start + size], pairs) for pairs, start, size in moves]


COST_US = {
    "attend": 60,
    "out": 30,
    "hidden_grad": 9,
    "hidden": 80,
    "branch": 8,
    "out_back": 45,
    "unit_other": 8,
    "unit_mine": 10,
    "qkv_other": 5,
    "qkv_mine": 6,
    "attend_back": 80,
    "project_back": 6,
    "input_grad": 100,
}


def call(kernel, outs, args, scalars, name, flops, scratch=()):
    spec = [pl.BlockSpec(memory_space=pltpu.SMEM)] * len(scalars)
    spec += [pl.BlockSpec(memory_space=pltpu.VMEM)] * len(args)
    moved = sum(math.prod(a.shape) * a.dtype.itemsize for a in args)
    moved += sum(math.prod(o[0]) * jnp.dtype(o[1]).itemsize for o in outs)
    return pl.pallas_call(
        kernel,
        in_specs=spec,
        out_specs=[pl.BlockSpec(memory_space=pltpu.VMEM)] * len(outs),
        out_shape=[jax.ShapeDtypeStruct(s, d) for s, d in outs],
        scratch_shapes=list(scratch),
        compiler_params=pltpu.CompilerParams(vmem_limit_bytes=VMEM_BYTES),
        cost_estimate=pl.CostEstimate(flops=1000, bytes_accessed=int(COST_US[name] * 3e6), transcendentals=0),
        name=name,
    )(*scalars, *args)


def put_tokens(member_ref, pieces, put, rows, count):
    half, middle = count // 2, rows // 2
    at = 0
    for k in range(count):
        member = member_ref[k]
        if k == half:
            put(member, 0, pieces[at][...])
            put(member, 1, pieces[at + 1][...])
            at += 2
        else:
            put(member, 0, pieces[at][:middle, :])
            put(member, 1, pieces[at][middle:, :])
            at += 1


def put_shards(place_ref, pair_ref, peer_ref, out_ref):
    seq = place_ref[0]
    height = out_ref.shape[0] // 4
    for k in range(4):
        source = pair_ref if k % 2 == 0 else peer_ref
        start = pl.multiple_of((seq ^ k) * height, 16)
        out_ref[pl.ds(start, height), :] = source[k // 2]


def causal(step, start, keys):
    query = lax.broadcasted_iota(jnp.int32, (step, keys), 0) + start
    return lax.broadcasted_iota(jnp.int32, (step, keys), 1) <= query


def each_step(tokens, run):
    if tokens <= 1024:
        step = min(256, tokens)
        for start in range(0, tokens, step):
            run(start, slice(start, start + step), step, start + step)
    else:
        step = 128

        @pl.loop(0, tokens // step)
        def _(i):
            start = pl.multiple_of(i * step, step)
            run(start, pl.ds(start, step), step, tokens)


def attend_kernel(
    n_pieces, heads, member_ref, place_ref, pair_of_ref, who_ref, pair_ref, peer_ref, shift_ref, *rest
):
    pieces = rest[:n_pieces]
    x_ref, w_ref, qkv_ref, full_ref, low_ref, lse_ref = rest[n_pieces:]
    count, rows, group = low_ref.shape
    tokens, block = count * rows, rows // 2
    put_shards(place_ref, pair_ref, peer_ref, w_ref)

    def put(member, half, values):
        pair = pair_of_ref[member]
        at = (2 * count - 1 - pair if half else pair) * block
        x_ref[pl.ds(pl.multiple_of(at, block), block), :] = values

    put_tokens(member_ref, pieces, put, rows, count)

    def project(start, part, step, keys):
        qkv_ref[part, :] = (dot(x_ref[part, :], w_ref[...]) + shift_ref[...]).astype(LOW)

    def some(start, part, step, keys):
        allowed = causal(step, start, keys)
        for h in range(heads):
            a, b = h * HEAD, (h + 1) * HEAD
            query = (qkv_ref[part, a:b] * (1.0 / math.sqrt(HEAD))).astype(LOW)
            score = jnp.where(allowed, dot_t(query, qkv_ref[:keys, group + a : group + b]), NEGATIVE)
            top = jnp.max(score, axis=1, keepdims=True)
            weight = jnp.exp(score - top)
            total = jnp.sum(weight, axis=1, keepdims=True)
            result = dot(weight.astype(LOW), qkv_ref[:keys, 2 * group + a : 2 * group + b]) / total
            full_ref[part, a:b] = result
            lse_ref[part, h : h + 1] = top + jnp.log(total)

    each_step(tokens, project)
    each_step(tokens, some)
    for j in range(2 * count):
        half = j // count * block
        low_ref[who_ref[j], half : half + block, :] = full_ref[j * block : (j + 1) * block, :].astype(LOW)


def attend_back_kernel(
    heads,
    who_ref,
    far_ref,
    qkv_ref,
    w_ref,
    full_ref,
    lse_ref,
    come_ref,
    out_ref,
    sum_ref,
    low_ref,
    dk_ref,
    dv_ref,
    grad_ref,
):
    count, rows, group = come_ref.shape
    tokens, block = count * rows, rows // 2
    scale = 1.0 / math.sqrt(HEAD)
    dk_ref[...] = jnp.zeros_like(dk_ref)
    dv_ref[...] = jnp.zeros_like(dv_ref)
    for j in range(2 * count):
        half = j // count * block
        grad_ref[j * block : (j + 1) * block, :] = come_ref[who_ref[j], half : half + block, :]

    def some(start, part, step, keys):
        allowed = causal(step, start, keys)
        for h in range(heads):
            a, b = h * HEAD, (h + 1) * HEAD
            query = (qkv_ref[part, a:b] * scale).astype(LOW)
            key = qkv_ref[:keys, group + a : group + b]
            value = qkv_ref[:keys, 2 * group + a : 2 * group + b]
            grad = grad_ref[part, a:b]
            delta = jnp.sum(grad.astype(FULL) * full_ref[part, a:b], axis=1, keepdims=True)
            score = dot_t(query, key)
            prob = jnp.where(allowed, jnp.exp(score - lse_ref[part, h : h + 1]), 0.0)
            score_grad = (prob * (dot_t(grad, value) - delta)).astype(LOW)
            out_ref[part, a:b] = (dot(score_grad, key) * scale).astype(LOW)
            dk_ref[:keys, a:b] += t_dot(score_grad, query)
            dv_ref[:keys, a:b] += t_dot(prob.astype(LOW), grad)

    each_step(tokens, some)
    out_ref[:, group : 2 * group] = dk_ref[...].astype(LOW)
    out_ref[:, 2 * group :] = dv_ref[...].astype(LOW)
    sum_ref[...] = jnp.sum(out_ref[...].astype(FULL), axis=0, keepdims=True)
    for half in range(2):
        start = pl.multiple_of(far_ref[half] * block, block)
        low_ref[half * block : (half + 1) * block, :] = dot_t(out_ref[pl.ds(start, block), :], w_ref[...]).astype(LOW)


def project_back_kernel(far_ref, grad_ref, w_ref, x_ref, norm_ref, gain_ref):
    count, rows, width = norm_ref.shape
    tokens, block = count * rows, rows // 2
    gain_ref[...] = jnp.zeros_like(gain_ref)
    step = min(256, tokens)
    for start in range(0, tokens, step):
        part = slice(start, start + step)
        total = dot_t(grad_ref[part, :], w_ref[...])
        gain_ref[0:1, :] += jnp.sum(total * x_ref[part, :].astype(FULL), axis=0, keepdims=True)
        gain_ref[1:2, :] += jnp.sum(total, axis=0, keepdims=True)
        for j in range(start // block, (start + step) // block):
            half, at = j // count * block, j * block - start
            norm_ref[far_ref[j], half : half + block, :] = total[at : at + block, :].astype(LOW)


def input_grad_kernel(sum_ref, mid_ref, scaled_ref, rate_ref, gain_ref, out_ref):
    part = norm_back(sum_ref[...], scaled_ref[...], rate_ref[...], gain_ref[...])
    out_ref[...] = (mid_ref[...] + part).astype(LOW)


def put_ring(offset, count, full_ref, low_ref, start, values):
    end = start + values.shape[0]

    @pl.when(offset == count // 2)
    def _():
        low_ref[start:end, :] = values.astype(LOW)

    @pl.when(offset != count // 2)
    def _():
        full_ref[offset, start:end, :] = values.astype(LOW)


def out_kernel(back_ref, input_ref, bias_ref, gain_ref, shift_ref, w_ref, mid_ref, low_ref, scaled_ref, rate_ref, attn_ref, wide_ref):
    count, rows, group = back_ref.shape
    width = mid_ref.shape[1]
    for d in range(count):
        wide_ref[:, d * group : (d + 1) * group] = back_ref[d]
    attn_ref[...] = wide_ref[:, :width]
    quarter, size = w_ref.shape[3], w_ref.shape[2]
    mid_ref[...] = input_ref[...].astype(FULL) + bias_ref[...]
    parts = [attn_ref[:, s * quarter : (s + 1) * quarter] for s in range(4)]
    for d in range(count):
        total = dot_t(parts[0], w_ref[0, d])
        for s in range(1, 4):
            total = total + dot_t(parts[s], w_ref[s, d])
        mid_ref[:, d * size : (d + 1) * size] += total
    scaled, rate = norm_parts(mid_ref[...])
    scaled_ref[...] = scaled
    rate_ref[...] = rate
    low_ref[...] = (scaled * gain_ref[...] + shift_ref[...]).astype(LOW)


def out_back_kernel(
    core_ref,
    sum_ref,
    cot_ref,
    scaled_ref,
    rate_ref,
    gain_ref,
    w_ref,
    attn_ref,
    mid_ref,
    low_ref,
    grad_ref,
    line_ref,
    mine_ref,
    other_ref,
    wide_ref,
    part_ref,
):
    count, rows, group = grad_ref.shape
    width = mid_ref.shape[1]
    cot = cot_ref[...].astype(FULL)
    total, scaled = sum_ref[...], scaled_ref[...]
    mid_ref[...] = cot + norm_back(total, scaled, rate_ref[...], gain_ref[...])
    low_ref[...] = mid_ref[...].astype(LOW)
    line_ref[0:1, :] = jnp.sum(low_ref[...].astype(FULL), axis=0, keepdims=True)
    line_ref[1:2, :] = jnp.sum(total * scaled, axis=0, keepdims=True)
    line_ref[2:3, :] = jnp.sum(total, axis=0, keepdims=True)
    line_ref[3:4, :] = jnp.sum(cot, axis=0, keepdims=True)
    quarter, size = w_ref.shape[3], w_ref.shape[2]
    wide_ref[:, width:] = jnp.zeros((rows, count * group - width), LOW)
    parts = [low_ref[:, d * size : (d + 1) * size] for d in range(count)]
    for s in range(4):
        part_ref[s] = attn_ref[:, s * quarter : (s + 1) * quarter]
        total = dot(parts[0], w_ref[s, 0])
        for d in range(1, count):
            total = total + dot(parts[d], w_ref[s, d])
        wide_ref[:, s * quarter : (s + 1) * quarter] = total.astype(LOW)
    core = core_ref[0]
    for d in range(count):
        grad_ref[d] = wide_ref[:, d * group : (d + 1) * group]
        for y in range(2):
            lanes = slice(y * quarter, (y + 1) * quarter)
            mine_ref[d, :, lanes] = t_dot(parts[d], part_ref[2 * y + core])
            other_ref[d, :, lanes] = t_dot(parts[d], part_ref[2 * y + 1 - core]).astype(LOW)


def seq_dots(core, left_ref, right, put):
    part = left_ref.shape[1] // 4
    for some in range(2):

        @pl.when(core == some)
        def _(some=some):
            for y in range(2):
                at = (2 * y + some) * part
                put(y, t_dot(left_ref[:, at : at + part], right))


def other_kernel(core_ref, *rest):
    *pairs, out_ref = rest

    for m in range(len(pairs) // 2):

        def put(y, total, m=m):
            out_ref[m, y] = total.astype(LOW)

        seq_dots(1 - core_ref[0], pairs[2 * m], pairs[2 * m + 1][...], put)


def mine_kernel(core_ref, row_ref, got_ref, *rest):
    *pairs, keep_ref, send_ref = rest

    for m in range(len(pairs) // 2):

        def put(y, total, m=m):
            total = total + got_ref[m, y].astype(FULL)

            @pl.when(row_ref[0] == y)
            def _():
                keep_ref[m] = total

            @pl.when(row_ref[0] != y)
            def _():
                send_ref[m] = total.astype(LOW)

        seq_dots(core_ref[0], pairs[2 * m], pairs[2 * m + 1][...], put)


def hidden_grad_kernel(place_ref, cot_ref, pair_ref, peer_ref, w_ref, grad_ref):
    put_shards(place_ref, pair_ref, peer_ref, w_ref)
    step = min(512, cot_ref.shape[0])
    for start in range(0, cot_ref.shape[0], step):
        grad_ref[start : start + step, :] = dot(cot_ref[start : start + step, :], w_ref[...])


def hidden_kernel(
    n_pieces, member_ref, offset_ref, place_ref, pair_ref, peer_ref, bias_ref, grad_ref, *rest
):
    pieces = rest[:n_pieces]
    x_ref, value_ref, slope_ref, sum_ref, far_ref, unit_ref, w_ref = rest[n_pieces:]
    count, rows, _ = sum_ref.shape
    middle = rows // 2
    put_shards(place_ref, pair_ref, peer_ref, w_ref)

    def put(member, half, values):
        at = pl.multiple_of(member * rows + half * middle, middle)
        x_ref[pl.ds(at, middle), :] = values

    put_tokens(member_ref, pieces, put, rows, count)
    unit_ref[...] = jnp.zeros_like(unit_ref)
    step = min(512, count * rows)
    for start in range(0, count * rows, step):
        part = slice(start, start + step)
        value, slope = gelu_parts(dot(x_ref[part, :], w_ref[...]) + bias_ref[...])
        value_ref[part, :] = value.astype(LOW)
        low = (grad_ref[part, :] * slope).astype(LOW)
        slope_ref[part, :] = low
        unit_ref[...] += jnp.sum(low.astype(FULL), axis=0, keepdims=True)
        total = dot_t(low, w_ref[...])
        for m in range(start // rows, (start + step) // rows):
            at = m * rows - start
            put_ring(offset_ref[m], count, sum_ref, far_ref, 0, total[at : at + rows, :])


def branch_kernel(value_ref, w_ref, out_ref):
    step = min(512, value_ref.shape[0])
    for start in range(0, value_ref.shape[0], step):
        part = slice(start, start + step)
        out_ref[part, :] = dot_t(value_ref[part, :], w_ref[...]).astype(LOW)


def body(
    block_input,
    out_cot,
    pair_of,
    ln1_gain,
    ln1_bias,
    qkv_weight,
    qv_bias,
    out_weight,
    out_bias,
    ln2_gain,
    ln2_bias,
    fc_weight,
    fc_bias,
    proj_weight,
    proj_bias,
):
    rows, width = block_input.shape[2], block_input.shape[3]
    count = lax.axis_size("ctx")
    tokens = count * rows
    fused = count <= 8
    seq, ctx = lax.axis_index("seq"), lax.axis_index("ctx")
    core, row = seq % 2, seq // 2
    order = np.array(ring_order(count), np.int32)
    rank = np.argsort(order)
    member = jnp.asarray(np.stack([np.roll(order, -i) for i in rank]).astype(np.int32))[ctx]
    offset = jnp.asarray(((rank[None, :] - rank[:, None]) % count).astype(np.int32))[ctx]
    place, core_at, row_at = seq[None], core[None], row[None]
    ranks = jnp.arange(count, dtype=jnp.int32)
    who = jnp.sum(jnp.where(pair_of[None, :] == ranks[:, None], ranks[None, :], 0), axis=1)
    who = jnp.concatenate([who, who[::-1]]).astype(jnp.int32)
    far_of = offset[who]
    input_low = block_input.reshape(rows, width)
    inputs = input_low.astype(FULL)
    cot_low = out_cot.reshape(rows, width)

    group, moves, sent, kept = head_plan(count, width)
    heads = group // HEAD
    pick_sent = picker(jnp.asarray(sent)[ctx], qkv_weight.shape[1])
    pick_kept = picker(jnp.asarray(kept)[ctx], sent.shape[1])
    scaled_one, rate_one = norm_parts(inputs)
    normed_one = (scaled_one * ln1_gain + ln1_bias).astype(LOW)
    units = fc_weight.shape[1]
    held = {}

    with jax.named_scope("to_heads"):
        sent_heads = dot(qkv_weight, pick_sent).astype(LOW)
    first = len(moves) // 2

    def ride_first(hold):
        with jax.named_scope("to_heads"):
            held["first"] = take_rounds(sent_heads, moves[:first])
        return held["first"]

    def ride_second(hold):
        with jax.named_scope("to_heads"):
            held["second"] = take_rounds(hold(sent_heads), moves[first:])
        held["out"] = lax.all_gather(jnp.transpose(hold(out_weight)), ("seq", "ctx"), axis=0)
        return held["second"]

    def ride_row_parts(hold):
        with jax.named_scope("qkv_parts"):
            pieces = jnp.concatenate(held["first"] + held["second"], axis=1)
            own = dot(hold(pieces), pick_kept).astype(LOW)
            held["own"], held["row"] = own, swap(own, "seq", 2)
        return ()

    def ride_core_parts(hold):
        with jax.named_scope("qkv_parts"):
            held["pair"] = jnp.stack([held["own"], hold(held["row"])])
            held["peer"] = swap(held["pair"], "seq", 1)
        return ()

    with jax.named_scope("gather_one"):
        gathered = ring_gather(normed_one, [ride_first, ride_second, ride_row_parts, ride_core_parts])
    qkv_pair, qkv_peer = held["pair"], held["peer"]
    out_t = held["out"].reshape(4, count, out_weight.shape[1], out_weight.shape[0])
    bias_rows = jnp.pad(qv_bias, ((0, 0), (0, count * group - width)))
    bias_mine = lax.dynamic_slice_in_dim(bias_rows, ctx * group, group, 1)
    qkv_shift = jnp.concatenate([bias_mine[:1], jnp.zeros((1, group), FULL), bias_mine[1:]], axis=1)
    with jax.named_scope("unit_parts"):
        proj_own = after(jnp.transpose(proj_weight), qkv_peer)
        proj_pair = jnp.stack([proj_own, swap(proj_own, "seq", 2)])

    one_tokens, qkv_cols, qkv, attn_full, attn_part, lse = call(
        functools.partial(attend_kernel, len(gathered), heads),
        [
            ((tokens, width), LOW),
            ((width, 3 * group), LOW),
            ((tokens, 3 * group), LOW),
            ((tokens, group), FULL),
            ((count, rows, group), LOW),
            ((tokens, heads), FULL),
        ],
        [qkv_pair, qkv_peer, qkv_shift, *gathered],
        [member, place, pair_of, who],
        "attend",
        2 * tokens * width * 3 * group + 16 * tokens * tokens * group,
    )
    attn_part, proj_pair = lax.optimization_barrier((attn_part, proj_pair))
    with jax.named_scope("unit_parts"):
        fc_own = after(fc_weight, attn_part)
        fc_pair = jnp.stack([fc_own, swap(fc_own, "seq", 2)])
    cots = lax.all_gather(after(cot_low, qkv_peer), "ctx", axis=0, tiled=True)

    back = lax.all_to_all(attn_part, "ctx", 0, 0, tiled=True)
    back, proj_pair, fc_pair = lax.optimization_barrier((back, proj_pair, fc_pair))
    with jax.named_scope("unit_parts"):
        proj_peer = swap(proj_pair, "seq", 1)
        fc_peer = swap(fc_pair, "seq", 1)
    middle, normed_two, scaled_two, rate_two, attn_low = call(
        out_kernel,
        [
            ((rows, width), FULL),
            ((rows, width), LOW),
            ((rows, width), FULL),
            ((rows, 1), FULL),
            ((rows, width), LOW),
        ],
        [back, input_low, out_bias[None], ln2_gain[None], ln2_bias[None], out_t],
        [],
        "out",
        2 * rows * width * width,
        [pltpu.VMEM((rows, count * group), LOW)],
    )

    proj_cols, hidden_grad = call(
        hidden_grad_kernel,
        [((width, units), LOW), ((tokens, units), FULL)],
        [cots, proj_pair, proj_peer],
        [place],
        "hidden_grad",
        2 * tokens * width * units,
    )
    with jax.named_scope("gather_two"):
        two_gathered = ring_gather(normed_two)
    bias_units = lax.dynamic_slice_in_dim(fc_bias, ctx * units, units)[None]
    if fused:
        two_tokens, hidden, hidden_pre_grad, two_parts, two_far, units_grad = call(
            functools.partial(hidden_kernel, len(two_gathered)),
            [
                ((tokens, width), LOW),
                ((tokens, units), LOW),
                ((tokens, units), LOW),
                ((count, rows, width), LOW),
                ((rows, width), LOW),
                ((1, units), FULL),
            ],
            [fc_pair, fc_peer, bias_units, hidden_grad, *two_gathered],
            [member, offset, place],
            "hidden",
            4 * tokens * width * units,
            [pltpu.VMEM((width, units), LOW)],
        )
    else:
        far = count // 2
        pieces = two_gathered[:far] + [jnp.concatenate(two_gathered[far : far + 2])] + two_gathered[far + 2 :]
        two_tokens = pick(jnp.stack(pieces), offset, count).reshape(tokens, width)
        shards = jnp.stack([fc_pair[0], fc_peer[0], fc_pair[1], fc_peer[1]])
        fc_cols = pick(shards, seq ^ jnp.arange(4), 4).reshape(width, units)
        value, slope = gelu_parts(dot(two_tokens, fc_cols) + bias_units)
        hidden = value.astype(LOW)
        hidden_pre_grad = (hidden_grad * slope).astype(LOW)
        two_parts = pick(dot_t(hidden_pre_grad, fc_cols).reshape(count, rows, width), member, count)
        two_far = two_parts[far].astype(LOW)
        units_grad = jnp.sum(hidden_pre_grad.astype(FULL), axis=0)
    def ride_branch(hold):
        (held["branch"],) = call(
            branch_kernel, [((tokens, width), LOW)], [hold(hidden), proj_cols], [], "branch", 2 * tokens * width * units
        )
        return (held["branch"],)

    def ride_other(hold):
        with jax.named_scope("unit_sum"):
            (other,) = call(
                other_kernel,
                [((2, 2, width // 4, units), LOW)],
                [two_tokens, hidden_pre_grad, cots, hidden],
                [hold(core_at)],
                "unit_other",
                0,
            )
            held["peer"] = swap(other, "seq", 1)
        return (other,)

    with jax.named_scope("sum_two"):
        normed_two_grad = ring_sum(two_parts, two_far, [lambda hold: (), ride_branch, ride_other])
    branch_two = lax.psum_scatter(held["branch"], "ctx", scatter_dimension=0, tiled=True)
    block_output = (middle + branch_two.astype(FULL) + proj_bias).astype(LOW).reshape(block_input.shape)

    size, quarter = out_t.shape[2], out_t.shape[3]
    middle_grad, branch_low, attn_grad, lines, whole_out, other = call(
        out_back_kernel,
        [
            ((rows, width), FULL),
            ((rows, width), LOW),
            ((count, rows, group), LOW),
            ((4, width), FULL),
            ((count, size, 2 * quarter), FULL),
            ((count, size, 2 * quarter), LOW),
        ],
        [normed_two_grad, cot_low, scaled_two, rate_two, ln2_gain[None], out_t, attn_low],
        [core_at],
        "out_back",
        2 * rows * width * width,
        [pltpu.VMEM((rows, count * group), LOW), pltpu.VMEM((4, rows, quarter), LOW)],
    )
    grad_part = lax.all_to_all(attn_grad, "ctx", 0, 0, tiled=True)
    with jax.named_scope("out_sum"):
        got_core_out = swap(other, "seq", 1)
        half_sum = (whole_out + got_core_out.astype(FULL)).astype(LOW)
        with jax.named_scope("unit_sum"):
            keep_units, send_units = call(
                mine_kernel,
                [((2, width // 4, units), FULL), ((2, width // 4, units), LOW)],
                [held["peer"], two_tokens, hidden_pre_grad, cots, hidden],
                [after(core_at, half_sum), row_at],
                "unit_mine",
                0,
            )
        grad_part, send_units = lax.optimization_barrier((grad_part, send_units))
        with jax.named_scope("unit_sum"):
            got_units = swap(send_units, "seq", 2)
        grad_part, half_sum = lax.optimization_barrier((grad_part, half_sum))
        out_sum = lax.psum_scatter(half_sum, "ctx", scatter_dimension=0)

    far_pair = pair_of[member[count // 2]]
    qkv_grad, cols_sum, one_far = call(
        functools.partial(attend_back_kernel, heads),
        [((tokens, 3 * group), LOW), ((1, 3 * group), FULL), ((rows, width), LOW)],
        [qkv, qkv_cols, attn_full, lse, grad_part],
        [who, jnp.stack([far_pair, 2 * count - 1 - far_pair])],
        "attend_back",
        0,
        [pltpu.VMEM((tokens, group), FULL)] * 2 + [pltpu.VMEM((tokens, group), LOW)],
    )
    if fused:
        one_parts, one_lines = call(
            project_back_kernel,
            [((count, rows, width), LOW), ((2, width), FULL)],
            [qkv_grad, qkv_cols, one_tokens],
            [after(far_of, got_units)],
            "project_back",
            0,
        )
    else:
        parts = dot_t(qkv_grad, qkv_cols)
        one_lines = jnp.stack([jnp.sum(parts * one_tokens.astype(FULL), axis=0), jnp.sum(parts, axis=0)])
        parts = parts.reshape(2 * count, rows // 2, width)
        pairs = pair_of[member]
        one_parts = jnp.concatenate([pick(parts, pairs, count), pick(parts, 2 * count - 1 - pairs, count)], axis=1)

    shift_one = one_lines[1]
    gain_one = (one_lines[0] - ln1_bias * shift_one) / ln1_gain
    qv_sums = jnp.concatenate([cols_sum[:, :group], cols_sum[:, 2 * group :]])
    qv_sums = lax.dynamic_update_slice(
        jnp.zeros((2, count * group), FULL), qv_sums, (0, ctx * group)
    )[:, :width]
    unit_sums = lax.dynamic_update_slice(
        jnp.zeros((count * units,), FULL), units_grad.reshape(-1), (ctx * units,)
    )
    flat = [gain_one, shift_one, qv_sums.reshape(-1), lines.reshape(-1), unit_sums]
    flat = jnp.concatenate(flat)

    def ride_core(hold):
        with jax.named_scope("qkv_sum"):
            (other,) = call(
                other_kernel,
                [((1, 2, width // 4, 3 * group), LOW)],
                [one_tokens, qkv_grad],
                [core_at],
                "qkv_other",
                0,
            )
            held["core"] = swap(other, "seq", 1)
        return (held["core"],)

    def ride_row(hold):
        with jax.named_scope("qkv_sum"):
            held["qkv"], send = call(
                mine_kernel,
                [((1, width // 4, 3 * group), FULL), ((1, width // 4, 3 * group), LOW)],
                [held["core"], one_tokens, qkv_grad],
                [hold(core_at), row_at],
                "qkv_mine",
                0,
            )
            held["row"] = swap(send, "seq", 2)
        with jax.named_scope("sum_vectors"):
            held["flat"] = sum_over(hold(flat), "seq")
        return (send, block_output)

    def ride_out(hold):
        with jax.named_scope("out_sum"):
            keep, send = ordered(row, out_sum[:, :quarter], out_sum[:, quarter:])
            held["out_sum"] = keep.astype(FULL) + swap(send, "seq", 2).astype(FULL)
        return (held["out_sum"],)

    def ride_heads(hold):
        with jax.named_scope("from_heads"):
            whole = (held["qkv"] + hold(held["row"]).astype(FULL))[0]
            sent_back = dot_t(whole.astype(LOW), pick_kept).astype(LOW)
            held["sent"] = take_rounds(sent_back, backward)
        with jax.named_scope("sum_vectors"):
            held["flat"] = sum_over(hold(held["flat"]), "ctx")
        with jax.named_scope("unit_sum"):
            got = hold(got_units).astype(FULL)
            held["fc"] = keep_units[0] + got[0]
            held["proj"] = jnp.transpose(keep_units[1] + got[1])
        return ()

    backward = [([(b, a) for a, b in pairs], start, size) for pairs, start, size in moves]
    with jax.named_scope("sum_one"):
        normed_one_grad = ring_sum(one_parts, one_far, [ride_core, ride_row, ride_out, ride_heads])
    with jax.named_scope("out_sum"):
        out_weight_grad = jnp.transpose(held["out_sum"])
    (input_grad,) = call(
        input_grad_kernel,
        [((rows, width), LOW)],
        [normed_one_grad, middle_grad, scaled_one, rate_one, ln1_gain[None]],
        [],
        "input_grad",
        0,
    )
    input_grad = input_grad.reshape(block_input.shape)
    with jax.named_scope("from_heads"):
        qkv_weight_grad = dot_t(jnp.concatenate(held["sent"], axis=1), pick_sent)
    fc_weight_grad, proj_weight_grad = held["fc"], held["proj"]
    flat = held["flat"]
    vectors = flat[: 8 * width].reshape(8, width)
    return (
        block_output,
        input_grad,
        vectors[0],
        vectors[1],
        qkv_weight_grad,
        vectors[2:4],
        out_weight_grad,
        vectors[4],
        vectors[5],
        vectors[6],
        fc_weight_grad,
        flat[8 * width :],
        proj_weight_grad,
        vectors[7],
    )


def solution(mesh):
    rows = P("seq", "ctx", None, None)
    cols = P("seq", "ctx")
    flip = P("ctx", "seq")
    one = P()
    return jax.shard_map(
        body,
        mesh=mesh,
        in_specs=(rows, rows, one, one, one, cols, one, cols, one, one, one, cols, one, flip, one),
        out_specs=(rows, rows, one, one, cols, one, cols, one, one, one, cols, one, flip, one),
        check_vma=False,
    )
```

```python
import functools
import math
import random

import jax
import jax.numpy as jnp
import numpy as np
from jax import lax
from jax.experimental import pallas as pl
from jax.experimental.pallas import tpu as pltpu
from jax.sharding import PartitionSpec as P

HEAD = 64
EPSILON = 1e-05
NEGATIVE = -1e30
GELU_COEF = 0.7978845608028654
LOW = jnp.bfloat16
FULL = jnp.float32
VMEM_BYTES = 56 * 2**20


def norm_parts(values):
    center = values - jnp.mean(values, axis=-1, keepdims=True)
    rate = lax.rsqrt(jnp.mean(center * center, axis=-1, keepdims=True) + EPSILON)
    return center * rate, rate


def norm_back(grad, scaled, rate, gain):
    inner = grad * gain
    return rate * (
        inner
        - jnp.mean(inner, axis=-1, keepdims=True)
        - scaled * jnp.mean(inner * scaled, axis=-1, keepdims=True)
    )


def gelu_parts(values):
    square = values * values
    bent = jnp.tanh(GELU_COEF * values * (1.0 + 0.044715 * square))
    slope = 0.5 * (1.0 + bent) + 0.5 * values * (1.0 - bent * bent) * GELU_COEF * (
        1.0 + 3.0 * 0.044715 * square
    )
    return 0.5 * values * (1.0 + bent), slope


def dot(left, right):
    return jnp.dot(left, right, preferred_element_type=FULL)


def dot_t(left, right):
    return lax.dot_general(left, right, (((1,), (1,)), ((), ())), preferred_element_type=FULL)


def t_dot(left, right):
    return lax.dot_general(left, right, (((0,), (0,)), ((), ())), preferred_element_type=FULL)


def swap(values, axis, bit):
    count = lax.axis_size(axis)
    return lax.ppermute(values, axis, [(i, i ^ bit) for i in range(count)])


def pick(values, places, count):
    return jnp.stack([lax.dynamic_index_in_dim(values, places[i], keepdims=False) for i in range(count)])


def ordered(flag, own, got):
    return jnp.where(flag == 0, own, got), jnp.where(flag == 0, got, own)


def joined(flag, own, got, axis):
    return jnp.concatenate(ordered(flag, own, got), axis)


def after(value, *first):
    return lax.optimization_barrier((value, *first))[0]


def after_all(first, value, *more):
    return after(value, *first, *more)


def ring_order(count):
    return list(range(0, count, 2)) + list(range(count - 1, 0, -2))


def shift(values, offset):
    order = ring_order(lax.axis_size("ctx"))
    count = len(order)
    return lax.ppermute(
        values, "ctx", [(order[i], order[(i + offset) % count]) for i in range(count)]
    )


def ring_gather(values, riders=()):
    count = lax.axis_size("ctx")
    half, rows = count // 2, values.shape[0] // 2
    ahead = behind = values
    riders = list(riders)
    pieces = [values] + [None] * (count - 1)
    for k in range(1, half + 1):
        rode = riders.pop(0)(lambda x, *more: after(x, ahead, behind, *more)) if riders else ()
        if k == half:
            pieces[half] = (shift(ahead[:rows], 1), shift(behind[rows:], -1))
            break
        ahead, behind = shift(ahead, 1), shift(behind, -1)
        pieces[count - k], pieces[k] = ahead, behind
        if rode:
            ahead, behind, *_ = lax.optimization_barrier((ahead, behind, *rode))
    return pieces[:half] + list(pieces[half]) + pieces[half + 1 :]


def ring_sum(held, far, riders=()):
    count = lax.axis_size("ctx")
    half, rows = count // 2, far.shape[0] // 2
    riders = list(riders)
    up, down = far[:rows], far[rows:]
    state = (up, down)
    for k in range(half - 1, -1, -1):
        rode = riders.pop(0)(functools.partial(after_all, state)) if riders else ()
        low_up, low_down = up.astype(LOW), down.astype(LOW)
        up, down = shift(low_up, 1).astype(FULL), shift(low_down, -1).astype(FULL)
        if k == half - 1:
            near, back = held[k], held[count - k]
            zero = jnp.zeros_like(up)
            up = near.astype(FULL) + jnp.concatenate([up, zero])
            down = back.astype(FULL) + jnp.concatenate([zero, down])
        elif k:
            up, down = held[k].astype(FULL) + up, held[count - k].astype(FULL) + down
        state = (up, down)
        if rode:
            up, down, *_ = lax.optimization_barrier((up, down, *rode))
    return held[0].astype(FULL) + up + down


def sum_over(values, axis, *gate):
    bit = 1
    while bit < lax.axis_size(axis):
        values = values + swap(values, axis, bit)
        bit *= 2
        if gate and 2 * bit == lax.axis_size(axis):
            values = after(values, *gate)
    return values


def seq_parts(shard):
    other = swap(shard, "seq", 2)
    pair = jnp.stack([shard, other])
    return pair, swap(pair, "seq", 1)


def seq_columns(tokens, core):
    part = tokens.shape[1] // 4
    blocks = [tokens[:, i * part : (i + 1) * part] for i in range(4)]
    return ordered(
        core, jnp.concatenate([blocks[0], blocks[2]], 1), jnp.concatenate([blocks[1], blocks[3]], 1)
    )


def seq_halves(held, got, row):
    half = held.shape[-2] // 2
    held = held + got.astype(FULL)
    keep, send = ordered(row, held[..., :half, :], held[..., half:, :])
    return keep, send.astype(LOW)


def head_plan(count, width):
    heads = width // HEAD
    group = -(-heads // count) * HEAD
    shard = 3 * width // count
    small = min(group, 128)
    edges = []
    for to in range(count):
        for part in range(3):
            low = part * width + to * group
            high = min(part * width + (to + 1) * group, (part + 1) * width)
            for come in range(count):
                a, b = max(low, come * shard), min(high, (come + 1) * shard)
                if a < b:
                    edges.append((come, to, a - come * shard, part * group + a - low, b - a))
    draw = random.Random(0)
    best, least = None, None
    for _ in range(300):
        draw.shuffle(edges)
        rounds = []
        for edge in sorted(edges, key=lambda e: e[4] <= small):
            for known in rounds:
                if all(edge[0] != e[0] and edge[1] != e[1] for e in known):
                    known.append(edge)
                    break
            else:
                rounds.append([edge])
        cost = sum(200 + (small if all(e[4] <= small for e in r) else group) for r in rounds)
        if least is None or cost < least:
            best, least = [list(r) for r in rounds], cost
    pairs, starts, sizes, total = [], [], [], 0
    for known in best:
        pairs.append([(e[0], e[1]) for e in known])
        starts.append(total)
        sizes.append(small if all(e[4] <= small for e in known) else group)
        total += sizes[-1]
    sent = np.full((count, total), -1, np.int32)
    kept = np.full((count, 3 * group), -1, np.int32)
    for known, begin in zip(best, starts, strict=True):
        for come, to, start, place, size in known:
            sent[come, begin : begin + size] = np.arange(start, start + size)
            kept[to, place : place + size] = begin + np.arange(size)
    moves = list(zip(pairs, starts, sizes, strict=True))
    return group, moves, sent, kept


def picker(places, size):
    return (lax.broadcasted_iota(jnp.int32, (size, places.shape[0]), 0) == places[None, :]).astype(LOW)


def move(values, pairs):
    return values if all(a == b for a, b in pairs) else lax.ppermute(values, "ctx", pairs)


def take_rounds(sent, moves):
    return [move(sent[:, start : start + size], pairs) for pairs, start, size in moves]


COST_US = {
    "attend": 60,
    "out": 30,
    "hidden_grad": 9,
    "hidden": 80,
    "branch": 8,
    "out_back": 45,
    "unit_other": 8,
    "unit_mine": 10,
    "qkv_other": 5,
    "qkv_mine": 6,
    "attend_back": 80,
    "project_back": 6,
    "input_grad": 100,
}


def call(kernel, outs, args, scalars, name, flops, scratch=()):
    spec = [pl.BlockSpec(memory_space=pltpu.SMEM)] * len(scalars)
    spec += [pl.BlockSpec(memory_space=pltpu.VMEM)] * len(args)
    moved = sum(math.prod(a.shape) * a.dtype.itemsize for a in args)
    moved += sum(math.prod(o[0]) * jnp.dtype(o[1]).itemsize for o in outs)
    return pl.pallas_call(
        kernel,
        in_specs=spec,
        out_specs=[pl.BlockSpec(memory_space=pltpu.VMEM)] * len(outs),
        out_shape=[jax.ShapeDtypeStruct(s, d) for s, d in outs],
        scratch_shapes=list(scratch),
        compiler_params=pltpu.CompilerParams(vmem_limit_bytes=VMEM_BYTES),
        cost_estimate=pl.CostEstimate(flops=1000, bytes_accessed=int(COST_US[name] * 3e6), transcendentals=0),
        name=name,
    )(*scalars, *args)


def put_tokens(member_ref, pieces, put, rows, count):
    half, middle = count // 2, rows // 2
    at = 0
    for k in range(count):
        member = member_ref[k]
        if k == half:
            put(member, 0, pieces[at][...])
            put(member, 1, pieces[at + 1][...])
            at += 2
        else:
            put(member, 0, pieces[at][:middle, :])
            put(member, 1, pieces[at][middle:, :])
            at += 1


def put_shards(place_ref, pair_ref, peer_ref, out_ref):
    seq = place_ref[0]
    height = out_ref.shape[0] // 4
    for k in range(4):
        source = pair_ref if k % 2 == 0 else peer_ref
        start = pl.multiple_of((seq ^ k) * height, 16)
        out_ref[pl.ds(start, height), :] = source[k // 2]


def causal(step, start, keys):
    query = lax.broadcasted_iota(jnp.int32, (step, keys), 0) + start
    return lax.broadcasted_iota(jnp.int32, (step, keys), 1) <= query


def each_step(tokens, run):
    if tokens <= 1024:
        step = min(256, tokens)
        for start in range(0, tokens, step):
            run(start, slice(start, start + step), step, start + step)
    else:
        step = 128

        @pl.loop(0, tokens // step)
        def _(i):
            start = pl.multiple_of(i * step, step)
            run(start, pl.ds(start, step), step, tokens)


def attend_kernel(
    n_pieces, heads, member_ref, place_ref, pair_of_ref, who_ref, pair_ref, peer_ref, shift_ref, *rest
):
    pieces = rest[:n_pieces]
    x_ref, w_ref, qkv_ref, full_ref, low_ref, lse_ref = rest[n_pieces:]
    count, rows, group = low_ref.shape
    tokens, block = count * rows, rows // 2
    put_shards(place_ref, pair_ref, peer_ref, w_ref)

    def put(member, half, values):
        pair = pair_of_ref[member]
        at = (2 * count - 1 - pair if half else pair) * block
        x_ref[pl.ds(pl.multiple_of(at, block), block), :] = values

    put_tokens(member_ref, pieces, put, rows, count)

    def project(start, part, step, keys):
        qkv_ref[part, :] = (dot(x_ref[part, :], w_ref[...]) + shift_ref[...]).astype(LOW)

    def some(start, part, step, keys):
        allowed = causal(step, start, keys)
        for h in range(heads):
            a, b = h * HEAD, (h + 1) * HEAD
            query = (qkv_ref[part, a:b] * (1.0 / math.sqrt(HEAD))).astype(LOW)
            score = jnp.where(allowed, dot_t(query, qkv_ref[:keys, group + a : group + b]), NEGATIVE)
            top = jnp.max(score, axis=1, keepdims=True)
            weight = jnp.exp(score - top)
            total = jnp.sum(weight, axis=1, keepdims=True)
            result = dot(weight.astype(LOW), qkv_ref[:keys, 2 * group + a : 2 * group + b]) / total
            full_ref[part, a:b] = result
            lse_ref[part, h : h + 1] = top + jnp.log(total)

    each_step(tokens, project)
    each_step(tokens, some)
    for j in range(2 * count):
        half = j // count * block
        low_ref[who_ref[j], half : half + block, :] = full_ref[j * block : (j + 1) * block, :].astype(LOW)


def attend_back_kernel(
    heads,
    who_ref,
    far_ref,
    qkv_ref,
    w_ref,
    full_ref,
    lse_ref,
    come_ref,
    out_ref,
    sum_ref,
    low_ref,
    dk_ref,
    dv_ref,
    grad_ref,
):
    count, rows, group = come_ref.shape
    tokens, block = count * rows, rows // 2
    scale = 1.0 / math.sqrt(HEAD)
    dk_ref[...] = jnp.zeros_like(dk_ref)
    dv_ref[...] = jnp.zeros_like(dv_ref)
    for j in range(2 * count):
        half = j // count * block
        grad_ref[j * block : (j + 1) * block, :] = come_ref[who_ref[j], half : half + block, :]

    def some(start, part, step, keys):
        allowed = causal(step, start, keys)
        for h in range(heads):
            a, b = h * HEAD, (h + 1) * HEAD
            query = (qkv_ref[part, a:b] * scale).astype(LOW)
            key = qkv_ref[:keys, group + a : group + b]
            value = qkv_ref[:keys, 2 * group + a : 2 * group + b]
            grad = grad_ref[part, a:b]
            delta = jnp.sum(grad.astype(FULL) * full_ref[part, a:b], axis=1, keepdims=True)
            score = dot_t(query, key)
            prob = jnp.where(allowed, jnp.exp(score - lse_ref[part, h : h + 1]), 0.0)
            score_grad = (prob * (dot_t(grad, value) - delta)).astype(LOW)
            out_ref[part, a:b] = (dot(score_grad, key) * scale).astype(LOW)
            dk_ref[:keys, a:b] += t_dot(score_grad, query)
            dv_ref[:keys, a:b] += t_dot(prob.astype(LOW), grad)

    each_step(tokens, some)
    out_ref[:, group : 2 * group] = dk_ref[...].astype(LOW)
    out_ref[:, 2 * group :] = dv_ref[...].astype(LOW)
    sum_ref[...] = jnp.sum(out_ref[...].astype(FULL), axis=0, keepdims=True)
    for half in range(2):
        start = pl.multiple_of(far_ref[half] * block, block)
        low_ref[half * block : (half + 1) * block, :] = dot_t(out_ref[pl.ds(start, block), :], w_ref[...]).astype(LOW)


def project_back_kernel(far_ref, grad_ref, w_ref, x_ref, norm_ref, gain_ref):
    count, rows, width = norm_ref.shape
    tokens, block = count * rows, rows // 2
    gain_ref[...] = jnp.zeros_like(gain_ref)
    step = min(256, tokens)
    for start in range(0, tokens, step):
        part = slice(start, start + step)
        total = dot_t(grad_ref[part, :], w_ref[...])
        gain_ref[0:1, :] += jnp.sum(total * x_ref[part, :].astype(FULL), axis=0, keepdims=True)
        gain_ref[1:2, :] += jnp.sum(total, axis=0, keepdims=True)
        for j in range(start // block, (start + step) // block):
            half, at = j // count * block, j * block - start
            norm_ref[far_ref[j], half : half + block, :] = total[at : at + block, :].astype(LOW)


def input_grad_kernel(sum_ref, mid_ref, scaled_ref, rate_ref, gain_ref, out_ref):
    part = norm_back(sum_ref[...], scaled_ref[...], rate_ref[...], gain_ref[...])
    out_ref[...] = (mid_ref[...] + part).astype(LOW)


def put_ring(offset, count, full_ref, low_ref, start, values):
    end = start + values.shape[0]

    @pl.when(offset == count // 2)
    def _():
        low_ref[start:end, :] = values.astype(LOW)

    @pl.when(offset != count // 2)
    def _():
        full_ref[offset, start:end, :] = values.astype(LOW)


def out_kernel(back_ref, input_ref, bias_ref, gain_ref, shift_ref, w_ref, mid_ref, low_ref, scaled_ref, rate_ref, attn_ref, wide_ref):
    count, rows, group = back_ref.shape
    width = mid_ref.shape[1]
    for d in range(count):
        wide_ref[:, d * group : (d + 1) * group] = back_ref[d]
    attn_ref[...] = wide_ref[:, :width]
    quarter, size = w_ref.shape[3], w_ref.shape[2]
    mid_ref[...] = input_ref[...].astype(FULL) + bias_ref[...]
    parts = [attn_ref[:, s * quarter : (s + 1) * quarter] for s in range(4)]
    for d in range(count):
        total = dot_t(parts[0], w_ref[0, d])
        for s in range(1, 4):
            total = total + dot_t(parts[s], w_ref[s, d])
        mid_ref[:, d * size : (d + 1) * size] += total
    scaled, rate = norm_parts(mid_ref[...])
    scaled_ref[...] = scaled
    rate_ref[...] = rate
    low_ref[...] = (scaled * gain_ref[...] + shift_ref[...]).astype(LOW)


def out_back_kernel(
    core_ref,
    sum_ref,
    cot_ref,
    scaled_ref,
    rate_ref,
    gain_ref,
    w_ref,
    attn_ref,
    mid_ref,
    low_ref,
    grad_ref,
    line_ref,
    mine_ref,
    other_ref,
    wide_ref,
    part_ref,
):
    count, rows, group = grad_ref.shape
    width = mid_ref.shape[1]
    cot = cot_ref[...].astype(FULL)
    total, scaled = sum_ref[...], scaled_ref[...]
    mid_ref[...] = cot + norm_back(total, scaled, rate_ref[...], gain_ref[...])
    low_ref[...] = mid_ref[...].astype(LOW)
    line_ref[0:1, :] = jnp.sum(low_ref[...].astype(FULL), axis=0, keepdims=True)
    line_ref[1:2, :] = jnp.sum(total * scaled, axis=0, keepdims=True)
    line_ref[2:3, :] = jnp.sum(total, axis=0, keepdims=True)
    line_ref[3:4, :] = jnp.sum(cot, axis=0, keepdims=True)
    quarter, size = w_ref.shape[3], w_ref.shape[2]
    wide_ref[:, width:] = jnp.zeros((rows, count * group - width), LOW)
    parts = [low_ref[:, d * size : (d + 1) * size] for d in range(count)]
    for s in range(4):
        part_ref[s] = attn_ref[:, s * quarter : (s + 1) * quarter]
        total = dot(parts[0], w_ref[s, 0])
        for d in range(1, count):
            total = total + dot(parts[d], w_ref[s, d])
        wide_ref[:, s * quarter : (s + 1) * quarter] = total.astype(LOW)
    core = core_ref[0]
    for d in range(count):
        grad_ref[d] = wide_ref[:, d * group : (d + 1) * group]
        for y in range(2):
            lanes = slice(y * quarter, (y + 1) * quarter)
            mine_ref[d, :, lanes] = t_dot(parts[d], part_ref[2 * y + core])
            other_ref[d, :, lanes] = t_dot(parts[d], part_ref[2 * y + 1 - core]).astype(LOW)


def seq_dots(core, left_ref, right, put):
    part = left_ref.shape[1] // 4
    for some in range(2):

        @pl.when(core == some)
        def _(some=some):
            for y in range(2):
                at = (2 * y + some) * part
                put(y, t_dot(left_ref[:, at : at + part], right))


def other_kernel(core_ref, *rest):
    *pairs, out_ref = rest

    for m in range(len(pairs) // 2):

        def put(y, total, m=m):
            out_ref[m, y] = total.astype(LOW)

        seq_dots(1 - core_ref[0], pairs[2 * m], pairs[2 * m + 1][...], put)


def mine_kernel(core_ref, row_ref, got_ref, *rest):
    *pairs, keep_ref, send_ref = rest

    for m in range(len(pairs) // 2):

        def put(y, total, m=m):
            total = total + got_ref[m, y].astype(FULL)

            @pl.when(row_ref[0] == y)
            def _():
                keep_ref[m] = total

            @pl.when(row_ref[0] != y)
            def _():
                send_ref[m] = total.astype(LOW)

        seq_dots(core_ref[0], pairs[2 * m], pairs[2 * m + 1][...], put)


def hidden_grad_kernel(place_ref, cot_ref, pair_ref, peer_ref, w_ref, grad_ref):
    put_shards(place_ref, pair_ref, peer_ref, w_ref)
    step = min(512, cot_ref.shape[0])
    for start in range(0, cot_ref.shape[0], step):
        grad_ref[start : start + step, :] = dot(cot_ref[start : start + step, :], w_ref[...])


def hidden_kernel(
    n_pieces, member_ref, offset_ref, place_ref, pair_ref, peer_ref, bias_ref, grad_ref, *rest
):
    pieces = rest[:n_pieces]
    x_ref, value_ref, slope_ref, sum_ref, far_ref, unit_ref, w_ref = rest[n_pieces:]
    count, rows, _ = sum_ref.shape
    middle = rows // 2
    put_shards(place_ref, pair_ref, peer_ref, w_ref)

    def put(member, half, values):
        at = pl.multiple_of(member * rows + half * middle, middle)
        x_ref[pl.ds(at, middle), :] = values

    put_tokens(member_ref, pieces, put, rows, count)
    unit_ref[...] = jnp.zeros_like(unit_ref)
    step = min(512, count * rows)
    for start in range(0, count * rows, step):
        part = slice(start, start + step)
        value, slope = gelu_parts(dot(x_ref[part, :], w_ref[...]) + bias_ref[...])
        value_ref[part, :] = value.astype(LOW)
        low = (grad_ref[part, :] * slope).astype(LOW)
        slope_ref[part, :] = low
        unit_ref[...] += jnp.sum(low.astype(FULL), axis=0, keepdims=True)
        total = dot_t(low, w_ref[...])
        for m in range(start // rows, (start + step) // rows):
            at = m * rows - start
            put_ring(offset_ref[m], count, sum_ref, far_ref, 0, total[at : at + rows, :])


def branch_kernel(value_ref, w_ref, out_ref):
    step = min(512, value_ref.shape[0])
    for start in range(0, value_ref.shape[0], step):
        part = slice(start, start + step)
        out_ref[part, :] = dot_t(value_ref[part, :], w_ref[...]).astype(LOW)


def body(
    block_input,
    out_cot,
    pair_of,
    ln1_gain,
    ln1_bias,
    qkv_weight,
    qv_bias,
    out_weight,
    out_bias,
    ln2_gain,
    ln2_bias,
    fc_weight,
    fc_bias,
    proj_weight,
    proj_bias,
):
    rows, width = block_input.shape[2], block_input.shape[3]
    count = lax.axis_size("ctx")
    tokens = count * rows
    fused = count <= 8
    seq, ctx = lax.axis_index("seq"), lax.axis_index("ctx")
    core, row = seq % 2, seq // 2
    order = np.array(ring_order(count), np.int32)
    rank = np.argsort(order)
    member = jnp.asarray(np.stack([np.roll(order, -i) for i in rank]).astype(np.int32))[ctx]
    offset = jnp.asarray(((rank[None, :] - rank[:, None]) % count).astype(np.int32))[ctx]
    place, core_at, row_at = seq[None], core[None], row[None]
    ranks = jnp.arange(count, dtype=jnp.int32)
    who = jnp.sum(jnp.where(pair_of[None, :] == ranks[:, None], ranks[None, :], 0), axis=1)
    who = jnp.concatenate([who, who[::-1]]).astype(jnp.int32)
    far_of = offset[who]
    input_low = block_input.reshape(rows, width)
    inputs = input_low.astype(FULL)
    cot_low = out_cot.reshape(rows, width)

    group, moves, sent, kept = head_plan(count, width)
    heads = group // HEAD
    pick_sent = picker(jnp.asarray(sent)[ctx], qkv_weight.shape[1])
    pick_kept = picker(jnp.asarray(kept)[ctx], sent.shape[1])
    scaled_one, rate_one = norm_parts(inputs)
    normed_one = (scaled_one * ln1_gain + ln1_bias).astype(LOW)
    units = fc_weight.shape[1]
    held = {}

    with jax.named_scope("to_heads"):
        sent_heads = dot(qkv_weight, pick_sent).astype(LOW)
    first = len(moves) // 2

    def ride_first(hold):
        with jax.named_scope("to_heads"):
            held["first"] = take_rounds(sent_heads, moves[:first])
        return held["first"]

    def ride_second(hold):
        with jax.named_scope("to_heads"):
            held["second"] = take_rounds(hold(sent_heads), moves[first:])
        held["out"] = lax.all_gather(jnp.transpose(hold(out_weight)), ("seq", "ctx"), axis=0)
        return held["second"]

    def ride_row_parts(hold):
        with jax.named_scope("qkv_parts"):
            pieces = jnp.concatenate(held["first"] + held["second"], axis=1)
            own = dot(hold(pieces), pick_kept).astype(LOW)
            held["own"], held["row"] = own, swap(own, "seq", 2)
        return ()

    def ride_core_parts(hold):
        with jax.named_scope("qkv_parts"):
            held["pair"] = jnp.stack([held["own"], hold(held["row"])])
            held["peer"] = swap(held["pair"], "seq", 1)
        return ()

    with jax.named_scope("gather_one"):
        gathered = ring_gather(normed_one, [ride_first, ride_second, ride_row_parts, ride_core_parts])
    qkv_pair, qkv_peer = held["pair"], held["peer"]
    out_t = held["out"].reshape(4, count, out_weight.shape[1], out_weight.shape[0])
    bias_rows = jnp.pad(qv_bias, ((0, 0), (0, count * group - width)))
    bias_mine = lax.dynamic_slice_in_dim(bias_rows, ctx * group, group, 1)
    qkv_shift = jnp.concatenate([bias_mine[:1], jnp.zeros((1, group), FULL), bias_mine[1:]], axis=1)
    with jax.named_scope("unit_parts"):
        proj_own = after(jnp.transpose(proj_weight), qkv_peer)
        proj_pair = jnp.stack([proj_own, swap(proj_own, "seq", 2)])

    one_tokens, qkv_cols, qkv, attn_full, attn_part, lse = call(
        functools.partial(attend_kernel, len(gathered), heads),
        [
            ((tokens, width), LOW),
            ((width, 3 * group), LOW),
            ((tokens, 3 * group), LOW),
            ((tokens, group), FULL),
            ((count, rows, group), LOW),
            ((tokens, heads), FULL),
        ],
        [qkv_pair, qkv_peer, qkv_shift, *gathered],
        [member, place, pair_of, who],
        "attend",
        2 * tokens * width * 3 * group + 16 * tokens * tokens * group,
    )
    attn_part, proj_pair = lax.optimization_barrier((attn_part, proj_pair))
    with jax.named_scope("unit_parts"):
        fc_own = after(fc_weight, attn_part)
        fc_pair = jnp.stack([fc_own, swap(fc_own, "seq", 2)])
    cots = lax.all_gather(after(cot_low, qkv_peer), "ctx", axis=0, tiled=True)

    back = lax.all_to_all(attn_part, "ctx", 0, 0, tiled=True)
    back, proj_pair, fc_pair = lax.optimization_barrier((back, proj_pair, fc_pair))
    with jax.named_scope("unit_parts"):
        proj_peer = swap(proj_pair, "seq", 1)
        fc_peer = swap(fc_pair, "seq", 1)
    middle, normed_two, scaled_two, rate_two, attn_low = call(
        out_kernel,
        [
            ((rows, width), FULL),
            ((rows, width), LOW),
            ((rows, width), FULL),
            ((rows, 1), FULL),
            ((rows, width), LOW),
        ],
        [back, input_low, out_bias[None], ln2_gain[None], ln2_bias[None], out_t],
        [],
        "out",
        2 * rows * width * width,
        [pltpu.VMEM((rows, count * group), LOW)],
    )

    proj_cols, hidden_grad = call(
        hidden_grad_kernel,
        [((width, units), LOW), ((tokens, units), FULL)],
        [cots, proj_pair, proj_peer],
        [place],
        "hidden_grad",
        2 * tokens * width * units,
    )
    with jax.named_scope("gather_two"):
        two_gathered = ring_gather(normed_two)
    bias_units = lax.dynamic_slice_in_dim(fc_bias, ctx * units, units)[None]
    if fused:
        two_tokens, hidden, hidden_pre_grad, two_parts, two_far, units_grad = call(
            functools.partial(hidden_kernel, len(two_gathered)),
            [
                ((tokens, width), LOW),
                ((tokens, units), LOW),
                ((tokens, units), LOW),
                ((count, rows, width), LOW),
                ((rows, width), LOW),
                ((1, units), FULL),
            ],
            [fc_pair, fc_peer, bias_units, hidden_grad, *two_gathered],
            [member, offset, place],
            "hidden",
            4 * tokens * width * units,
            [pltpu.VMEM((width, units), LOW)],
        )
    else:
        far = count // 2
        pieces = two_gathered[:far] + [jnp.concatenate(two_gathered[far : far + 2])] + two_gathered[far + 2 :]
        two_tokens = pick(jnp.stack(pieces), offset, count).reshape(tokens, width)
        shards = jnp.stack([fc_pair[0], fc_peer[0], fc_pair[1], fc_peer[1]])
        fc_cols = pick(shards, seq ^ jnp.arange(4), 4).reshape(width, units)
        value, slope = gelu_parts(dot(two_tokens, fc_cols) + bias_units)
        hidden = value.astype(LOW)
        hidden_pre_grad = (hidden_grad * slope).astype(LOW)
        two_parts = pick(dot_t(hidden_pre_grad, fc_cols).reshape(count, rows, width), member, count)
        two_far = two_parts[far].astype(LOW)
        units_grad = jnp.sum(hidden_pre_grad.astype(FULL), axis=0)
    def ride_branch(hold):
        (held["branch"],) = call(
            branch_kernel, [((tokens, width), LOW)], [hold(hidden), proj_cols], [], "branch", 2 * tokens * width * units
        )
        return (held["branch"],)

    def ride_other(hold):
        with jax.named_scope("unit_sum"):
            (other,) = call(
                other_kernel,
                [((2, 2, width // 4, units), LOW)],
                [two_tokens, hidden_pre_grad, cots, hidden],
                [hold(core_at)],
                "unit_other",
                0,
            )
            held["peer"] = swap(other, "seq", 1)
        return (other,)

    with jax.named_scope("sum_two"):
        normed_two_grad = ring_sum(two_parts, two_far, [lambda hold: (), ride_branch, ride_other])
    branch_two = lax.psum_scatter(held["branch"], "ctx", scatter_dimension=0, tiled=True)
    block_output = (middle + branch_two.astype(FULL) + proj_bias).astype(LOW).reshape(block_input.shape)

    size, quarter = out_t.shape[2], out_t.shape[3]
    middle_grad, branch_low, attn_grad, lines, whole_out, other = call(
        out_back_kernel,
        [
            ((rows, width), FULL),
            ((rows, width), LOW),
            ((count, rows, group), LOW),
            ((4, width), FULL),
            ((count, size, 2 * quarter), FULL),
            ((count, size, 2 * quarter), LOW),
        ],
        [normed_two_grad, cot_low, scaled_two, rate_two, ln2_gain[None], out_t, attn_low],
        [core_at],
        "out_back",
        2 * rows * width * width,
        [pltpu.VMEM((rows, count * group), LOW), pltpu.VMEM((4, rows, quarter), LOW)],
    )
    grad_part = lax.all_to_all(attn_grad, "ctx", 0, 0, tiled=True)
    with jax.named_scope("out_sum"):
        got_core_out = swap(other, "seq", 1)
        half_sum = (whole_out + got_core_out.astype(FULL)).astype(LOW)
        with jax.named_scope("unit_sum"):
            keep_units, send_units = call(
                mine_kernel,
                [((2, width // 4, units), FULL), ((2, width // 4, units), LOW)],
                [held["peer"], two_tokens, hidden_pre_grad, cots, hidden],
                [after(core_at, half_sum), row_at],
                "unit_mine",
                0,
            )
        grad_part, send_units = lax.optimization_barrier((grad_part, send_units))
        with jax.named_scope("unit_sum"):
            got_units = swap(send_units, "seq", 2)
        out_sum = lax.psum_scatter(half_sum, "ctx", scatter_dimension=0)

    far_pair = pair_of[member[count // 2]]
    qkv_grad, cols_sum, one_far = call(
        functools.partial(attend_back_kernel, heads),
        [((tokens, 3 * group), LOW), ((1, 3 * group), FULL), ((rows, width), LOW)],
        [qkv, qkv_cols, attn_full, lse, grad_part],
        [who, jnp.stack([far_pair, 2 * count - 1 - far_pair])],
        "attend_back",
        0,
        [pltpu.VMEM((tokens, group), FULL)] * 2 + [pltpu.VMEM((tokens, group), LOW)],
    )
    if fused:
        one_parts, one_lines = call(
            project_back_kernel,
            [((count, rows, width), LOW), ((2, width), FULL)],
            [qkv_grad, qkv_cols, one_tokens],
            [after(far_of, got_units)],
            "project_back",
            0,
        )
    else:
        parts = dot_t(qkv_grad, qkv_cols)
        one_lines = jnp.stack([jnp.sum(parts * one_tokens.astype(FULL), axis=0), jnp.sum(parts, axis=0)])
        parts = parts.reshape(2 * count, rows // 2, width)
        pairs = pair_of[member]
        one_parts = jnp.concatenate([pick(parts, pairs, count), pick(parts, 2 * count - 1 - pairs, count)], axis=1)

    shift_one = one_lines[1]
    gain_one = (one_lines[0] - ln1_bias * shift_one) / ln1_gain
    qv_sums = jnp.concatenate([cols_sum[:, :group], cols_sum[:, 2 * group :]])
    qv_sums = lax.dynamic_update_slice(
        jnp.zeros((2, count * group), FULL), qv_sums, (0, ctx * group)
    )[:, :width]
    unit_sums = lax.dynamic_update_slice(
        jnp.zeros((count * units,), FULL), units_grad.reshape(-1), (ctx * units,)
    )
    flat = [gain_one, shift_one, qv_sums.reshape(-1), lines.reshape(-1), unit_sums]
    flat = jnp.concatenate(flat)

    def ride_core(hold):
        with jax.named_scope("qkv_sum"):
            (other,) = call(
                other_kernel,
                [((1, 2, width // 4, 3 * group), LOW)],
                [one_tokens, qkv_grad],
                [core_at],
                "qkv_other",
                0,
            )
            held["core"] = swap(other, "seq", 1)
        return (held["core"],)

    def ride_row(hold):
        with jax.named_scope("sum_vectors"):
            held["flat"] = sum_over(hold(flat), "seq")
        with jax.named_scope("qkv_sum"):
            held["qkv"], send = call(
                mine_kernel,
                [((1, width // 4, 3 * group), FULL), ((1, width // 4, 3 * group), LOW)],
                [held["core"], one_tokens, qkv_grad],
                [hold(core_at, held["flat"]), row_at],
                "qkv_mine",
                0,
            )
            held["row"] = swap(send, "seq", 2)
        return (send, block_output)

    def ride_out(hold):
        with jax.named_scope("out_sum"):
            keep, send = ordered(row, out_sum[:, :quarter], out_sum[:, quarter:])
            some = send.shape[0] // 2
            first = swap(send[:some], "seq", 2)
            second = swap(after(send[some:], first), "seq", 2)
            held["out_sum"] = keep.astype(FULL) + jnp.concatenate([first, second]).astype(FULL)
        return (held["out_sum"],)

    def ride_heads(hold):
        with jax.named_scope("from_heads"):
            whole = (held["qkv"] + hold(held["row"]).astype(FULL))[0]
            sent_back = dot_t(whole.astype(LOW), pick_kept).astype(LOW)
            held["sent"] = take_rounds(sent_back, backward)
        with jax.named_scope("sum_vectors"):
            held["flat"] = sum_over(hold(held["flat"]), "ctx")
        with jax.named_scope("unit_sum"):
            got = hold(got_units).astype(FULL)
            held["fc"] = keep_units[0] + got[0]
            held["proj"] = jnp.transpose(keep_units[1] + got[1])
        return ()

    backward = [([(b, a) for a, b in pairs], start, size) for pairs, start, size in moves]
    with jax.named_scope("sum_one"):
        normed_one_grad = ring_sum(one_parts, one_far, [ride_core, ride_row, ride_out, ride_heads])
    with jax.named_scope("out_sum"):
        out_weight_grad = jnp.transpose(held["out_sum"])
    (input_grad,) = call(
        input_grad_kernel,
        [((rows, width), LOW)],
        [normed_one_grad, middle_grad, scaled_one, rate_one, ln1_gain[None]],
        [],
        "input_grad",
        0,
    )
    input_grad = input_grad.reshape(block_input.shape)
    with jax.named_scope("from_heads"):
        qkv_weight_grad = dot_t(jnp.concatenate(held["sent"], axis=1), pick_sent)
    fc_weight_grad, proj_weight_grad = held["fc"], held["proj"]
    flat = held["flat"]
    vectors = flat[: 8 * width].reshape(8, width)
    return (
        block_output,
        input_grad,
        vectors[0],
        vectors[1],
        qkv_weight_grad,
        vectors[2:4],
        out_weight_grad,
        vectors[4],
        vectors[5],
        vectors[6],
        fc_weight_grad,
        flat[8 * width :],
        proj_weight_grad,
        vectors[7],
    )


def solution(mesh):
    rows = P("seq", "ctx", None, None)
    cols = P("seq", "ctx")
    flip = P("ctx", "seq")
    one = P()
    return jax.shard_map(
        body,
        mesh=mesh,
        in_specs=(rows, rows, one, one, one, cols, one, cols, one, one, one, cols, one, flip, one),
        out_specs=(rows, rows, one, one, cols, one, cols, one, one, one, cols, one, flip, one),
        check_vma=False,
    )
```

```python
import functools
import math
import random

import jax
import jax.numpy as jnp
import numpy as np
from jax import lax
from jax.experimental import pallas as pl
from jax.experimental.pallas import tpu as pltpu
from jax.sharding import PartitionSpec as P

HEAD = 64
EPSILON = 1e-05
NEGATIVE = -1e30
GELU_COEF = 0.7978845608028654
LOW = jnp.bfloat16
FULL = jnp.float32
VMEM_BYTES = 56 * 2**20


def norm_parts(values):
    center = values - jnp.mean(values, axis=-1, keepdims=True)
    rate = lax.rsqrt(jnp.mean(center * center, axis=-1, keepdims=True) + EPSILON)
    return center * rate, rate


def norm_back(grad, scaled, rate, gain):
    inner = grad * gain
    return rate * (
        inner
        - jnp.mean(inner, axis=-1, keepdims=True)
        - scaled * jnp.mean(inner * scaled, axis=-1, keepdims=True)
    )


def gelu_parts(values):
    square = values * values
    bent = jnp.tanh(GELU_COEF * values * (1.0 + 0.044715 * square))
    slope = 0.5 * (1.0 + bent) + 0.5 * values * (1.0 - bent * bent) * GELU_COEF * (
        1.0 + 3.0 * 0.044715 * square
    )
    return 0.5 * values * (1.0 + bent), slope


def dot(left, right):
    return jnp.dot(left, right, preferred_element_type=FULL)


def dot_t(left, right):
    return lax.dot_general(left, right, (((1,), (1,)), ((), ())), preferred_element_type=FULL)


def t_dot(left, right):
    return lax.dot_general(left, right, (((0,), (0,)), ((), ())), preferred_element_type=FULL)


def swap(values, axis, bit):
    count = lax.axis_size(axis)
    return lax.ppermute(values, axis, [(i, i ^ bit) for i in range(count)])


def pick(values, places, count):
    return jnp.stack([lax.dynamic_index_in_dim(values, places[i], keepdims=False) for i in range(count)])


def ordered(flag, own, got):
    return jnp.where(flag == 0, own, got), jnp.where(flag == 0, got, own)


def joined(flag, own, got, axis):
    return jnp.concatenate(ordered(flag, own, got), axis)


def after(value, *first):
    return lax.optimization_barrier((value, *first))[0]


def after_all(first, value, *more):
    return after(value, *first, *more)


def ring_order(count):
    return list(range(0, count, 2)) + list(range(count - 1, 0, -2))


def shift(values, offset):
    order = ring_order(lax.axis_size("ctx"))
    count = len(order)
    return lax.ppermute(
        values, "ctx", [(order[i], order[(i + offset) % count]) for i in range(count)]
    )


def ring_gather(values, riders=()):
    count = lax.axis_size("ctx")
    half, rows = count // 2, values.shape[0] // 2
    ahead = behind = values
    riders = list(riders)
    pieces = [values] + [None] * (count - 1)
    for k in range(1, half + 1):
        rode = riders.pop(0)(lambda x, *more: after(x, ahead, behind, *more)) if riders else ()
        if k == half:
            pieces[half] = (shift(ahead[:rows], 1), shift(behind[rows:], -1))
            break
        ahead, behind = shift(ahead, 1), shift(behind, -1)
        pieces[count - k], pieces[k] = ahead, behind
        if rode:
            ahead, behind, *_ = lax.optimization_barrier((ahead, behind, *rode))
    return pieces[:half] + list(pieces[half]) + pieces[half + 1 :]


def ring_sum(held, far, riders=()):
    count = lax.axis_size("ctx")
    half, rows = count // 2, far.shape[0] // 2
    riders = list(riders)
    up, down = far[:rows], far[rows:]
    state = (up, down)
    for k in range(half - 1, -1, -1):
        rode = riders.pop(0)(functools.partial(after_all, state)) if riders else ()
        low_up, low_down = up.astype(LOW), down.astype(LOW)
        up, down = shift(low_up, 1).astype(FULL), shift(low_down, -1).astype(FULL)
        if k == half - 1:
            near, back = held[k], held[count - k]
            zero = jnp.zeros_like(up)
            up = near.astype(FULL) + jnp.concatenate([up, zero])
            down = back.astype(FULL) + jnp.concatenate([zero, down])
        elif k:
            up, down = held[k].astype(FULL) + up, held[count - k].astype(FULL) + down
        state = (up, down)
        if rode:
            up, down, *_ = lax.optimization_barrier((up, down, *rode))
    return held[0].astype(FULL) + up + down


def sum_over(values, axis, *gate):
    bit = 1
    while bit < lax.axis_size(axis):
        values = values + swap(values, axis, bit)
        bit *= 2
        if gate and 2 * bit == lax.axis_size(axis):
            values = after(values, *gate)
    return values


def seq_parts(shard):
    other = swap(shard, "seq", 2)
    pair = jnp.stack([shard, other])
    return pair, swap(pair, "seq", 1)


def seq_columns(tokens, core):
    part = tokens.shape[1] // 4
    blocks = [tokens[:, i * part : (i + 1) * part] for i in range(4)]
    return ordered(
        core, jnp.concatenate([blocks[0], blocks[2]], 1), jnp.concatenate([blocks[1], blocks[3]], 1)
    )


def seq_halves(held, got, row):
    half = held.shape[-2] // 2
    held = held + got.astype(FULL)
    keep, send = ordered(row, held[..., :half, :], held[..., half:, :])
    return keep, send.astype(LOW)


def head_plan(count, width):
    heads = width // HEAD
    group = -(-heads // count) * HEAD
    shard = 3 * width // count
    small = min(group, 128)
    edges = []
    for to in range(count):
        for part in range(3):
            low = part * width + to * group
            high = min(part * width + (to + 1) * group, (part + 1) * width)
            for come in range(count):
                a, b = max(low, come * shard), min(high, (come + 1) * shard)
                if a < b:
                    edges.append((come, to, a - come * shard, part * group + a - low, b - a))
    draw = random.Random(0)
    best, least = None, None
    for _ in range(300):
        draw.shuffle(edges)
        rounds = []
        for edge in sorted(edges, key=lambda e: e[4] <= small):
            for known in rounds:
                if all(edge[0] != e[0] and edge[1] != e[1] for e in known):
                    known.append(edge)
                    break
            else:
                rounds.append([edge])
        cost = sum(200 + (small if all(e[4] <= small for e in r) else group) for r in rounds)
        if least is None or cost < least:
            best, least = [list(r) for r in rounds], cost
    pairs, starts, sizes, total = [], [], [], 0
    for known in best:
        pairs.append([(e[0], e[1]) for e in known])
        starts.append(total)
        sizes.append(small if all(e[4] <= small for e in known) else group)
        total += sizes[-1]
    sent = np.full((count, total), -1, np.int32)
    kept = np.full((count, 3 * group), -1, np.int32)
    for known, begin in zip(best, starts, strict=True):
        for come, to, start, place, size in known:
            sent[come, begin : begin + size] = np.arange(start, start + size)
            kept[to, place : place + size] = begin + np.arange(size)
    moves = list(zip(pairs, starts, sizes, strict=True))
    return group, moves, sent, kept


def picker(places, size):
    return (lax.broadcasted_iota(jnp.int32, (size, places.shape[0]), 0) == places[None, :]).astype(LOW)


def move(values, pairs):
    return values if all(a == b for a, b in pairs) else lax.ppermute(values, "ctx", pairs)


def take_rounds(sent, moves):
    return [move(sent[:, start : start + size], pairs) for pairs, start, size in moves]


COST_US = {
    "attend": 60,
    "out": 30,
    "hidden_grad": 9,
    "hidden": 80,
    "branch": 8,
    "out_back": 45,
    "unit_other": 8,
    "unit_mine": 10,
    "qkv_other": 5,
    "qkv_mine": 6,
    "attend_back": 80,
    "project_back": 6,
    "input_grad": 100,
}


def call(kernel, outs, args, scalars, name, flops, scratch=()):
    spec = [pl.BlockSpec(memory_space=pltpu.SMEM)] * len(scalars)
    spec += [pl.BlockSpec(memory_space=pltpu.VMEM)] * len(args)
    moved = sum(math.prod(a.shape) * a.dtype.itemsize for a in args)
    moved += sum(math.prod(o[0]) * jnp.dtype(o[1]).itemsize for o in outs)
    return pl.pallas_call(
        kernel,
        in_specs=spec,
        out_specs=[pl.BlockSpec(memory_space=pltpu.VMEM)] * len(outs),
        out_shape=[jax.ShapeDtypeStruct(s, d) for s, d in outs],
        scratch_shapes=list(scratch),
        compiler_params=pltpu.CompilerParams(vmem_limit_bytes=VMEM_BYTES),
        cost_estimate=pl.CostEstimate(flops=1000, bytes_accessed=int(COST_US[name] * 3e6), transcendentals=0),
        name=name,
    )(*scalars, *args)


def put_tokens(member_ref, pieces, put, rows, count):
    half, middle = count // 2, rows // 2
    at = 0
    for k in range(count):
        member = member_ref[k]
        if k == half:
            put(member, 0, pieces[at][...])
            put(member, 1, pieces[at + 1][...])
            at += 2
        else:
            put(member, 0, pieces[at][:middle, :])
            put(member, 1, pieces[at][middle:, :])
            at += 1


def put_shards(place_ref, pair_ref, peer_ref, out_ref):
    seq = place_ref[0]
    height = out_ref.shape[0] // 4
    for k in range(4):
        source = pair_ref if k % 2 == 0 else peer_ref
        start = pl.multiple_of((seq ^ k) * height, 16)
        out_ref[pl.ds(start, height), :] = source[k // 2]


def causal(step, start, keys):
    query = lax.broadcasted_iota(jnp.int32, (step, keys), 0) + start
    return lax.broadcasted_iota(jnp.int32, (step, keys), 1) <= query


def each_step(tokens, run):
    if tokens <= 1024:
        step = min(256, tokens)
        for start in range(0, tokens, step):
            run(start, slice(start, start + step), step, start + step)
    else:
        step = 128

        @pl.loop(0, tokens // step)
        def _(i):
            start = pl.multiple_of(i * step, step)
            run(start, pl.ds(start, step), step, tokens)


def attend_kernel(
    n_pieces, heads, member_ref, place_ref, pair_of_ref, who_ref, pair_ref, peer_ref, shift_ref, *rest
):
    pieces = rest[:n_pieces]
    x_ref, w_ref, qkv_ref, full_ref, low_ref, lse_ref = rest[n_pieces:]
    count, rows, group = low_ref.shape
    tokens, block = count * rows, rows // 2
    put_shards(place_ref, pair_ref, peer_ref, w_ref)

    def put(member, half, values):
        pair = pair_of_ref[member]
        at = (2 * count - 1 - pair if half else pair) * block
        x_ref[pl.ds(pl.multiple_of(at, block), block), :] = values

    put_tokens(member_ref, pieces, put, rows, count)

    def project(start, part, step, keys):
        qkv_ref[part, :] = (dot(x_ref[part, :], w_ref[...]) + shift_ref[...]).astype(LOW)

    def some(start, part, step, keys):
        allowed = causal(step, start, keys)
        for h in range(heads):
            a, b = h * HEAD, (h + 1) * HEAD
            query = (qkv_ref[part, a:b] * (1.0 / math.sqrt(HEAD))).astype(LOW)
            score = jnp.where(allowed, dot_t(query, qkv_ref[:keys, group + a : group + b]), NEGATIVE)
            top = jnp.max(score, axis=1, keepdims=True)
            weight = jnp.exp(score - top)
            total = jnp.sum(weight, axis=1, keepdims=True)
            result = dot(weight.astype(LOW), qkv_ref[:keys, 2 * group + a : 2 * group + b]) / total
            full_ref[part, a:b] = result
            lse_ref[part, h : h + 1] = top + jnp.log(total)

    each_step(tokens, project)
    each_step(tokens, some)
    for j in range(2 * count):
        half = j // count * block
        low_ref[who_ref[j], half : half + block, :] = full_ref[j * block : (j + 1) * block, :].astype(LOW)


def attend_back_kernel(
    heads,
    who_ref,
    far_ref,
    qkv_ref,
    w_ref,
    full_ref,
    lse_ref,
    come_ref,
    out_ref,
    sum_ref,
    low_ref,
    dk_ref,
    dv_ref,
    grad_ref,
):
    count, rows, group = come_ref.shape
    tokens, block = count * rows, rows // 2
    scale = 1.0 / math.sqrt(HEAD)
    dk_ref[...] = jnp.zeros_like(dk_ref)
    dv_ref[...] = jnp.zeros_like(dv_ref)
    for j in range(2 * count):
        half = j // count * block
        grad_ref[j * block : (j + 1) * block, :] = come_ref[who_ref[j], half : half + block, :]

    def some(start, part, step, keys):
        allowed = causal(step, start, keys)
        for h in range(heads):
            a, b = h * HEAD, (h + 1) * HEAD
            query = (qkv_ref[part, a:b] * scale).astype(LOW)
            key = qkv_ref[:keys, group + a : group + b]
            value = qkv_ref[:keys, 2 * group + a : 2 * group + b]
            grad = grad_ref[part, a:b]
            delta = jnp.sum(grad.astype(FULL) * full_ref[part, a:b], axis=1, keepdims=True)
            score = dot_t(query, key)
            prob = jnp.where(allowed, jnp.exp(score - lse_ref[part, h : h + 1]), 0.0)
            score_grad = (prob * (dot_t(grad, value) - delta)).astype(LOW)
            out_ref[part, a:b] = (dot(score_grad, key) * scale).astype(LOW)
            dk_ref[:keys, a:b] += t_dot(score_grad, query)
            dv_ref[:keys, a:b] += t_dot(prob.astype(LOW), grad)

    each_step(tokens, some)
    out_ref[:, group : 2 * group] = dk_ref[...].astype(LOW)
    out_ref[:, 2 * group :] = dv_ref[...].astype(LOW)
    sum_ref[...] = jnp.sum(out_ref[...].astype(FULL), axis=0, keepdims=True)
    for half in range(2):
        start = pl.multiple_of(far_ref[half] * block, block)
        low_ref[half * block : (half + 1) * block, :] = dot_t(out_ref[pl.ds(start, block), :], w_ref[...]).astype(LOW)


def project_back_kernel(far_ref, grad_ref, w_ref, x_ref, norm_ref, gain_ref):
    count, rows, width = norm_ref.shape
    tokens, block = count * rows, rows // 2
    gain_ref[...] = jnp.zeros_like(gain_ref)
    step = min(256, tokens)
    for start in range(0, tokens, step):
        part = slice(start, start + step)
        total = dot_t(grad_ref[part, :], w_ref[...])
        gain_ref[0:1, :] += jnp.sum(total * x_ref[part, :].astype(FULL), axis=0, keepdims=True)
        gain_ref[1:2, :] += jnp.sum(total, axis=0, keepdims=True)
        for j in range(start // block, (start + step) // block):
            half, at = j // count * block, j * block - start
            norm_ref[far_ref[j], half : half + block, :] = total[at : at + block, :].astype(LOW)


def input_grad_kernel(sum_ref, mid_ref, scaled_ref, rate_ref, gain_ref, out_ref):
    part = norm_back(sum_ref[...], scaled_ref[...], rate_ref[...], gain_ref[...])
    out_ref[...] = (mid_ref[...] + part).astype(LOW)


def put_ring(offset, count, full_ref, low_ref, start, values):
    end = start + values.shape[0]

    @pl.when(offset == count // 2)
    def _():
        low_ref[start:end, :] = values.astype(LOW)

    @pl.when(offset != count // 2)
    def _():
        full_ref[offset, start:end, :] = values.astype(LOW)


def out_kernel(back_ref, input_ref, bias_ref, gain_ref, shift_ref, w_ref, mid_ref, low_ref, scaled_ref, rate_ref, attn_ref, wide_ref):
    count, rows, group = back_ref.shape
    width = mid_ref.shape[1]
    for d in range(count):
        wide_ref[:, d * group : (d + 1) * group] = back_ref[d]
    attn_ref[...] = wide_ref[:, :width]
    quarter, size = w_ref.shape[3], w_ref.shape[2]
    mid_ref[...] = input_ref[...].astype(FULL) + bias_ref[...]
    parts = [attn_ref[:, s * quarter : (s + 1) * quarter] for s in range(4)]
    for d in range(count):
        total = dot_t(parts[0], w_ref[0, d])
        for s in range(1, 4):
            total = total + dot_t(parts[s], w_ref[s, d])
        mid_ref[:, d * size : (d + 1) * size] += total
    scaled, rate = norm_parts(mid_ref[...])
    scaled_ref[...] = scaled
    rate_ref[...] = rate
    low_ref[...] = (scaled * gain_ref[...] + shift_ref[...]).astype(LOW)


def out_back_kernel(
    core_ref,
    sum_ref,
    cot_ref,
    scaled_ref,
    rate_ref,
    gain_ref,
    w_ref,
    attn_ref,
    mid_ref,
    low_ref,
    grad_ref,
    line_ref,
    mine_ref,
    other_ref,
    wide_ref,
    part_ref,
):
    count, rows, group = grad_ref.shape
    width = mid_ref.shape[1]
    cot = cot_ref[...].astype(FULL)
    total, scaled = sum_ref[...], scaled_ref[...]
    mid_ref[...] = cot + norm_back(total, scaled, rate_ref[...], gain_ref[...])
    low_ref[...] = mid_ref[...].astype(LOW)
    line_ref[0:1, :] = jnp.sum(low_ref[...].astype(FULL), axis=0, keepdims=True)
    line_ref[1:2, :] = jnp.sum(total * scaled, axis=0, keepdims=True)
    line_ref[2:3, :] = jnp.sum(total, axis=0, keepdims=True)
    line_ref[3:4, :] = jnp.sum(cot, axis=0, keepdims=True)
    quarter, size = w_ref.shape[3], w_ref.shape[2]
    wide_ref[:, width:] = jnp.zeros((rows, count * group - width), LOW)
    parts = [low_ref[:, d * size : (d + 1) * size] for d in range(count)]
    for s in range(4):
        part_ref[s] = attn_ref[:, s * quarter : (s + 1) * quarter]
        total = dot(parts[0], w_ref[s, 0])
        for d in range(1, count):
            total = total + dot(parts[d], w_ref[s, d])
        wide_ref[:, s * quarter : (s + 1) * quarter] = total.astype(LOW)
    core = core_ref[0]
    for d in range(count):
        grad_ref[d] = wide_ref[:, d * group : (d + 1) * group]
        for y in range(2):
            lanes = slice(y * quarter, (y + 1) * quarter)
            mine_ref[d, :, lanes] = t_dot(parts[d], part_ref[2 * y + core])
            other_ref[d, :, lanes] = t_dot(parts[d], part_ref[2 * y + 1 - core]).astype(LOW)


def seq_dots(core, left_ref, right, put):
    part = left_ref.shape[1] // 4
    for some in range(2):

        @pl.when(core == some)
        def _(some=some):
            for y in range(2):
                at = (2 * y + some) * part
                put(y, t_dot(left_ref[:, at : at + part], right))


def other_kernel(core_ref, *rest):
    *pairs, out_ref = rest

    for m in range(len(pairs) // 2):

        def put(y, total, m=m):
            out_ref[m, y] = total.astype(LOW)

        seq_dots(1 - core_ref[0], pairs[2 * m], pairs[2 * m + 1][...], put)


def mine_kernel(core_ref, row_ref, got_ref, *rest):
    *pairs, keep_ref, send_ref = rest

    for m in range(len(pairs) // 2):

        def put(y, total, m=m):
            total = total + got_ref[m, y].astype(FULL)

            @pl.when(row_ref[0] == y)
            def _():
                keep_ref[m] = total

            @pl.when(row_ref[0] != y)
            def _():
                send_ref[m] = total.astype(LOW)

        seq_dots(core_ref[0], pairs[2 * m], pairs[2 * m + 1][...], put)


def hidden_grad_kernel(place_ref, cot_ref, pair_ref, peer_ref, w_ref, grad_ref):
    put_shards(place_ref, pair_ref, peer_ref, w_ref)
    step = min(512, cot_ref.shape[0])
    for start in range(0, cot_ref.shape[0], step):
        grad_ref[start : start + step, :] = dot(cot_ref[start : start + step, :], w_ref[...])


def hidden_kernel(
    n_pieces, member_ref, offset_ref, place_ref, pair_ref, peer_ref, bias_ref, grad_ref, *rest
):
    pieces = rest[:n_pieces]
    x_ref, value_ref, slope_ref, sum_ref, far_ref, unit_ref, w_ref = rest[n_pieces:]
    count, rows, _ = sum_ref.shape
    middle = rows // 2
    put_shards(place_ref, pair_ref, peer_ref, w_ref)

    def put(member, half, values):
        at = pl.multiple_of(member * rows + half * middle, middle)
        x_ref[pl.ds(at, middle), :] = values

    put_tokens(member_ref, pieces, put, rows, count)
    unit_ref[...] = jnp.zeros_like(unit_ref)
    step = min(512, count * rows)
    for start in range(0, count * rows, step):
        part = slice(start, start + step)
        value, slope = gelu_parts(dot(x_ref[part, :], w_ref[...]) + bias_ref[...])
        value_ref[part, :] = value.astype(LOW)
        low = (grad_ref[part, :] * slope).astype(LOW)
        slope_ref[part, :] = low
        unit_ref[...] += jnp.sum(low.astype(FULL), axis=0, keepdims=True)
        total = dot_t(low, w_ref[...])
        for m in range(start // rows, (start + step) // rows):
            at = m * rows - start
            put_ring(offset_ref[m], count, sum_ref, far_ref, 0, total[at : at + rows, :])


def branch_kernel(value_ref, w_ref, out_ref):
    step = min(512, value_ref.shape[0])
    for start in range(0, value_ref.shape[0], step):
        part = slice(start, start + step)
        out_ref[part, :] = dot_t(value_ref[part, :], w_ref[...]).astype(LOW)


def body(
    block_input,
    out_cot,
    pair_of,
    ln1_gain,
    ln1_bias,
    qkv_weight,
    qv_bias,
    out_weight,
    out_bias,
    ln2_gain,
    ln2_bias,
    fc_weight,
    fc_bias,
    proj_weight,
    proj_bias,
):
    rows, width = block_input.shape[2], block_input.shape[3]
    count = lax.axis_size("ctx")
    tokens = count * rows
    fused = count <= 8
    seq, ctx = lax.axis_index("seq"), lax.axis_index("ctx")
    core, row = seq % 2, seq // 2
    order = np.array(ring_order(count), np.int32)
    rank = np.argsort(order)
    member = jnp.asarray(np.stack([np.roll(order, -i) for i in rank]).astype(np.int32))[ctx]
    offset = jnp.asarray(((rank[None, :] - rank[:, None]) % count).astype(np.int32))[ctx]
    place, core_at, row_at = seq[None], core[None], row[None]
    ranks = jnp.arange(count, dtype=jnp.int32)
    who = jnp.sum(jnp.where(pair_of[None, :] == ranks[:, None], ranks[None, :], 0), axis=1)
    who = jnp.concatenate([who, who[::-1]]).astype(jnp.int32)
    far_of = offset[who]
    input_low = block_input.reshape(rows, width)
    inputs = input_low.astype(FULL)
    cot_low = out_cot.reshape(rows, width)

    group, moves, sent, kept = head_plan(count, width)
    heads = group // HEAD
    pick_sent = picker(jnp.asarray(sent)[ctx], qkv_weight.shape[1])
    pick_kept = picker(jnp.asarray(kept)[ctx], sent.shape[1])
    scaled_one, rate_one = norm_parts(inputs)
    normed_one = (scaled_one * ln1_gain + ln1_bias).astype(LOW)
    units = fc_weight.shape[1]
    held = {}

    with jax.named_scope("to_heads"):
        sent_heads = dot(qkv_weight, pick_sent).astype(LOW)
    first = len(moves) // 2

    def ride_first(hold):
        with jax.named_scope("to_heads"):
            held["first"] = take_rounds(sent_heads, moves[:first])
        held["out"] = lax.all_gather(jnp.transpose(out_weight), ("seq", "ctx"), axis=0)
        return held["first"]

    def ride_second(hold):
        with jax.named_scope("to_heads"):
            held["second"] = take_rounds(hold(sent_heads), moves[first:])
        return held["second"]

    def ride_row_parts(hold):
        with jax.named_scope("qkv_parts"):
            pieces = jnp.concatenate(held["first"] + held["second"], axis=1)
            own = dot(hold(pieces), pick_kept).astype(LOW)
            held["own"], held["row"] = own, swap(own, "seq", 2)
        return ()

    def ride_core_parts(hold):
        with jax.named_scope("qkv_parts"):
            held["pair"] = jnp.stack([held["own"], hold(held["row"])])
            held["peer"] = swap(held["pair"], "seq", 1)
        return ()

    with jax.named_scope("gather_one"):
        gathered = ring_gather(normed_one, [ride_first, ride_second, ride_row_parts, ride_core_parts])
    qkv_pair, qkv_peer = held["pair"], held["peer"]
    out_t = held["out"].reshape(4, count, out_weight.shape[1], out_weight.shape[0])
    bias_rows = jnp.pad(qv_bias, ((0, 0), (0, count * group - width)))
    bias_mine = lax.dynamic_slice_in_dim(bias_rows, ctx * group, group, 1)
    qkv_shift = jnp.concatenate([bias_mine[:1], jnp.zeros((1, group), FULL), bias_mine[1:]], axis=1)
    with jax.named_scope("unit_parts"):
        proj_own = after(jnp.transpose(proj_weight), qkv_peer)
        proj_pair = jnp.stack([proj_own, swap(proj_own, "seq", 2)])

    one_tokens, qkv_cols, qkv, attn_full, attn_part, lse = call(
        functools.partial(attend_kernel, len(gathered), heads),
        [
            ((tokens, width), LOW),
            ((width, 3 * group), LOW),
            ((tokens, 3 * group), LOW),
            ((tokens, group), FULL),
            ((count, rows, group), LOW),
            ((tokens, heads), FULL),
        ],
        [qkv_pair, qkv_peer, qkv_shift, *gathered],
        [member, place, pair_of, who],
        "attend",
        2 * tokens * width * 3 * group + 16 * tokens * tokens * group,
    )
    attn_part, proj_pair = lax.optimization_barrier((attn_part, proj_pair))
    with jax.named_scope("unit_parts"):
        fc_own = after(fc_weight, attn_part)
        fc_pair = jnp.stack([fc_own, swap(fc_own, "seq", 2)])
    cots = lax.all_gather(after(cot_low, qkv_peer), "ctx", axis=0, tiled=True)

    back = lax.all_to_all(attn_part, "ctx", 0, 0, tiled=True)
    back, proj_pair, fc_pair = lax.optimization_barrier((back, proj_pair, fc_pair))
    with jax.named_scope("unit_parts"):
        proj_peer = swap(proj_pair, "seq", 1)
        fc_peer = swap(fc_pair, "seq", 1)
    middle, normed_two, scaled_two, rate_two, attn_low = call(
        out_kernel,
        [
            ((rows, width), FULL),
            ((rows, width), LOW),
            ((rows, width), FULL),
            ((rows, 1), FULL),
            ((rows, width), LOW),
        ],
        [back, input_low, out_bias[None], ln2_gain[None], ln2_bias[None], out_t],
        [],
        "out",
        2 * rows * width * width,
        [pltpu.VMEM((rows, count * group), LOW)],
    )

    proj_cols, hidden_grad = call(
        hidden_grad_kernel,
        [((width, units), LOW), ((tokens, units), FULL)],
        [cots, proj_pair, proj_peer],
        [place],
        "hidden_grad",
        2 * tokens * width * units,
    )
    with jax.named_scope("gather_two"):
        two_gathered = ring_gather(normed_two)
    bias_units = lax.dynamic_slice_in_dim(fc_bias, ctx * units, units)[None]
    if fused:
        two_tokens, hidden, hidden_pre_grad, two_parts, two_far, units_grad = call(
            functools.partial(hidden_kernel, len(two_gathered)),
            [
                ((tokens, width), LOW),
                ((tokens, units), LOW),
                ((tokens, units), LOW),
                ((count, rows, width), LOW),
                ((rows, width), LOW),
                ((1, units), FULL),
            ],
            [fc_pair, fc_peer, bias_units, hidden_grad, *two_gathered],
            [member, offset, place],
            "hidden",
            4 * tokens * width * units,
            [pltpu.VMEM((width, units), LOW)],
        )
    else:
        far = count // 2
        pieces = two_gathered[:far] + [jnp.concatenate(two_gathered[far : far + 2])] + two_gathered[far + 2 :]
        two_tokens = pick(jnp.stack(pieces), offset, count).reshape(tokens, width)
        shards = jnp.stack([fc_pair[0], fc_peer[0], fc_pair[1], fc_peer[1]])
        fc_cols = pick(shards, seq ^ jnp.arange(4), 4).reshape(width, units)
        value, slope = gelu_parts(dot(two_tokens, fc_cols) + bias_units)
        hidden = value.astype(LOW)
        hidden_pre_grad = (hidden_grad * slope).astype(LOW)
        two_parts = pick(dot_t(hidden_pre_grad, fc_cols).reshape(count, rows, width), member, count)
        two_far = two_parts[far].astype(LOW)
        units_grad = jnp.sum(hidden_pre_grad.astype(FULL), axis=0)
    def ride_branch(hold):
        (held["branch"],) = call(
            branch_kernel, [((tokens, width), LOW)], [hold(hidden), proj_cols], [], "branch", 2 * tokens * width * units
        )
        return (held["branch"],)

    def ride_other(hold):
        with jax.named_scope("unit_sum"):
            (other,) = call(
                other_kernel,
                [((2, 2, width // 4, units), LOW)],
                [two_tokens, hidden_pre_grad, cots, hidden],
                [hold(core_at)],
                "unit_other",
                0,
            )
            held["peer"] = swap(other, "seq", 1)
        return (other,)

    with jax.named_scope("sum_two"):
        normed_two_grad = ring_sum(two_parts, two_far, [lambda hold: (), ride_branch, ride_other])
    branch_two = lax.psum_scatter(held["branch"], "ctx", scatter_dimension=0, tiled=True)
    block_output = (middle + branch_two.astype(FULL) + proj_bias).astype(LOW).reshape(block_input.shape)

    size, quarter = out_t.shape[2], out_t.shape[3]
    middle_grad, branch_low, attn_grad, lines, whole_out, other = call(
        out_back_kernel,
        [
            ((rows, width), FULL),
            ((rows, width), LOW),
            ((count, rows, group), LOW),
            ((4, width), FULL),
            ((count, size, 2 * quarter), FULL),
            ((count, size, 2 * quarter), LOW),
        ],
        [normed_two_grad, cot_low, scaled_two, rate_two, ln2_gain[None], out_t, attn_low],
        [core_at],
        "out_back",
        2 * rows * width * width,
        [pltpu.VMEM((rows, count * group), LOW), pltpu.VMEM((4, rows, quarter), LOW)],
    )
    grad_part = lax.all_to_all(attn_grad, "ctx", 0, 0, tiled=True)
    with jax.named_scope("out_sum"):
        got_core_out = swap(other, "seq", 1)
        half_sum = (whole_out + got_core_out.astype(FULL)).astype(LOW)
        with jax.named_scope("unit_sum"):
            keep_units, send_units = call(
                mine_kernel,
                [((2, width // 4, units), FULL), ((2, width // 4, units), LOW)],
                [held["peer"], two_tokens, hidden_pre_grad, cots, hidden],
                [after(core_at, half_sum), row_at],
                "unit_mine",
                0,
            )
        grad_part, send_units = lax.optimization_barrier((grad_part, send_units))
        with jax.named_scope("unit_sum"):
            got_units = swap(send_units, "seq", 2)
        out_sum = lax.psum_scatter(half_sum, "ctx", scatter_dimension=0)

    far_pair = pair_of[member[count // 2]]
    qkv_grad, cols_sum, one_far = call(
        functools.partial(attend_back_kernel, heads),
        [((tokens, 3 * group), LOW), ((1, 3 * group), FULL), ((rows, width), LOW)],
        [qkv, qkv_cols, attn_full, lse, grad_part],
        [who, jnp.stack([far_pair, 2 * count - 1 - far_pair])],
        "attend_back",
        0,
        [pltpu.VMEM((tokens, group), FULL)] * 2 + [pltpu.VMEM((tokens, group), LOW)],
    )
    if fused:
        one_parts, one_lines = call(
            project_back_kernel,
            [((count, rows, width), LOW), ((2, width), FULL)],
            [qkv_grad, qkv_cols, one_tokens],
            [after(far_of, got_units)],
            "project_back",
            0,
        )
    else:
        parts = dot_t(qkv_grad, qkv_cols)
        one_lines = jnp.stack([jnp.sum(parts * one_tokens.astype(FULL), axis=0), jnp.sum(parts, axis=0)])
        parts = parts.reshape(2 * count, rows // 2, width)
        pairs = pair_of[member]
        one_parts = jnp.concatenate([pick(parts, pairs, count), pick(parts, 2 * count - 1 - pairs, count)], axis=1)

    shift_one = one_lines[1]
    gain_one = (one_lines[0] - ln1_bias * shift_one) / ln1_gain
    qv_sums = jnp.concatenate([cols_sum[:, :group], cols_sum[:, 2 * group :]])
    qv_sums = lax.dynamic_update_slice(
        jnp.zeros((2, count * group), FULL), qv_sums, (0, ctx * group)
    )[:, :width]
    unit_sums = lax.dynamic_update_slice(
        jnp.zeros((count * units,), FULL), units_grad.reshape(-1), (ctx * units,)
    )
    flat = [gain_one, shift_one, qv_sums.reshape(-1), lines.reshape(-1), unit_sums]
    flat = jnp.concatenate(flat)

    def ride_core(hold):
        with jax.named_scope("qkv_sum"):
            (other,) = call(
                other_kernel,
                [((1, 2, width // 4, 3 * group), LOW)],
                [one_tokens, qkv_grad],
                [core_at],
                "qkv_other",
                0,
            )
            held["core"] = swap(other, "seq", 1)
        return (held["core"],)

    def ride_row(hold):
        with jax.named_scope("sum_vectors"):
            held["flat"] = sum_over(hold(flat), "seq")
        with jax.named_scope("qkv_sum"):
            held["qkv"], send = call(
                mine_kernel,
                [((1, width // 4, 3 * group), FULL), ((1, width // 4, 3 * group), LOW)],
                [held["core"], one_tokens, qkv_grad],
                [hold(core_at, held["flat"]), row_at],
                "qkv_mine",
                0,
            )
            held["row"] = swap(send, "seq", 2)
        return (send, block_output)

    def ride_out(hold):
        with jax.named_scope("out_sum"):
            keep, send = ordered(row, out_sum[:, :quarter], out_sum[:, quarter:])
            some = send.shape[0] // 2
            first = swap(send[:some], "seq", 2)
            second = swap(after(send[some:], first), "seq", 2)
            held["out_sum"] = keep.astype(FULL) + jnp.concatenate([first, second]).astype(FULL)
        return (held["out_sum"],)

    def ride_heads(hold):
        with jax.named_scope("from_heads"):
            whole = (held["qkv"] + hold(held["row"]).astype(FULL))[0]
            sent_back = dot_t(whole.astype(LOW), pick_kept).astype(LOW)
            held["sent"] = take_rounds(sent_back, backward)
        with jax.named_scope("sum_vectors"):
            held["flat"] = sum_over(hold(held["flat"]), "ctx")
        with jax.named_scope("unit_sum"):
            got = hold(got_units).astype(FULL)
            held["fc"] = keep_units[0] + got[0]
            held["proj"] = jnp.transpose(keep_units[1] + got[1])
        return ()

    backward = [([(b, a) for a, b in pairs], start, size) for pairs, start, size in moves]
    with jax.named_scope("sum_one"):
        normed_one_grad = ring_sum(one_parts, one_far, [ride_core, ride_row, ride_out, ride_heads])
    with jax.named_scope("out_sum"):
        out_weight_grad = jnp.transpose(held["out_sum"])
    (input_grad,) = call(
        input_grad_kernel,
        [((rows, width), LOW)],
        [normed_one_grad, middle_grad, scaled_one, rate_one, ln1_gain[None]],
        [],
        "input_grad",
        0,
    )
    input_grad = input_grad.reshape(block_input.shape)
    with jax.named_scope("from_heads"):
        qkv_weight_grad = dot_t(jnp.concatenate(held["sent"], axis=1), pick_sent)
    fc_weight_grad, proj_weight_grad = held["fc"], held["proj"]
    flat = held["flat"]
    vectors = flat[: 8 * width].reshape(8, width)
    return (
        block_output,
        input_grad,
        vectors[0],
        vectors[1],
        qkv_weight_grad,
        vectors[2:4],
        out_weight_grad,
        vectors[4],
        vectors[5],
        vectors[6],
        fc_weight_grad,
        flat[8 * width :],
        proj_weight_grad,
        vectors[7],
    )


def solution(mesh):
    rows = P("seq", "ctx", None, None)
    cols = P("seq", "ctx")
    flip = P("ctx", "seq")
    one = P()
    return jax.shard_map(
        body,
        mesh=mesh,
        in_specs=(rows, rows, one, one, one, cols, one, cols, one, one, one, cols, one, flip, one),
        out_specs=(rows, rows, one, one, cols, one, cols, one, one, one, cols, one, flip, one),
        check_vma=False,
    )
```

```python
import functools
import math
import random

import jax
import jax.numpy as jnp
import numpy as np
from jax import lax
from jax.experimental import pallas as pl
from jax.experimental.pallas import tpu as pltpu
from jax.sharding import PartitionSpec as P

HEAD = 64
EPSILON = 1e-05
NEGATIVE = -1e30
GELU_COEF = 0.7978845608028654
LOW = jnp.bfloat16
FULL = jnp.float32
VMEM_BYTES = 56 * 2**20


def norm_parts(values):
    center = values - jnp.mean(values, axis=-1, keepdims=True)
    rate = lax.rsqrt(jnp.mean(center * center, axis=-1, keepdims=True) + EPSILON)
    return center * rate, rate


def norm_back(grad, scaled, rate, gain):
    inner = grad * gain
    return rate * (
        inner
        - jnp.mean(inner, axis=-1, keepdims=True)
        - scaled * jnp.mean(inner * scaled, axis=-1, keepdims=True)
    )


def gelu_parts(values):
    square = values * values
    bent = jnp.tanh(GELU_COEF * values * (1.0 + 0.044715 * square))
    slope = 0.5 * (1.0 + bent) + 0.5 * values * (1.0 - bent * bent) * GELU_COEF * (
        1.0 + 3.0 * 0.044715 * square
    )
    return 0.5 * values * (1.0 + bent), slope


def dot(left, right):
    return jnp.dot(left, right, preferred_element_type=FULL)


def dot_t(left, right):
    return lax.dot_general(left, right, (((1,), (1,)), ((), ())), preferred_element_type=FULL)


def t_dot(left, right):
    return lax.dot_general(left, right, (((0,), (0,)), ((), ())), preferred_element_type=FULL)


def swap(values, axis, bit):
    count = lax.axis_size(axis)
    return lax.ppermute(values, axis, [(i, i ^ bit) for i in range(count)])


def pick(values, places, count):
    return jnp.stack([lax.dynamic_index_in_dim(values, places[i], keepdims=False) for i in range(count)])


def ordered(flag, own, got):
    return jnp.where(flag == 0, own, got), jnp.where(flag == 0, got, own)


def joined(flag, own, got, axis):
    return jnp.concatenate(ordered(flag, own, got), axis)


def after(value, *first):
    return lax.optimization_barrier((value, *first))[0]


def after_all(first, value, *more):
    return after(value, *first, *more)


def ring_order(count):
    return list(range(0, count, 2)) + list(range(count - 1, 0, -2))


def shift(values, offset):
    order = ring_order(lax.axis_size("ctx"))
    count = len(order)
    return lax.ppermute(
        values, "ctx", [(order[i], order[(i + offset) % count]) for i in range(count)]
    )


def ring_gather(values, riders=()):
    count = lax.axis_size("ctx")
    half, rows = count // 2, values.shape[0] // 2
    ahead = behind = values
    riders = list(riders)
    pieces = [values] + [None] * (count - 1)
    for k in range(1, half + 1):
        rode = riders.pop(0)(lambda x, *more: after(x, ahead, behind, *more)) if riders else ()
        if k == half:
            pieces[half] = (shift(ahead[:rows], 1), shift(behind[rows:], -1))
            break
        ahead, behind = shift(ahead, 1), shift(behind, -1)
        pieces[count - k], pieces[k] = ahead, behind
        if rode:
            ahead, behind, *_ = lax.optimization_barrier((ahead, behind, *rode))
    return pieces[:half] + list(pieces[half]) + pieces[half + 1 :]


def ring_sum(held, far, riders=()):
    count = lax.axis_size("ctx")
    half, rows = count // 2, far.shape[0] // 2
    riders = list(riders)
    up, down = far[:rows], far[rows:]
    state = (up, down)
    for k in range(half - 1, -1, -1):
        rode = riders.pop(0)(functools.partial(after_all, state)) if riders else ()
        low_up, low_down = up.astype(LOW), down.astype(LOW)
        up, down = shift(low_up, 1).astype(FULL), shift(low_down, -1).astype(FULL)
        if k == half - 1:
            near, back = held[k], held[count - k]
            zero = jnp.zeros_like(up)
            up = near.astype(FULL) + jnp.concatenate([up, zero])
            down = back.astype(FULL) + jnp.concatenate([zero, down])
        elif k:
            up, down = held[k].astype(FULL) + up, held[count - k].astype(FULL) + down
        state = (up, down)
        if rode:
            up, down, *_ = lax.optimization_barrier((up, down, *rode))
    return held[0].astype(FULL) + up + down


def sum_over(values, axis, *gate):
    bit = 1
    while bit < lax.axis_size(axis):
        values = values + swap(values, axis, bit)
        bit *= 2
        if gate and 2 * bit == lax.axis_size(axis):
            values = after(values, *gate)
    return values


def seq_parts(shard):
    other = swap(shard, "seq", 2)
    pair = jnp.stack([shard, other])
    return pair, swap(pair, "seq", 1)


def seq_columns(tokens, core):
    part = tokens.shape[1] // 4
    blocks = [tokens[:, i * part : (i + 1) * part] for i in range(4)]
    return ordered(
        core, jnp.concatenate([blocks[0], blocks[2]], 1), jnp.concatenate([blocks[1], blocks[3]], 1)
    )


def seq_halves(held, got, row):
    half = held.shape[-2] // 2
    held = held + got.astype(FULL)
    keep, send = ordered(row, held[..., :half, :], held[..., half:, :])
    return keep, send.astype(LOW)


def head_plan(count, width):
    heads = width // HEAD
    group = -(-heads // count) * HEAD
    shard = 3 * width // count
    small = min(group, 128)
    edges = []
    for to in range(count):
        for part in range(3):
            low = part * width + to * group
            high = min(part * width + (to + 1) * group, (part + 1) * width)
            for come in range(count):
                a, b = max(low, come * shard), min(high, (come + 1) * shard)
                if a < b:
                    edges.append((come, to, a - come * shard, part * group + a - low, b - a))
    draw = random.Random(0)
    best, least = None, None
    for _ in range(300):
        draw.shuffle(edges)
        rounds = []
        for edge in sorted(edges, key=lambda e: e[4] <= small):
            for known in rounds:
                if all(edge[0] != e[0] and edge[1] != e[1] for e in known):
                    known.append(edge)
                    break
            else:
                rounds.append([edge])
        cost = sum(200 + (small if all(e[4] <= small for e in r) else group) for r in rounds)
        if least is None or cost < least:
            best, least = [list(r) for r in rounds], cost
    pairs, starts, sizes, total = [], [], [], 0
    for known in best:
        pairs.append([(e[0], e[1]) for e in known])
        starts.append(total)
        sizes.append(small if all(e[4] <= small for e in known) else group)
        total += sizes[-1]
    sent = np.full((count, total), -1, np.int32)
    kept = np.full((count, 3 * group), -1, np.int32)
    for known, begin in zip(best, starts, strict=True):
        for come, to, start, place, size in known:
            sent[come, begin : begin + size] = np.arange(start, start + size)
            kept[to, place : place + size] = begin + np.arange(size)
    moves = list(zip(pairs, starts, sizes, strict=True))
    return group, moves, sent, kept


def picker(places, size):
    return (lax.broadcasted_iota(jnp.int32, (size, places.shape[0]), 0) == places[None, :]).astype(LOW)


def move(values, pairs):
    return values if all(a == b for a, b in pairs) else lax.ppermute(values, "ctx", pairs)


def take_rounds(sent, moves):
    return [move(sent[:, start : start + size], pairs) for pairs, start, size in moves]


COST_US = {
    "attend": 60,
    "out": 30,
    "hidden_grad": 9,
    "hidden": 80,
    "branch": 8,
    "out_back": 45,
    "unit_other": 8,
    "unit_mine": 10,
    "qkv_other": 5,
    "qkv_mine": 6,
    "attend_back": 80,
    "project_back": 6,
    "input_grad": 100,
}


def call(kernel, outs, args, scalars, name, flops, scratch=()):
    spec = [pl.BlockSpec(memory_space=pltpu.SMEM)] * len(scalars)
    spec += [pl.BlockSpec(memory_space=pltpu.VMEM)] * len(args)
    moved = sum(math.prod(a.shape) * a.dtype.itemsize for a in args)
    moved += sum(math.prod(o[0]) * jnp.dtype(o[1]).itemsize for o in outs)
    return pl.pallas_call(
        kernel,
        in_specs=spec,
        out_specs=[pl.BlockSpec(memory_space=pltpu.VMEM)] * len(outs),
        out_shape=[jax.ShapeDtypeStruct(s, d) for s, d in outs],
        scratch_shapes=list(scratch),
        compiler_params=pltpu.CompilerParams(vmem_limit_bytes=VMEM_BYTES),
        cost_estimate=pl.CostEstimate(flops=1000, bytes_accessed=int(COST_US[name] * 3e6), transcendentals=0),
        name=name,
    )(*scalars, *args)


def put_tokens(member_ref, pieces, put, rows, count):
    half, middle = count // 2, rows // 2
    at = 0
    for k in range(count):
        member = member_ref[k]
        if k == half:
            put(member, 0, pieces[at][...])
            put(member, 1, pieces[at + 1][...])
            at += 2
        else:
            put(member, 0, pieces[at][:middle, :])
            put(member, 1, pieces[at][middle:, :])
            at += 1


def put_shards(place_ref, pair_ref, peer_ref, out_ref):
    seq = place_ref[0]
    height = out_ref.shape[0] // 4
    for k in range(4):
        source = pair_ref if k % 2 == 0 else peer_ref
        start = pl.multiple_of((seq ^ k) * height, 16)
        out_ref[pl.ds(start, height), :] = source[k // 2]


def causal(step, start, keys):
    query = lax.broadcasted_iota(jnp.int32, (step, keys), 0) + start
    return lax.broadcasted_iota(jnp.int32, (step, keys), 1) <= query


def each_step(tokens, run):
    if tokens <= 1024:
        step = min(256, tokens)
        for start in range(0, tokens, step):
            run(start, slice(start, start + step), step, start + step)
    else:
        step = 128

        @pl.loop(0, tokens // step)
        def _(i):
            start = pl.multiple_of(i * step, step)
            run(start, pl.ds(start, step), step, tokens)


def attend_kernel(
    n_pieces, heads, member_ref, place_ref, pair_of_ref, who_ref, pair_ref, peer_ref, shift_ref, *rest
):
    pieces = rest[:n_pieces]
    x_ref, w_ref, qkv_ref, full_ref, low_ref, lse_ref = rest[n_pieces:]
    count, rows, group = low_ref.shape
    tokens, block = count * rows, rows // 2
    put_shards(place_ref, pair_ref, peer_ref, w_ref)

    def put(member, half, values):
        pair = pair_of_ref[member]
        at = (2 * count - 1 - pair if half else pair) * block
        x_ref[pl.ds(pl.multiple_of(at, block), block), :] = values

    put_tokens(member_ref, pieces, put, rows, count)

    def project(start, part, step, keys):
        qkv_ref[part, :] = (dot(x_ref[part, :], w_ref[...]) + shift_ref[...]).astype(LOW)

    def some(start, part, step, keys):
        allowed = causal(step, start, keys)
        for h in range(heads):
            a, b = h * HEAD, (h + 1) * HEAD
            query = (qkv_ref[part, a:b] * (1.0 / math.sqrt(HEAD))).astype(LOW)
            score = jnp.where(allowed, dot_t(query, qkv_ref[:keys, group + a : group + b]), NEGATIVE)
            top = jnp.max(score, axis=1, keepdims=True)
            weight = jnp.exp(score - top)
            total = jnp.sum(weight, axis=1, keepdims=True)
            result = dot(weight.astype(LOW), qkv_ref[:keys, 2 * group + a : 2 * group + b]) / total
            full_ref[part, a:b] = result
            lse_ref[part, h : h + 1] = top + jnp.log(total)

    each_step(tokens, project)
    each_step(tokens, some)
    for j in range(2 * count):
        half = j // count * block
        low_ref[who_ref[j], half : half + block, :] = full_ref[j * block : (j + 1) * block, :].astype(LOW)


def attend_back_kernel(
    heads,
    who_ref,
    far_ref,
    qkv_ref,
    w_ref,
    full_ref,
    lse_ref,
    come_ref,
    out_ref,
    sum_ref,
    low_ref,
    dk_ref,
    dv_ref,
    grad_ref,
):
    count, rows, group = come_ref.shape
    tokens, block = count * rows, rows // 2
    scale = 1.0 / math.sqrt(HEAD)
    dk_ref[...] = jnp.zeros_like(dk_ref)
    dv_ref[...] = jnp.zeros_like(dv_ref)
    for j in range(2 * count):
        half = j // count * block
        grad_ref[j * block : (j + 1) * block, :] = come_ref[who_ref[j], half : half + block, :]

    def some(start, part, step, keys):
        allowed = causal(step, start, keys)
        for h in range(heads):
            a, b = h * HEAD, (h + 1) * HEAD
            query = (qkv_ref[part, a:b] * scale).astype(LOW)
            key = qkv_ref[:keys, group + a : group + b]
            value = qkv_ref[:keys, 2 * group + a : 2 * group + b]
            grad = grad_ref[part, a:b]
            delta = jnp.sum(grad.astype(FULL) * full_ref[part, a:b], axis=1, keepdims=True)
            score = dot_t(query, key)
            prob = jnp.where(allowed, jnp.exp(score - lse_ref[part, h : h + 1]), 0.0)
            score_grad = (prob * (dot_t(grad, value) - delta)).astype(LOW)
            out_ref[part, a:b] = (dot(score_grad, key) * scale).astype(LOW)
            dk_ref[:keys, a:b] += t_dot(score_grad, query)
            dv_ref[:keys, a:b] += t_dot(prob.astype(LOW), grad)

    each_step(tokens, some)
    out_ref[:, group : 2 * group] = dk_ref[...].astype(LOW)
    out_ref[:, 2 * group :] = dv_ref[...].astype(LOW)
    sum_ref[...] = jnp.sum(out_ref[...].astype(FULL), axis=0, keepdims=True)
    for half in range(2):
        start = pl.multiple_of(far_ref[half] * block, block)
        low_ref[half * block : (half + 1) * block, :] = dot_t(out_ref[pl.ds(start, block), :], w_ref[...]).astype(LOW)


def project_back_kernel(far_ref, grad_ref, w_ref, x_ref, norm_ref, gain_ref):
    count, rows, width = norm_ref.shape
    tokens, block = count * rows, rows // 2
    gain_ref[...] = jnp.zeros_like(gain_ref)
    step = min(256, tokens)
    for start in range(0, tokens, step):
        part = slice(start, start + step)
        total = dot_t(grad_ref[part, :], w_ref[...])
        gain_ref[0:1, :] += jnp.sum(total * x_ref[part, :].astype(FULL), axis=0, keepdims=True)
        gain_ref[1:2, :] += jnp.sum(total, axis=0, keepdims=True)
        for j in range(start // block, (start + step) // block):
            half, at = j // count * block, j * block - start
            norm_ref[far_ref[j], half : half + block, :] = total[at : at + block, :].astype(LOW)


def input_grad_kernel(sum_ref, mid_ref, scaled_ref, rate_ref, gain_ref, out_ref):
    part = norm_back(sum_ref[...], scaled_ref[...], rate_ref[...], gain_ref[...])
    out_ref[...] = (mid_ref[...] + part).astype(LOW)


def put_ring(offset, count, full_ref, low_ref, start, values):
    end = start + values.shape[0]

    @pl.when(offset == count // 2)
    def _():
        low_ref[start:end, :] = values.astype(LOW)

    @pl.when(offset != count // 2)
    def _():
        full_ref[offset, start:end, :] = values.astype(LOW)


def out_kernel(back_ref, input_ref, bias_ref, gain_ref, shift_ref, w_ref, mid_ref, low_ref, scaled_ref, rate_ref, attn_ref, wide_ref):
    count, rows, group = back_ref.shape
    width = mid_ref.shape[1]
    for d in range(count):
        wide_ref[:, d * group : (d + 1) * group] = back_ref[d]
    attn_ref[...] = wide_ref[:, :width]
    quarter, size = w_ref.shape[3], w_ref.shape[2]
    mid_ref[...] = input_ref[...].astype(FULL) + bias_ref[...]
    parts = [attn_ref[:, s * quarter : (s + 1) * quarter] for s in range(4)]
    for d in range(count):
        total = dot_t(parts[0], w_ref[0, d])
        for s in range(1, 4):
            total = total + dot_t(parts[s], w_ref[s, d])
        mid_ref[:, d * size : (d + 1) * size] += total
    scaled, rate = norm_parts(mid_ref[...])
    scaled_ref[...] = scaled
    rate_ref[...] = rate
    low_ref[...] = (scaled * gain_ref[...] + shift_ref[...]).astype(LOW)


def out_back_kernel(
    core_ref,
    sum_ref,
    cot_ref,
    scaled_ref,
    rate_ref,
    gain_ref,
    w_ref,
    attn_ref,
    mid_ref,
    low_ref,
    grad_ref,
    line_ref,
    mine_ref,
    other_ref,
    wide_ref,
    part_ref,
):
    count, rows, group = grad_ref.shape
    width = mid_ref.shape[1]
    cot = cot_ref[...].astype(FULL)
    total, scaled = sum_ref[...], scaled_ref[...]
    mid_ref[...] = cot + norm_back(total, scaled, rate_ref[...], gain_ref[...])
    low_ref[...] = mid_ref[...].astype(LOW)
    line_ref[0:1, :] = jnp.sum(low_ref[...].astype(FULL), axis=0, keepdims=True)
    line_ref[1:2, :] = jnp.sum(total * scaled, axis=0, keepdims=True)
    line_ref[2:3, :] = jnp.sum(total, axis=0, keepdims=True)
    line_ref[3:4, :] = jnp.sum(cot, axis=0, keepdims=True)
    quarter, size = w_ref.shape[3], w_ref.shape[2]
    wide_ref[:, width:] = jnp.zeros((rows, count * group - width), LOW)
    parts = [low_ref[:, d * size : (d + 1) * size] for d in range(count)]
    for s in range(4):
        part_ref[s] = attn_ref[:, s * quarter : (s + 1) * quarter]
        total = dot(parts[0], w_ref[s, 0])
        for d in range(1, count):
            total = total + dot(parts[d], w_ref[s, d])
        wide_ref[:, s * quarter : (s + 1) * quarter] = total.astype(LOW)
    core = core_ref[0]
    for d in range(count):
        grad_ref[d] = wide_ref[:, d * group : (d + 1) * group]
        for y in range(2):
            lanes = slice(y * quarter, (y + 1) * quarter)
            mine_ref[d, :, lanes] = t_dot(parts[d], part_ref[2 * y + core])
            other_ref[d, :, lanes] = t_dot(parts[d], part_ref[2 * y + 1 - core]).astype(LOW)


def seq_dots(core, left_ref, right, put):
    part = left_ref.shape[1] // 4
    for some in range(2):

        @pl.when(core == some)
        def _(some=some):
            for y in range(2):
                at = (2 * y + some) * part
                put(y, t_dot(left_ref[:, at : at + part], right))


def other_kernel(core_ref, *rest):
    *pairs, out_ref = rest

    for m in range(len(pairs) // 2):

        def put(y, total, m=m):
            out_ref[m, y] = total.astype(LOW)

        seq_dots(1 - core_ref[0], pairs[2 * m], pairs[2 * m + 1][...], put)


def mine_kernel(core_ref, row_ref, got_ref, *rest):
    *pairs, keep_ref, send_ref = rest

    for m in range(len(pairs) // 2):

        def put(y, total, m=m):
            total = total + got_ref[m, y].astype(FULL)

            @pl.when(row_ref[0] == y)
            def _():
                keep_ref[m] = total

            @pl.when(row_ref[0] != y)
            def _():
                send_ref[m] = total.astype(LOW)

        seq_dots(core_ref[0], pairs[2 * m], pairs[2 * m + 1][...], put)


def hidden_grad_kernel(place_ref, cot_ref, pair_ref, peer_ref, w_ref, grad_ref):
    put_shards(place_ref, pair_ref, peer_ref, w_ref)
    step = min(512, cot_ref.shape[0])
    for start in range(0, cot_ref.shape[0], step):
        grad_ref[start : start + step, :] = dot(cot_ref[start : start + step, :], w_ref[...])


def hidden_kernel(
    n_pieces, member_ref, offset_ref, place_ref, pair_ref, peer_ref, bias_ref, grad_ref, *rest
):
    pieces = rest[:n_pieces]
    x_ref, value_ref, slope_ref, sum_ref, far_ref, unit_ref, w_ref = rest[n_pieces:]
    count, rows, _ = sum_ref.shape
    middle = rows // 2
    put_shards(place_ref, pair_ref, peer_ref, w_ref)

    def put(member, half, values):
        at = pl.multiple_of(member * rows + half * middle, middle)
        x_ref[pl.ds(at, middle), :] = values

    put_tokens(member_ref, pieces, put, rows, count)
    unit_ref[...] = jnp.zeros_like(unit_ref)
    step = min(512, count * rows)
    for start in range(0, count * rows, step):
        part = slice(start, start + step)
        value, slope = gelu_parts(dot(x_ref[part, :], w_ref[...]) + bias_ref[...])
        value_ref[part, :] = value.astype(LOW)
        low = (grad_ref[part, :] * slope).astype(LOW)
        slope_ref[part, :] = low
        unit_ref[...] += jnp.sum(low.astype(FULL), axis=0, keepdims=True)
        total = dot_t(low, w_ref[...])
        for m in range(start // rows, (start + step) // rows):
            at = m * rows - start
            put_ring(offset_ref[m], count, sum_ref, far_ref, 0, total[at : at + rows, :])


def branch_kernel(value_ref, w_ref, out_ref):
    step = min(512, value_ref.shape[0])
    for start in range(0, value_ref.shape[0], step):
        part = slice(start, start + step)
        out_ref[part, :] = dot_t(value_ref[part, :], w_ref[...]).astype(LOW)


def body(
    block_input,
    out_cot,
    pair_of,
    ln1_gain,
    ln1_bias,
    qkv_weight,
    qv_bias,
    out_weight,
    out_bias,
    ln2_gain,
    ln2_bias,
    fc_weight,
    fc_bias,
    proj_weight,
    proj_bias,
):
    rows, width = block_input.shape[2], block_input.shape[3]
    count = lax.axis_size("ctx")
    tokens = count * rows
    fused = count <= 8
    seq, ctx = lax.axis_index("seq"), lax.axis_index("ctx")
    core, row = seq % 2, seq // 2
    order = np.array(ring_order(count), np.int32)
    rank = np.argsort(order)
    member = jnp.asarray(np.stack([np.roll(order, -i) for i in rank]).astype(np.int32))[ctx]
    offset = jnp.asarray(((rank[None, :] - rank[:, None]) % count).astype(np.int32))[ctx]
    place, core_at, row_at = seq[None], core[None], row[None]
    ranks = jnp.arange(count, dtype=jnp.int32)
    who = jnp.sum(jnp.where(pair_of[None, :] == ranks[:, None], ranks[None, :], 0), axis=1)
    who = jnp.concatenate([who, who[::-1]]).astype(jnp.int32)
    far_of = offset[who]
    input_low = block_input.reshape(rows, width)
    inputs = input_low.astype(FULL)
    cot_low = out_cot.reshape(rows, width)

    group, moves, sent, kept = head_plan(count, width)
    heads = group // HEAD
    pick_sent = picker(jnp.asarray(sent)[ctx], qkv_weight.shape[1])
    pick_kept = picker(jnp.asarray(kept)[ctx], sent.shape[1])
    scaled_one, rate_one = norm_parts(inputs)
    normed_one = (scaled_one * ln1_gain + ln1_bias).astype(LOW)
    units = fc_weight.shape[1]
    held = {}

    with jax.named_scope("to_heads"):
        sent_heads = dot(qkv_weight, pick_sent).astype(LOW)
    first = len(moves) // 2

    def ride_first(hold):
        with jax.named_scope("to_heads"):
            held["first"] = take_rounds(sent_heads, moves[:first])
        held["out"] = lax.all_gather(jnp.transpose(out_weight), ("seq", "ctx"), axis=0)
        return held["first"]

    def ride_second(hold):
        with jax.named_scope("to_heads"):
            held["second"] = take_rounds(hold(sent_heads), moves[first:])
        return held["second"]

    def ride_row_parts(hold):
        with jax.named_scope("qkv_parts"):
            pieces = jnp.concatenate(held["first"] + held["second"], axis=1)
            own = dot(hold(pieces), pick_kept).astype(LOW)
            held["own"], held["row"] = own, swap(own, "seq", 2)
        return ()

    def ride_core_parts(hold):
        with jax.named_scope("qkv_parts"):
            held["pair"] = jnp.stack([held["own"], hold(held["row"])])
            held["peer"] = swap(held["pair"], "seq", 1)
        return ()

    with jax.named_scope("gather_one"):
        gathered = ring_gather(normed_one, [ride_first, ride_second, ride_row_parts, ride_core_parts])
    qkv_pair, qkv_peer = held["pair"], held["peer"]
    out_t = held["out"].reshape(4, count, out_weight.shape[1], out_weight.shape[0])
    bias_rows = jnp.pad(qv_bias, ((0, 0), (0, count * group - width)))
    bias_mine = lax.dynamic_slice_in_dim(bias_rows, ctx * group, group, 1)
    qkv_shift = jnp.concatenate([bias_mine[:1], jnp.zeros((1, group), FULL), bias_mine[1:]], axis=1)
    with jax.named_scope("unit_parts"):
        proj_own = after(jnp.transpose(proj_weight), qkv_peer)
        proj_pair = jnp.stack([proj_own, swap(proj_own, "seq", 2)])

    one_tokens, qkv_cols, qkv, attn_full, attn_part, lse = call(
        functools.partial(attend_kernel, len(gathered), heads),
        [
            ((tokens, width), LOW),
            ((width, 3 * group), LOW),
            ((tokens, 3 * group), LOW),
            ((tokens, group), FULL),
            ((count, rows, group), LOW),
            ((tokens, heads), FULL),
        ],
        [qkv_pair, qkv_peer, qkv_shift, *gathered],
        [member, place, pair_of, who],
        "attend",
        2 * tokens * width * 3 * group + 16 * tokens * tokens * group,
    )
    attn_part, proj_pair = lax.optimization_barrier((attn_part, proj_pair))
    with jax.named_scope("unit_parts"):
        fc_own = after(fc_weight, attn_part)
        fc_pair = jnp.stack([fc_own, swap(fc_own, "seq", 2)])
    cots = lax.all_gather(after(cot_low, qkv_peer), "ctx", axis=0, tiled=True)

    back = lax.all_to_all(attn_part, "ctx", 0, 0, tiled=True)
    back, proj_pair, fc_pair = lax.optimization_barrier((back, proj_pair, fc_pair))
    with jax.named_scope("unit_parts"):
        proj_peer = swap(proj_pair, "seq", 1)
        fc_peer = swap(fc_pair, "seq", 1)
    middle, normed_two, scaled_two, rate_two, attn_low = call(
        out_kernel,
        [
            ((rows, width), FULL),
            ((rows, width), LOW),
            ((rows, width), FULL),
            ((rows, 1), FULL),
            ((rows, width), LOW),
        ],
        [back, input_low, out_bias[None], ln2_gain[None], ln2_bias[None], out_t],
        [],
        "out",
        2 * rows * width * width,
        [pltpu.VMEM((rows, count * group), LOW)],
    )

    proj_cols, hidden_grad = call(
        hidden_grad_kernel,
        [((width, units), LOW), ((tokens, units), FULL)],
        [cots, proj_pair, proj_peer],
        [place],
        "hidden_grad",
        2 * tokens * width * units,
    )
    with jax.named_scope("gather_two"):
        two_gathered = ring_gather(normed_two, [lambda hold: (), lambda hold: (), lambda hold: (hidden_grad,)])
    bias_units = lax.dynamic_slice_in_dim(fc_bias, ctx * units, units)[None]
    if fused:
        two_tokens, hidden, hidden_pre_grad, two_parts, two_far, units_grad = call(
            functools.partial(hidden_kernel, len(two_gathered)),
            [
                ((tokens, width), LOW),
                ((tokens, units), LOW),
                ((tokens, units), LOW),
                ((count, rows, width), LOW),
                ((rows, width), LOW),
                ((1, units), FULL),
            ],
            [fc_pair, fc_peer, bias_units, hidden_grad, *two_gathered],
            [member, offset, place],
            "hidden",
            4 * tokens * width * units,
            [pltpu.VMEM((width, units), LOW)],
        )
    else:
        far = count // 2
        pieces = two_gathered[:far] + [jnp.concatenate(two_gathered[far : far + 2])] + two_gathered[far + 2 :]
        two_tokens = pick(jnp.stack(pieces), offset, count).reshape(tokens, width)
        shards = jnp.stack([fc_pair[0], fc_peer[0], fc_pair[1], fc_peer[1]])
        fc_cols = pick(shards, seq ^ jnp.arange(4), 4).reshape(width, units)
        value, slope = gelu_parts(dot(two_tokens, fc_cols) + bias_units)
        hidden = value.astype(LOW)
        hidden_pre_grad = (hidden_grad * slope).astype(LOW)
        two_parts = pick(dot_t(hidden_pre_grad, fc_cols).reshape(count, rows, width), member, count)
        two_far = two_parts[far].astype(LOW)
        units_grad = jnp.sum(hidden_pre_grad.astype(FULL), axis=0)
    def ride_branch(hold):
        (held["branch"],) = call(
            branch_kernel, [((tokens, width), LOW)], [hold(hidden), proj_cols], [], "branch", 2 * tokens * width * units
        )
        return (held["branch"],)

    def ride_other(hold):
        with jax.named_scope("unit_sum"):
            (other,) = call(
                other_kernel,
                [((2, 2, width // 4, units), LOW)],
                [two_tokens, hidden_pre_grad, cots, hidden],
                [hold(core_at)],
                "unit_other",
                0,
            )
            held["peer"] = swap(other, "seq", 1)
        return (other,)

    with jax.named_scope("sum_two"):
        normed_two_grad = ring_sum(two_parts, two_far, [lambda hold: (), ride_branch, ride_other])
    branch_two = lax.psum_scatter(held["branch"], "ctx", scatter_dimension=0, tiled=True)
    block_output = (middle + branch_two.astype(FULL) + proj_bias).astype(LOW).reshape(block_input.shape)

    size, quarter = out_t.shape[2], out_t.shape[3]
    middle_grad, branch_low, attn_grad, lines, whole_out, other = call(
        out_back_kernel,
        [
            ((rows, width), FULL),
            ((rows, width), LOW),
            ((count, rows, group), LOW),
            ((4, width), FULL),
            ((count, size, 2 * quarter), FULL),
            ((count, size, 2 * quarter), LOW),
        ],
        [normed_two_grad, cot_low, scaled_two, rate_two, ln2_gain[None], out_t, attn_low],
        [core_at],
        "out_back",
        2 * rows * width * width,
        [pltpu.VMEM((rows, count * group), LOW), pltpu.VMEM((4, rows, quarter), LOW)],
    )
    grad_part = lax.all_to_all(attn_grad, "ctx", 0, 0, tiled=True)
    with jax.named_scope("out_sum"):
        got_core_out = swap(other, "seq", 1)
        half_sum = (whole_out + got_core_out.astype(FULL)).astype(LOW)
        with jax.named_scope("unit_sum"):
            keep_units, send_units = call(
                mine_kernel,
                [((2, width // 4, units), FULL), ((2, width // 4, units), LOW)],
                [held["peer"], two_tokens, hidden_pre_grad, cots, hidden],
                [after(core_at, half_sum), row_at],
                "unit_mine",
                0,
            )
        grad_part, send_units = lax.optimization_barrier((grad_part, send_units))
        with jax.named_scope("unit_sum"):
            got_units = swap(send_units, "seq", 2)
        out_sum = lax.psum_scatter(half_sum, "ctx", scatter_dimension=0)

    far_pair = pair_of[member[count // 2]]
    qkv_grad, cols_sum, one_far = call(
        functools.partial(attend_back_kernel, heads),
        [((tokens, 3 * group), LOW), ((1, 3 * group), FULL), ((rows, width), LOW)],
        [qkv, qkv_cols, attn_full, lse, grad_part],
        [who, jnp.stack([far_pair, 2 * count - 1 - far_pair])],
        "attend_back",
        0,
        [pltpu.VMEM((tokens, group), FULL)] * 2 + [pltpu.VMEM((tokens, group), LOW)],
    )
    if fused:
        one_parts, one_lines = call(
            project_back_kernel,
            [((count, rows, width), LOW), ((2, width), FULL)],
            [qkv_grad, qkv_cols, one_tokens],
            [after(far_of, got_units)],
            "project_back",
            0,
        )
    else:
        parts = dot_t(qkv_grad, qkv_cols)
        one_lines = jnp.stack([jnp.sum(parts * one_tokens.astype(FULL), axis=0), jnp.sum(parts, axis=0)])
        parts = parts.reshape(2 * count, rows // 2, width)
        pairs = pair_of[member]
        one_parts = jnp.concatenate([pick(parts, pairs, count), pick(parts, 2 * count - 1 - pairs, count)], axis=1)

    shift_one = one_lines[1]
    gain_one = (one_lines[0] - ln1_bias * shift_one) / ln1_gain
    qv_sums = jnp.concatenate([cols_sum[:, :group], cols_sum[:, 2 * group :]])
    qv_sums = lax.dynamic_update_slice(
        jnp.zeros((2, count * group), FULL), qv_sums, (0, ctx * group)
    )[:, :width]
    unit_sums = lax.dynamic_update_slice(
        jnp.zeros((count * units,), FULL), units_grad.reshape(-1), (ctx * units,)
    )
    flat = [gain_one, shift_one, qv_sums.reshape(-1), lines.reshape(-1), unit_sums]
    flat = jnp.concatenate(flat)

    def ride_core(hold):
        with jax.named_scope("qkv_sum"):
            (other,) = call(
                other_kernel,
                [((1, 2, width // 4, 3 * group), LOW)],
                [one_tokens, qkv_grad],
                [core_at],
                "qkv_other",
                0,
            )
            held["core"] = swap(other, "seq", 1)
        return (held["core"],)

    def ride_row(hold):
        with jax.named_scope("sum_vectors"):
            held["flat"] = sum_over(hold(flat), "seq")
        with jax.named_scope("qkv_sum"):
            held["qkv"], send = call(
                mine_kernel,
                [((1, width // 4, 3 * group), FULL), ((1, width // 4, 3 * group), LOW)],
                [held["core"], one_tokens, qkv_grad],
                [hold(core_at, held["flat"]), row_at],
                "qkv_mine",
                0,
            )
            held["row"] = swap(send, "seq", 2)
        return (send, block_output)

    def ride_out(hold):
        with jax.named_scope("out_sum"):
            keep, send = ordered(row, out_sum[:, :quarter], out_sum[:, quarter:])
            some = send.shape[0] // 2
            first = swap(send[:some], "seq", 2)
            second = swap(after(send[some:], first), "seq", 2)
            held["out_sum"] = keep.astype(FULL) + jnp.concatenate([first, second]).astype(FULL)
        return (held["out_sum"],)

    def ride_heads(hold):
        with jax.named_scope("from_heads"):
            whole = (held["qkv"] + hold(held["row"]).astype(FULL))[0]
            sent_back = dot_t(whole.astype(LOW), pick_kept).astype(LOW)
            held["sent"] = take_rounds(sent_back, backward)
        with jax.named_scope("sum_vectors"):
            held["flat"] = sum_over(hold(held["flat"]), "ctx")
        with jax.named_scope("unit_sum"):
            got = hold(got_units).astype(FULL)
            held["fc"] = keep_units[0] + got[0]
            held["proj"] = jnp.transpose(keep_units[1] + got[1])
        return ()

    backward = [([(b, a) for a, b in pairs], start, size) for pairs, start, size in moves]
    with jax.named_scope("sum_one"):
        normed_one_grad = ring_sum(one_parts, one_far, [ride_core, ride_row, ride_out, ride_heads])
    with jax.named_scope("out_sum"):
        out_weight_grad = jnp.transpose(held["out_sum"])
    (input_grad,) = call(
        input_grad_kernel,
        [((rows, width), LOW)],
        [normed_one_grad, middle_grad, scaled_one, rate_one, ln1_gain[None]],
        [],
        "input_grad",
        0,
    )
    input_grad = input_grad.reshape(block_input.shape)
    with jax.named_scope("from_heads"):
        qkv_weight_grad = dot_t(jnp.concatenate(held["sent"], axis=1), pick_sent)
    fc_weight_grad, proj_weight_grad = held["fc"], held["proj"]
    flat = held["flat"]
    vectors = flat[: 8 * width].reshape(8, width)
    return (
        block_output,
        input_grad,
        vectors[0],
        vectors[1],
        qkv_weight_grad,
        vectors[2:4],
        out_weight_grad,
        vectors[4],
        vectors[5],
        vectors[6],
        fc_weight_grad,
        flat[8 * width :],
        proj_weight_grad,
        vectors[7],
    )


def solution(mesh):
    rows = P("seq", "ctx", None, None)
    cols = P("seq", "ctx")
    flip = P("ctx", "seq")
    one = P()
    return jax.shard_map(
        body,
        mesh=mesh,
        in_specs=(rows, rows, one, one, one, cols, one, cols, one, one, one, cols, one, flip, one),
        out_specs=(rows, rows, one, one, cols, one, cols, one, one, one, cols, one, flip, one),
        check_vma=False,
    )
```
